32 devices in a mesh: rep: 4 (over z), dom: 8 (over y, x, core).
Axes of the slice: x: 2, y: 2, z: 4, core: 2. Of those that a mesh axis runs over, the one named last changes fastest.
Arguments:
- cols: int32 [64, 8], P('dom', 'rep'), may hold values from 0 to 63, as said below
- vals: bfloat16 [64, 8, 128, 128], P('dom', 'rep')
- features: bfloat16 [8192, 128], P(('rep', 'dom')), may hold values from -6 to 6
- weight: bfloat16 [128, 128], replicated, may hold values from -0.5 to 0.5
- bias: float32 [128], replicated, may hold values from -3 to 3
- cotangent: bfloat16 [8192, 128], P('dom'), may hold values from -6 to 6
Outputs:
- output: bfloat16 [8192, 128], P('dom')
- feature_grad: float32 [8192, 128], P(('rep', 'dom'))
- weight_grad: float32 [128, 128], replicated
The draws below stay inside these ranges and needn't reach their ends.
Inputs may be any that keep to these rules, and one draw needn't show every extreme that they name: For every block row and every quarter q of the block columns, entries q * 2 to (q + 1) * 2 - 1 of its row of cols are 2 distinct block columns in the range q * 16 to (q + 1) * 16 - 1 (quarters as many as the size of rep); every block row names its own diagonal block.
All inputs are finite; a program needn't handle non-finite values.
Results may differ from the reference program's by a relative error of at most 0.0055.
Values may be sent and summed in bfloat16 or wider, within the bound.
No kernel may reach another device: no remote copies, remote signals or barrier semaphores. Data moves between devices by JAX's collectives and lax.ppermute only.
A program may use at most 64 MiB of HBM per device.

```python
import jax
import jax.numpy as jnp
from jax import lax

F = 128
BS = 128
NBLK = 64
NODES = 8192
KQ = 2
N_REP = 4


def draw_cols(key, part):
    quarter_blocks = NBLK // N_REP
    scores = jax.random.randint(key, (NBLK, N_REP, quarter_blocks), 0, 1 << 20)
    slots = jnp.arange(quarter_blocks, dtype=jnp.int32)
    starts = (jnp.arange(N_REP, dtype=jnp.int32) * quarter_blocks)[None, :, None]
    targets = starts + slots[None, None, :]
    row_index = jnp.arange(NBLK, dtype=jnp.int32)[:, None, None]
    scores = scores * quarter_blocks + slots[None, None, :]
    scores = jnp.where(targets == row_index, -1, scores)
    order = jnp.argsort(scores, axis=2)[:, :, :KQ]
    return (order.astype(jnp.int32) + starts).reshape(NBLK, N_REP * KQ)


def draw_vals(key, part):
    shape = (NBLK, KQ * N_REP, BS, BS)
    key_values = jax.random.fold_in(key, 11)
    key_keep = jax.random.fold_in(key, 12)
    kept_of_sixteen = min(16, 128 // BS)
    entries = jnp.clip(jax.random.normal(key_values, shape, jnp.float32), -6.0, 6.0)
    keep = (jax.random.randint(key_keep, shape, 0, 16) < kept_of_sixteen).astype(jnp.float32)
    spread = (KQ * N_REP * BS * kept_of_sixteen / 16.0) ** (-0.5)
    return (entries * keep * spread).astype(jnp.bfloat16)


def block_scale(key, dims, shards, least, top_value):
    gain = 1.0
    for position, parts in shards:
        steps = jax.random.uniform(jax.random.fold_in(jax.random.fold_in(key, 6), position), (parts,), jnp.float32, least / len(shards), top_value / len(shards))
        gain = gain * jnp.repeat(jnp.exp(steps), dims[position] // parts).reshape((-1,) + (1,) * (len(dims) - 1 - position))
    return gain


def centred(own_key, dims, scale, reach, pieces=(), kind=jnp.bfloat16):
    values = jax.random.normal(own_key, dims, jnp.float32) * scale
    if len(pieces) > 0:
        values = block_scale(own_key, dims, pieces, -0.22, 0.18) * values
    return jnp.clip(values, min=-reach, max=reach).astype(kind)


def setup_inputs(seed: int = 0) -> dict:
    streams_of = jax.random.split(jax.random.key(seed), 7)
    cols = draw_cols(jax.random.fold_in(streams_of[6], 71), 0)
    vals = draw_vals(jax.random.fold_in(streams_of[6], 71), 0)
    features = centred(streams_of[2], (NODES, F), 1.0, 6.0, ((0, 32),))
    weight = centred(streams_of[3], (F, F), F ** -0.5, 0.5)
    bias = centred(streams_of[4], (F,), 0.5, 3.0, (), jnp.float32)
    cotangent = centred(streams_of[5], (NODES, F), 1.0, 6.0, ((0, 8),))
    return {"cols": cols, "vals": vals, "features": features, "weight": weight, "bias": bias, "cotangent": cotangent}


def reference(cols, vals, features, weight, bias, cotangent):
    blocks = features.reshape(NBLK, BS, F)

    def row_sum(item):
        row_cols, row_vals = item
        picked = blocks[row_cols].astype(jnp.float32)
        return jnp.einsum('kij,kjf->if', row_vals.astype(jnp.float32), picked)

    summed = lax.map(row_sum, (cols, vals)).reshape(NODES, F)
    aggregated = summed.astype(jnp.bfloat16)
    hidden = jnp.dot(aggregated, weight, preferred_element_type=jnp.float32) + bias
    gate_prob = jax.nn.sigmoid(hidden)
    output = (hidden * gate_prob).astype(jnp.bfloat16)
    grad_hidden = (cotangent.astype(jnp.float32) * gate_prob * (1.0 + hidden * (1.0 - gate_prob))).astype(jnp.bfloat16)
    weight_grad = jnp.dot(aggregated.T, grad_hidden, preferred_element_type=jnp.float32)
    grad_agg = jnp.dot(grad_hidden, weight.T, preferred_element_type=jnp.float32).astype(jnp.bfloat16)
    grad_rows = grad_agg.reshape(NBLK, BS, F)

    def scatter_row(total, item):
        row_cols, row_vals, row_grad = item
        terms = jnp.einsum('kij,if->kjf', row_vals.astype(jnp.float32), row_grad.astype(jnp.float32))
        return total.at[row_cols].add(terms), None

    start_total = jnp.zeros((NBLK, BS, F), jnp.float32)
    feature_grad, _ = lax.scan(scatter_row, start_total, (cols, vals, grad_rows))
    return output, feature_grad.reshape(NODES, F), weight_grad
```

```python
import jax
import jax.numpy as jnp
from jax import lax
from jax.sharding import PartitionSpec as P

BF16 = jnp.bfloat16
F32 = jnp.float32


def swap(value, axis, distance):
    size = lax.axis_size(axis)
    return lax.ppermute(value, axis, [(i, i ^ distance) for i in range(size)])


def body(cols, vals, features, weight, bias, cotangent):
    row_blocks, block_count, block_size, _ = vals.shape
    width = features.shape[1]
    dom, rep = lax.axis_size("dom"), lax.axis_size("rep")
    own_blocks = features.shape[0] // block_size
    quarter_blocks = own_blocks * dom
    me_dom, me_rep = lax.axis_index("dom"), lax.axis_index("rep")
    rows = row_blocks * block_size
    part = rows // rep

    local_cols = cols - me_rep * quarter_blocks
    slots = ((local_cols // own_blocks) ^ me_dom) * own_blocks + local_cols % own_blocks

    quarter = jnp.stack([features] + [swap(features, "dom", k) for k in range(1, dom)])
    quarter = quarter.reshape(quarter_blocks, block_size, width)
    picked = quarter[slots]
    partial_sum = jnp.einsum("rkij,rkjf->rif", vals, picked, preferred_element_type=F32)
    partial_sum = partial_sum.reshape(rep, part, width).astype(BF16)
    pieces = lax.all_to_all(partial_sum, "rep", split_axis=0, concat_axis=0)
    own_rows = pieces.astype(F32).sum(axis=0).astype(BF16)

    others = jnp.stack([own_rows] + [swap(own_rows, "rep", k) for k in range(1, rep)])
    aggregated = others[jnp.arange(rep) ^ me_rep].reshape(rows, width)

    hidden = jnp.dot(aggregated, weight, preferred_element_type=F32) + bias
    gate_prob = jax.nn.sigmoid(hidden)
    output = (hidden * gate_prob).astype(BF16)
    grad_hidden = (
        cotangent.astype(F32) * gate_prob * (1.0 + hidden * (1.0 - gate_prob))
    ).astype(BF16)
    weight_part = lax.dot_general(
        aggregated, grad_hidden, (((0,), (0,)), ((), ())), preferred_element_type=F32
    )
    grad_agg = lax.dot_general(
        grad_hidden, weight, (((1,), (1,)), ((), ())), preferred_element_type=F32
    ).astype(BF16)

    weight_rows = lax.all_to_all(
        weight_part.reshape(dom, width // dom, width), "dom", split_axis=0, concat_axis=0
    ).sum(axis=0)
    weight_grad = lax.all_gather(weight_rows, "dom", axis=0, tiled=True)

    grad_blocks = grad_agg.reshape(row_blocks, block_size, width)
    terms = jnp.einsum("rkij,rif->rkjf", vals, grad_blocks, preferred_element_type=F32)
    flat_terms = terms.reshape(row_blocks * block_count, block_size, width)
    contrib = jax.ops.segment_sum(flat_terms, slots.reshape(-1), num_segments=quarter_blocks)
    contrib = contrib.reshape(dom, own_blocks * block_size, width)
    total = contrib[0]
    for k in range(1, dom):
        total = total + swap(contrib[k].astype(BF16), "dom", k).astype(F32)
    return output, total, weight_grad


def solution(mesh):
    placed = (
        P("dom", "rep"),
        P("dom", "rep", None, None),
        P(("rep", "dom"), None),
        P(),
        P(),
        P("dom", None),
    )
    return jax.shard_map(
        body,
        mesh=mesh,
        in_specs=placed,
        out_specs=(P("dom", None), P(("rep", "dom"), None), P()),
        check_vma=False,
    )
```

```python
import functools

import jax
import jax.numpy as jnp
from jax import lax
from jax.experimental import pallas as pl
from jax.experimental.pallas import tpu as pltpu
from jax.sharding import PartitionSpec as P

BF16 = jnp.bfloat16
F32 = jnp.float32
VMEM = pl.BlockSpec(memory_space=pltpu.VMEM)
SMEM = pl.BlockSpec(memory_space=pltpu.SMEM)


def swap(value, axis, distance):
    size = lax.axis_size(axis)
    return lax.ppermute(value, axis, [(i, i ^ distance) for i in range(size)])


def matmul(a, b, contract):
    return lax.dot_general(a, b, ((contract[:1], contract[1:]), ((), ())), preferred_element_type=F32)


def slot_of(cols_ref, row, k, own_blocks, quarter_blocks):
    col = cols_ref[row, k] - lax.axis_index("rep") * quarter_blocks
    owner = lax.div(col, jnp.int32(own_blocks)) ^ lax.axis_index("dom")
    return owner * own_blocks + lax.rem(col, jnp.int32(own_blocks))


def aggregate_kernel(rep, cols_ref, vals_ref, own_ref, *refs):
    near, far = refs[: -rep - 2], refs[-rep - 2]
    outs, held = refs[-rep - 1 : -1], refs[-1]
    rows, count, size, _ = vals_ref.shape
    own_blocks = own_ref.shape[0] // size
    quarter_blocks = held.shape[0]
    chips = quarter_blocks // own_blocks // 2

    def put(slot, block):
        held[slot * own_blocks : (slot + 1) * own_blocks] = block.reshape(own_blocks, size, -1)

    put(0, own_ref[...])
    for chip in range(1, chips):
        put(2 * chip, near[chip - 1][...])
    nodes = own_blocks * size
    put(1, near[chips - 1][...])
    for chip in range(1, chips):
        put(2 * chip + 1, far[(chip - 1) * nodes : chip * nodes])

    share = rows // rep
    for j in range(rep):
        target = lax.axis_index("rep") ^ j
        for i in range(share):
            row = target * share + i
            total = None
            for k in range(count):
                slot = slot_of(cols_ref, row, k, own_blocks, quarter_blocks)
                term = matmul(vals_ref[row, k], held[slot], (1, 0))
                total = term if total is None else total + term
            outs[j][i * size : (i + 1) * size] = total.astype(outs[j].dtype)


def layer_kernel(
    rep, cols_ref, vals_ref, cotangent_ref, weight_ref, bias_ref, *refs
):
    pieces = refs[:rep]
    output_ref, send_ref, keep_ref, keep_weight_ref, contrib = refs[rep:]
    rows, count, size, _ = vals_ref.shape
    share = rows // rep
    quarter_blocks = contrib.shape[0]
    own_blocks = keep_ref.shape[1] // size
    contrib[...] = jnp.zeros_like(contrib)
    weight_part = jnp.zeros(weight_ref.shape, F32)
    for j in range(rep):
        target = lax.axis_index("rep") ^ j
        aggregated = pieces[j][...]
        part = aggregated.shape[0]
        here = pl.ds(pl.multiple_of(target * part, part), part)
        hidden = matmul(aggregated, weight_ref[...], (1, 0)) + bias_ref[...]
        gate_prob = jax.nn.sigmoid(hidden)
        output_ref[here, :] = (hidden * gate_prob).astype(BF16)
        grad_hidden = (
            cotangent_ref[here, :].astype(F32) * gate_prob * (1.0 + hidden * (1.0 - gate_prob))
        ).astype(BF16)
        weight_part += matmul(aggregated, grad_hidden, (0, 0))
        grad_agg = matmul(grad_hidden, weight_ref[...], (1, 1)).astype(BF16)
        for i in range(share):
            row = target * share + i
            grad_block = grad_agg[i * size : (i + 1) * size]
            for k in range(count):
                slot = slot_of(cols_ref, row, k, own_blocks, quarter_blocks)
                contrib[slot] += matmul(vals_ref[row, k], grad_block, (0, 0))
    chips = keep_ref.shape[0]
    nodes = own_blocks * size
    for chip in range(chips):
        even = contrib[2 * chip * own_blocks : (2 * chip + 1) * own_blocks]
        odd = contrib[(2 * chip + 1) * own_blocks : (2 * chip + 2) * own_blocks]
        keep_ref[chip] = even.reshape(nodes, -1)
        send_ref[chip * nodes : (chip + 1) * nodes] = odd.reshape(nodes, -1).astype(BF16)
    send_ref[chips * nodes :] = weight_part.astype(BF16)
    keep_weight_ref[...] = weight_part.astype(BF16)


def pair_kernel(keep_ref, keep_weight_ref, got_ref, own_ref, own_weight_ref, *outs):
    chips, nodes, _ = keep_ref.shape
    both = keep_weight_ref[...].astype(F32) + got_ref[chips * nodes :].astype(F32)
    both = both.astype(BF16)
    own_weight_ref[...] = both
    own_ref[...] = keep_ref[0] + got_ref[:nodes].astype(F32)
    for chip in range(1, chips):
        total = keep_ref[chip] + got_ref[chip * nodes : (chip + 1) * nodes].astype(F32)
        outs[chip - 1][:nodes] = total.astype(BF16)
        outs[chip - 1][nodes:] = both


def total_of(values):
    while len(values) > 1:
        values = [a + b for a, b in zip(values[::2], values[1::2])]
    return values[0]


def shape(dims, dtype):
    return jax.ShapeDtypeStruct(dims, dtype)


def body(cols, vals, features, weight, bias, cotangent):
    rows, count, size, _ = vals.shape
    nodes, width = features.shape
    dom, rep = lax.axis_size("dom"), lax.axis_size("rep")
    chips = dom // 2
    quarter_blocks = nodes * dom // size
    part = rows * size // rep
    params = pltpu.CompilerParams(vmem_limit_bytes=(8 + dom // 2) * 1024 * 1024)

    across = [swap(features, "dom", 2 * chip) for chip in range(1, chips)]
    beside = swap(features, "dom", 1)
    far = swap(jnp.concatenate(across), "dom", 1)
    partials = pl.pallas_call(
        functools.partial(aggregate_kernel, rep),
        out_shape=[shape((part, width), F32 if j == 0 else BF16) for j in range(rep)],
        in_specs=[SMEM] + [VMEM] * (chips + 3),
        out_specs=[VMEM] * rep,
        scratch_shapes=[pltpu.VMEM((quarter_blocks, size, width), BF16)],
        compiler_params=params,
    )(cols, vals, features, *across, beside, far)

    arrived = [partials[0]] + [swap(partials[j], "rep", j).astype(F32) for j in range(1, rep)]
    own_rows = total_of(arrived).astype(BF16)
    pieces = [own_rows] + [swap(own_rows, "rep", j) for j in range(1, rep)]

    output, send, keep, keep_weight = pl.pallas_call(
        functools.partial(layer_kernel, rep),
        out_shape=[
            shape((rows * size, width), BF16),
            shape((chips * nodes + width, width), BF16),
            shape((chips, nodes, width), F32),
            shape((width, width), BF16),
        ],
        in_specs=[SMEM] + [VMEM] * (4 + rep),
        out_specs=[VMEM] * 4,
        scratch_shapes=[pltpu.VMEM((quarter_blocks, size, width), F32)],
        compiler_params=params,
    )(cols, vals, cotangent, weight, bias.reshape(1, width), *pieces)

    own, own_weight, *sends = pl.pallas_call(
        pair_kernel,
        out_shape=[shape((nodes, width), F32), shape((width, width), BF16)]
        + [shape((nodes + width, width), BF16)] * (chips - 1),
        in_specs=[VMEM] * 3,
        out_specs=[VMEM] * (chips + 1),
        compiler_params=params,
    )(keep, keep_weight, swap(send, "dom", 1))

    got = [swap(sends[chip - 1], "dom", 2 * chip).astype(F32) for chip in range(1, chips)]
    feature_grad = total_of([own] + [value[:nodes] for value in got])
    weight_grad = total_of([own_weight.astype(F32)] + [value[nodes:] for value in got])
    return output, feature_grad, weight_grad


def solution(mesh):
    placed = (
        P("dom", "rep"),
        P("dom", "rep", None, None),
        P(("rep", "dom"), None),
        P(),
        P(),
        P("dom", None),
    )
    return jax.shard_map(
        body,
        mesh=mesh,
        in_specs=placed,
        out_specs=(P("dom", None), P(("rep", "dom"), None), P()),
        check_vma=False,
    )
```

```python
import functools

import jax
import jax.numpy as jnp
from jax import lax
from jax.experimental import pallas as pl
from jax.experimental.pallas import tpu as pltpu
from jax.sharding import PartitionSpec as P

BF16 = jnp.bfloat16
F32 = jnp.float32
VMEM = pl.BlockSpec(memory_space=pltpu.VMEM)
SMEM = pl.BlockSpec(memory_space=pltpu.SMEM)


def swap(value, axis, distance):
    size = lax.axis_size(axis)
    return lax.ppermute(value, axis, [(i, i ^ distance) for i in range(size)])


def matmul(a, b, contract):
    return lax.dot_general(a, b, ((contract[:1], contract[1:]), ((), ())), preferred_element_type=F32)


def slot_of(cols_ref, row, k, own_blocks, quarter_blocks):
    col = cols_ref[row, k] - lax.axis_index("rep") * quarter_blocks
    owner = lax.div(col, jnp.int32(own_blocks)) ^ lax.axis_index("dom")
    return owner, lax.rem(col, jnp.int32(own_blocks))


def transpose_kernel(vals_ref, near_ref, flipped_ref):
    rows, count, size, _ = vals_ref.shape
    near_ref[...] = vals_ref[...]
    for row in range(rows):
        for k in range(count):
            flipped_ref[row, k * size : (k + 1) * size] = vals_ref[row, k].T


def join_kernel(order, *refs):
    pieces, out_ref = refs[: len(order)], refs[-1]
    nodes = pieces[0].shape[0]
    for chip, piece in zip(order, pieces):
        out_ref[chip * nodes : (chip + 1) * nodes] = piece[...]


def aggregate_kernel(rep, own_blocks, j, cols_ref, vals_ref, mine_ref, far_ref, out_ref):
    rows, count, size, _ = vals_ref.shape
    quarter_blocks = 2 * mine_ref.shape[0] // size
    share = rows // rep
    target = lax.axis_index("rep") ^ j
    for i in range(share):
        row = target * share + i
        total = None
        for k in range(count):
            owner, rest = slot_of(cols_ref, row, k, own_blocks, quarter_blocks)
            index = (owner >> 1) * own_blocks + rest
            here = pl.ds(pl.multiple_of(index * size, size), size)
            block = jnp.where((owner & 1) == 1, far_ref[here, :], mine_ref[here, :])
            term = matmul(vals_ref[row, k], block, (1, 0))
            total = term if total is None else total + term
        out_ref[i * size : (i + 1) * size] = total.astype(out_ref.dtype)


def layer_kernel(
    rep, count, own_blocks, j, cols_ref, flipped_ref, cotangent_ref, weight_ref, bias_ref, *refs
):
    first, last = j == 0, j == 1
    piece_ref, refs = refs[0], refs[1:]
    if not first:
        (contrib_in, weight_in), refs = refs[:2], refs[2:]
    if last:
        output_ref, send_ref, keep_ref, keep_weight_ref, contrib = refs
    else:
        output_ref, contrib, weight_out = refs
    rows, _, size = flipped_ref.shape
    share = rows // rep
    quarter_blocks = contrib.shape[0]
    nodes = own_blocks * size
    contrib[...] = jnp.zeros_like(contrib) if first else contrib_in[...]

    target = lax.axis_index("rep") ^ j
    aggregated = piece_ref[...]
    part = aggregated.shape[0]
    here = pl.ds(pl.multiple_of(target * part, part), part)
    hidden = matmul(aggregated, weight_ref[...], (1, 0)) + bias_ref[...]
    gate_prob = jax.nn.sigmoid(hidden)
    output_ref[...] = (hidden * gate_prob).astype(BF16)
    grad_hidden = (
        cotangent_ref[here, :].astype(F32) * gate_prob * (1.0 + hidden * (1.0 - gate_prob))
    ).astype(BF16)
    weight_part = matmul(aggregated, grad_hidden, (0, 0))
    if not first:
        weight_part = weight_in[...] + weight_part
    grad_agg = matmul(grad_hidden, weight_ref[...], (1, 1)).astype(BF16)
    for i in range(share):
        row = target * share + i
        terms = matmul(flipped_ref[row], grad_agg[i * size : (i + 1) * size], (1, 0))
        for k in range(count):
            owner, rest = slot_of(cols_ref, row, k, own_blocks, quarter_blocks)
            contrib[owner * own_blocks + rest] += terms[k * size : (k + 1) * size]
    if not last:
        weight_out[...] = weight_part
        return
    chips = keep_ref.shape[0]
    for chip in range(chips):
        even = contrib[2 * chip * own_blocks : (2 * chip + 1) * own_blocks]
        odd = contrib[(2 * chip + 1) * own_blocks : (2 * chip + 2) * own_blocks]
        keep_ref[chip] = even.reshape(nodes, -1)
        send_ref[chip * nodes : (chip + 1) * nodes] = odd.reshape(nodes, -1).astype(BF16)
    send_ref[chips * nodes :] = weight_part.astype(BF16)
    keep_weight_ref[...] = weight_part.astype(BF16)


def add_kernel(a_ref, b_ref, out_ref):
    out_ref[...] = (a_ref[...] + b_ref[...].astype(F32)).astype(out_ref.dtype)


def place_kernel(order, *refs):
    pieces, out_ref = refs[:-1], refs[-1]
    part = pieces[0].shape[0]
    for j, piece in zip(order, pieces):
        target = lax.axis_index("rep") ^ j
        out_ref[pl.ds(pl.multiple_of(target * part, part), part), :] = piece[...]


def pair_kernel(keep_ref, keep_weight_ref, got_ref, own_ref, own_weight_ref, *outs):
    chips, nodes, _ = keep_ref.shape
    both = keep_weight_ref[...].astype(F32) + got_ref[chips * nodes :].astype(F32)
    both = both.astype(BF16)
    own_weight_ref[...] = both
    own_ref[...] = keep_ref[0] + got_ref[:nodes].astype(F32)
    for chip in range(1, chips):
        total = keep_ref[chip] + got_ref[chip * nodes : (chip + 1) * nodes].astype(F32)
        outs[chip - 1][:nodes] = total.astype(BF16)
        outs[chip - 1][nodes:] = both


def total_of(values):
    while len(values) > 1:
        values = [a + b for a, b in zip(values[::2], values[1::2])]
    return values[0]


def half_kernel(levels, *refs):
    for level in range(1, levels):
        first = 1 << level
        got = refs[: -levels + 1][::-1][first - 2 : 2 * first - 2]
        refs[level - levels][...] = total_of([g[...].astype(F32) for g in got])


def final_kernel(own_ref, own_weight_ref, got_ref, *refs):
    later, (feature_ref, weight_ref) = refs[:-2], refs[-2:]
    nodes = own_ref.shape[0]
    feature = own_ref[...] + got_ref[:nodes].astype(F32)
    weight = own_weight_ref[...].astype(F32) + got_ref[nodes:].astype(F32)
    for value in later:
        feature += value[:nodes]
        weight += value[nodes:]
    feature_ref[...] = feature
    weight_ref[...] = weight


def shape(dims, dtype):
    return jax.ShapeDtypeStruct(dims, dtype)


def body(cols, vals, features, weight, bias, cotangent):
    rows, count, size, _ = vals.shape
    nodes, width = features.shape
    dom, rep = lax.axis_size("dom"), lax.axis_size("rep")
    chips = dom // 2
    own_blocks = nodes // size
    quarter_blocks = own_blocks * dom
    part = rows * size // rep
    params = pltpu.CompilerParams(vmem_limit_bytes=(8 + dom // 2) * 1024 * 1024)

    def call(kernel, out_shape, in_specs, scratch=()):
        single = not isinstance(out_shape, list)
        return pl.pallas_call(
            kernel,
            out_shape=out_shape,
            in_specs=in_specs,
            out_specs=VMEM if single else [VMEM] * len(out_shape),
            scratch_shapes=scratch,
            compiler_params=params,
        )

    near, flipped = call(
        transpose_kernel,
        [shape(vals.shape, BF16), shape((rows, count * size, size), BF16)],
        [VMEM],
    )(vals)
    order = list(range(chips - 1, -1, -1))
    across = [swap(features, "dom", 2 * chip) for chip in order[:-1]] + [features]
    mine = call(
        functools.partial(join_kernel, order), shape((chips * nodes, width), BF16), [VMEM] * (chips + 1)
    )(*across, near)
    far = swap(mine, "dom", 1)

    arrived = {}
    for j in range(rep - 1, -1, -1):
        partial_sum = call(
            functools.partial(aggregate_kernel, rep, own_blocks, j),
            shape((part, width), BF16 if j else F32),
            [SMEM, VMEM, VMEM, VMEM],
        )(cols, near, mine, far)
        arrived[j] = swap(partial_sum, "rep", j) if j else partial_sum
    own_rows = arrived[0]
    for j in range(rep - 1, 0, -1):
        own_rows = call(add_kernel, shape((part, width), F32 if j > 1 else BF16), [VMEM] * 2)(
            own_rows, arrived[j]
        )

    pieces = {0: own_rows}
    for j in range(rep - 1, 0, -1):
        pieces[j] = swap(own_rows, "rep", j)

    outputs, carried = [], []
    for j, piece in pieces.items():
        if j != 1:
            outs = [shape((quarter_blocks, size, width), F32), shape((width, width), F32)]
            scratch = []
        else:
            outs = [
                shape((chips * nodes + width, width), BF16),
                shape((chips, nodes, width), F32),
                shape((width, width), BF16),
            ]
            scratch = [pltpu.VMEM((quarter_blocks, size, width), F32)]
        output, *carried = call(
            functools.partial(layer_kernel, rep, count, own_blocks, j),
            [shape((part, width), BF16)] + outs,
            [SMEM] + [VMEM] * (5 + len(carried)),
            scratch,
        )(cols, flipped, cotangent, weight, bias.reshape(1, width), piece, *carried)
        outputs.append(output)
    send, keep, keep_weight = carried

    own, own_weight, *sends = call(
        pair_kernel,
        [shape((nodes, width), F32), shape((width, width), BF16)]
        + [shape((nodes + width, width), BF16)] * (chips - 1),
        [VMEM] * 3,
    )(keep, keep_weight, swap(send, "dom", 1))
    got = {chip: swap(sends[chip - 1], "dom", 2 * chip) for chip in range(chips - 1, 0, -1)}
    output = call(
        functools.partial(place_kernel, list(pieces)), shape((rows * size, width), BF16), [VMEM] * rep
    )(*outputs)
    levels = chips.bit_length() - 1
    later = call(
        functools.partial(half_kernel, levels), [shape((nodes + width, width), F32)] * (levels - 1), [VMEM] * (chips - 2)
    )(*[got[chip] for chip in range(chips - 1, 1, -1)])
    feature_grad, weight_grad = call(
        final_kernel,
        [shape((nodes, width), F32), shape((width, width), F32)],
        [VMEM] * (levels + 2),
    )(own, own_weight, got[1], *later)
    return output, feature_grad, weight_grad


def solution(mesh):
    placed = (
        P("dom", "rep"),
        P("dom", "rep", None, None),
        P(("rep", "dom"), None),
        P(),
        P(),
        P("dom", None),
    )
    return jax.shard_map(
        body,
        mesh=mesh,
        in_specs=placed,
        out_specs=(P("dom", None), P(("rep", "dom"), None), P()),
        check_vma=False,
    )
```

```python
import functools

import jax
import jax.numpy as jnp
from jax import lax
from jax.experimental import pallas as pl
from jax.experimental.pallas import tpu as pltpu
from jax.sharding import PartitionSpec as P

BF16 = jnp.bfloat16
F32 = jnp.float32
VMEM = pl.BlockSpec(memory_space=pltpu.VMEM)


def swap(value, axis, distance):
    size = lax.axis_size(axis)
    return lax.ppermute(value, axis, [(i, i ^ distance) for i in range(size)])


def matmul(a, b, contract):
    return lax.dot_general(a, b, ((contract[:1], contract[1:]), ((), ())), preferred_element_type=F32)


def early_kernel(own_blocks, dom, cols_ref, vals_ref, *refs):
    flipped_ref, place_ref = refs[-2:]
    rows, count, size, _ = vals_ref.shape
    for row in range(rows):
        for k in range(count):
            flipped_ref[row, k * size : (k + 1) * size] = vals_ref[row, k].T
            col = cols_ref[row, k] - lax.axis_index("rep") * (own_blocks * dom)
            owner = lax.div(col, jnp.int32(own_blocks)) ^ lax.axis_index("dom")
            place = ((owner & 1) * (dom // 2) + (owner >> 1)) * own_blocks
            place += lax.rem(col, jnp.int32(own_blocks))
            place_ref[row * count + k : row * count + k + 1, :] = jnp.full((1, 128), place, jnp.int32)


def join_kernel(order, *refs):
    pieces, out_ref = refs[: len(order)], refs[-1]
    nodes = pieces[0].shape[0]
    for chip, piece in zip(order, pieces):
        out_ref[chip * nodes : (chip + 1) * nodes] = piece[...]


def aggregate_kernel(rep, place_ref, vals_ref, mine_ref, far_ref, *outs):
    rows, count, size, _ = vals_ref.shape
    half = mine_ref.shape[0] // size
    share = rows // rep
    for j in range(rep - 1, -1, -1):
        target = lax.axis_index("rep") ^ j
        for i in range(share):
            row = target * share + i
            total = None
            for k in range(count):
                place = place_ref[row * count + k, 0]
                beyond = place >= half
                index = jnp.where(beyond, place - half, place)
                here = pl.ds(pl.multiple_of(index * size, size), size)
                block = jnp.where(beyond, far_ref[here, :], mine_ref[here, :])
                term = matmul(vals_ref[row, k], block, (1, 0))
                total = term if total is None else total + term
            outs[j][i * size : (i + 1) * size] = total.astype(outs[j].dtype)


def layer_kernel(
    rep, count, own_blocks, j, place_ref, flipped_ref, cotangent_ref, weight_ref, bias_ref, *refs
):
    first, last = j == 0, j == 1
    piece_ref, refs = refs[0], refs[1:]
    if not first:
        (contrib_in, weight_in), refs = refs[:2], refs[2:]
    if last:
        output_ref, send_ref, keep_ref, keep_weight_ref, contrib = refs
    else:
        output_ref, contrib, weight_out = refs
    rows, _, size = flipped_ref.shape
    share = rows // rep
    quarter_blocks = contrib.shape[0]
    nodes = own_blocks * size
    contrib[...] = jnp.zeros_like(contrib) if first else contrib_in[...]

    target = lax.axis_index("rep") ^ j
    aggregated = piece_ref[...]
    part = aggregated.shape[0]
    here = pl.ds(pl.multiple_of(target * part, part), part)
    hidden = matmul(aggregated, weight_ref[...], (1, 0)) + bias_ref[...]
    gate_prob = jax.nn.sigmoid(hidden)
    output_ref[...] = (hidden * gate_prob).astype(BF16)
    grad_hidden = (
        cotangent_ref[here, :].astype(F32) * gate_prob * (1.0 + hidden * (1.0 - gate_prob))
    ).astype(BF16)
    weight_part = matmul(aggregated, grad_hidden, (0, 0))
    if not first:
        weight_part = weight_in[...] + weight_part
    grad_agg = matmul(grad_hidden, weight_ref[...], (1, 1)).astype(BF16)
    for i in range(share):
        row = target * share + i
        terms = matmul(flipped_ref[row], grad_agg[i * size : (i + 1) * size], (1, 0))
        for k in range(count):
            contrib[place_ref[row * count + k, 0]] += terms[k * size : (k + 1) * size]
    if not last:
        weight_out[...] = weight_part
        return
    chips = keep_ref.shape[0]
    half = quarter_blocks // 2
    keep_ref[...] = contrib[:half].reshape(keep_ref.shape)
    send_ref[: chips * nodes] = contrib[half:].reshape(chips * nodes, -1).astype(BF16)
    send_ref[chips * nodes :] = weight_part.astype(BF16)
    keep_weight_ref[...] = weight_part.astype(BF16)


def add_kernel(a_ref, b_ref, out_ref):
    out_ref[...] = (a_ref[...] + b_ref[...].astype(F32)).astype(out_ref.dtype)


def place_kernel(order, *refs):
    pieces, out_ref = refs[:-1], refs[-1]
    part = pieces[0].shape[0]
    for j, piece in zip(order, pieces):
        target = lax.axis_index("rep") ^ j
        out_ref[pl.ds(pl.multiple_of(target * part, part), part), :] = piece[...]


def pair_kernel(keep_ref, keep_weight_ref, got_ref, own_ref, own_weight_ref, *outs):
    chips, nodes, _ = keep_ref.shape
    both = keep_weight_ref[...].astype(F32) + got_ref[chips * nodes :].astype(F32)
    both = both.astype(BF16)
    own_weight_ref[...] = both
    own_ref[...] = keep_ref[0] + got_ref[:nodes].astype(F32)
    for chip in range(1, chips):
        total = keep_ref[chip] + got_ref[chip * nodes : (chip + 1) * nodes].astype(F32)
        outs[chip - 1][:nodes] = total.astype(BF16)
        outs[chip - 1][nodes:] = both


def total_of(values):
    while len(values) > 1:
        values = [a + b for a, b in zip(values[::2], values[1::2])]
    return values[0]


def half_kernel(levels, *refs):
    for level in range(1, levels):
        first = 1 << level
        got = refs[: -levels + 1][::-1][first - 2 : 2 * first - 2]
        refs[level - levels][...] = total_of([g[...].astype(F32) for g in got])


def final_kernel(own_ref, own_weight_ref, got_ref, *refs):
    later, (feature_ref, weight_ref) = refs[:-2], refs[-2:]
    nodes = own_ref.shape[0]
    feature = own_ref[...] + got_ref[:nodes].astype(F32)
    weight = own_weight_ref[...].astype(F32) + got_ref[nodes:].astype(F32)
    for value in later:
        feature += value[:nodes]
        weight += value[nodes:]
    feature_ref[...] = feature
    weight_ref[...] = weight


def shape(dims, dtype):
    return jax.ShapeDtypeStruct(dims, dtype)


def body(cols, vals, features, weight, bias, cotangent):
    rows, count, size, _ = vals.shape
    nodes, width = features.shape
    dom, rep = lax.axis_size("dom"), lax.axis_size("rep")
    chips = dom // 2
    own_blocks = nodes // size
    quarter_blocks = own_blocks * dom
    part = rows * size // rep
    params = pltpu.CompilerParams(vmem_limit_bytes=(8 + dom // 2) * 1024 * 1024)

    def call(kernel, out_shape, in_specs, scratch=()):
        single = not isinstance(out_shape, list)
        return pl.pallas_call(
            kernel,
            out_shape=out_shape,
            in_specs=in_specs,
            out_specs=VMEM if single else [VMEM] * len(out_shape),
            scratch_shapes=scratch,
            compiler_params=params,
        )

    bias = bias.reshape(1, width)
    flipped, place = call(
        functools.partial(early_kernel, own_blocks, dom),
        [shape((rows, count * size, size), BF16), shape((rows * count, 128), jnp.int32)],
        [VMEM] * 3,
    )(cols, vals, bias)
    order = list(range(chips - 1, -1, -1))
    across = [swap(features, "dom", 2 * chip) for chip in order[:-1]] + [features]
    mine = call(
        functools.partial(join_kernel, order), shape((chips * nodes, width), BF16), [VMEM] * (chips + 1)
    )(*across, place)
    far = swap(mine, "dom", 1)

    partials = call(
        functools.partial(aggregate_kernel, rep),
        [shape((part, width), BF16 if j else F32) for j in range(rep)],
        [VMEM] * 4,
    )(place, vals, mine, far)
    arrived = {j: swap(partials[j], "rep", j) if j else partials[j] for j in range(rep)}
    own_rows = arrived[0]
    for j in range(rep - 1, 0, -1):
        own_rows = call(add_kernel, shape((part, width), F32 if j > 1 else BF16), [VMEM] * 2)(
            own_rows, arrived[j]
        )

    pieces = {0: own_rows}
    for j in range(rep - 1, 0, -1):
        pieces[j] = swap(own_rows, "rep", j)

    outputs, carried = [], []
    for j, piece in pieces.items():
        if j != 1:
            outs = [shape((quarter_blocks, size, width), F32), shape((width, width), F32)]
            scratch = []
        else:
            outs = [
                shape((chips * nodes + width, width), BF16),
                shape((chips, nodes, width), F32),
                shape((width, width), BF16),
            ]
            scratch = [pltpu.VMEM((quarter_blocks, size, width), F32)]
        output, *carried = call(
            functools.partial(layer_kernel, rep, count, own_blocks, j),
            [shape((part, width), BF16)] + outs,
            [VMEM] * (6 + len(carried)),
            scratch,
        )(place, flipped, cotangent, weight, bias, piece, *carried)
        outputs.append(output)
    send, keep, keep_weight = carried

    own, own_weight, *sends = call(
        pair_kernel,
        [shape((nodes, width), F32), shape((width, width), BF16)]
        + [shape((nodes + width, width), BF16)] * (chips - 1),
        [VMEM] * 3,
    )(keep, keep_weight, swap(send, "dom", 1))
    got = {chip: swap(sends[chip - 1], "dom", 2 * chip) for chip in range(chips - 1, 0, -1)}
    output = call(
        functools.partial(place_kernel, list(pieces)), shape((rows * size, width), BF16), [VMEM] * rep
    )(*outputs)
    levels = chips.bit_length() - 1
    later = call(
        functools.partial(half_kernel, levels), [shape((nodes + width, width), F32)] * (levels - 1), [VMEM] * (chips - 2)
    )(*[got[chip] for chip in range(chips - 1, 1, -1)])
    feature_grad, weight_grad = call(
        final_kernel,
        [shape((nodes, width), F32), shape((width, width), F32)],
        [VMEM] * (levels + 2),
    )(own, own_weight, got[1], *later)
    return output, feature_grad, weight_grad


def solution(mesh):
    placed = (
        P("dom", "rep"),
        P("dom", "rep", None, None),
        P(("rep", "dom"), None),
        P(),
        P(),
        P("dom", None),
    )
    return jax.shard_map(
        body,
        mesh=mesh,
        in_specs=placed,
        out_specs=(P("dom", None), P(("rep", "dom"), None), P()),
        check_vma=False,
    )
```

```python
import functools

import jax
import jax.numpy as jnp
from jax import lax
from jax.experimental import pallas as pl
from jax.experimental.pallas import tpu as pltpu
from jax.sharding import PartitionSpec as P

BF16 = jnp.bfloat16
F32 = jnp.float32
VMEM = pl.BlockSpec(memory_space=pltpu.VMEM)


def swap(value, axis, distance):
    size = lax.axis_size(axis)
    return lax.ppermute(value, axis, [(i, i ^ distance) for i in range(size)])


def matmul(a, b, contract):
    return lax.dot_general(a, b, ((contract[:1], contract[1:]), ((), ())), preferred_element_type=F32)


def early_kernel(vals_ref, features_ref, flipped_ref, own_ref):
    rows, count, size, _ = vals_ref.shape
    own_ref[...] = features_ref[...]
    for row in range(rows):
        for k in range(count):
            flipped_ref[row, k * size : (k + 1) * size] = vals_ref[row, k].T


def place_kernel(own_blocks, dom, cols_ref, _, place_ref):
    count, rows = cols_ref.shape
    for row in range(rows):
        for k in range(count):
            col = cols_ref[k, row] - lax.axis_index("rep") * (own_blocks * dom)
            owner = lax.div(col, jnp.int32(own_blocks)) ^ lax.axis_index("dom")
            place = ((owner & 1) * (dom // 2) + (owner >> 1)) * own_blocks
            place += lax.rem(col, jnp.int32(own_blocks))
            place_ref[row * count + k : row * count + k + 1, :] = jnp.full((1, 128), place, jnp.int32)


def join_kernel(*refs):
    pieces, out_ref = refs[:-1], refs[-1]
    first = 0
    for piece in pieces:
        out_ref[first : first + piece.shape[0]] = piece[...]
        first += piece.shape[0]


def last_join_kernel(*refs):
    near, middle, out_ref = refs[:-2], refs[-2], refs[-1]
    nodes = near[0].shape[0]
    body = middle.shape[0] - 2 * nodes
    out_ref[:nodes] = middle[body : body + nodes]
    first = nodes
    for piece in near:
        out_ref[first : first + nodes] = piece[...]
        first += nodes
    out_ref[first : first + body] = middle[:body]
    out_ref[first + body :] = middle[body + nodes :]


def aggregate_kernel(rep, place_ref, vals_ref, mine_ref, far_ref, *outs):
    rows, count, size, _ = vals_ref.shape
    half = mine_ref.shape[0] // size
    share = rows // rep
    for j in range(rep - 1, -1, -1):
        target = lax.axis_index("rep") ^ j
        for i in range(share):
            row = target * share + i
            total = None
            for k in range(count):
                place = place_ref[row * count + k, 0]
                beyond = place >= half
                index = jnp.where(beyond, place - half, place)
                here = pl.ds(pl.multiple_of(index * size, size), size)
                block = jnp.where(beyond, far_ref[here, :], mine_ref[here, :])
                term = matmul(vals_ref[row, k], block, (1, 0))
                total = term if total is None else total + term
            outs[j][i * size : (i + 1) * size] = total.astype(outs[j].dtype)


def layer_kernel(
    rep, count, own_blocks, j, place_ref, flipped_ref, cotangent_ref, weight_ref, bias_ref, *refs
):
    first, last = j == 0, j == 1
    piece_ref, refs = refs[0], refs[1:]
    if not first:
        (contrib_in, weight_in), refs = refs[:2], refs[2:]
    if last:
        output_ref, send_ref, keep_ref, keep_weight_ref, contrib = refs
    else:
        output_ref, contrib, weight_out = refs
    rows, _, size = flipped_ref.shape
    share = rows // rep
    quarter_blocks = contrib.shape[0]
    nodes = own_blocks * size
    contrib[...] = jnp.zeros_like(contrib) if first else contrib_in[...]

    target = lax.axis_index("rep") ^ j
    aggregated = piece_ref[...]
    part = aggregated.shape[0]
    here = pl.ds(pl.multiple_of(target * part, part), part)
    hidden = matmul(aggregated, weight_ref[...], (1, 0)) + bias_ref[...]
    gate_prob = jax.nn.sigmoid(hidden)
    output_ref[...] = (hidden * gate_prob).astype(BF16)
    grad_hidden = (
        cotangent_ref[here, :].astype(F32) * gate_prob * (1.0 + hidden * (1.0 - gate_prob))
    ).astype(BF16)
    weight_part = matmul(aggregated, grad_hidden, (0, 0))
    if not first:
        weight_part = weight_in[...] + weight_part
    grad_agg = matmul(grad_hidden, weight_ref[...], (1, 1)).astype(BF16)
    for i in range(share):
        row = target * share + i
        terms = matmul(flipped_ref[row], grad_agg[i * size : (i + 1) * size], (1, 0))
        for k in range(count):
            contrib[place_ref[row * count + k, 0]] += terms[k * size : (k + 1) * size]
    if not last:
        weight_out[...] = weight_part
        return
    chips = keep_ref.shape[0]
    half = quarter_blocks // 2
    keep_ref[...] = contrib[:half].reshape(keep_ref.shape)
    send_ref[: chips * nodes] = contrib[half:].reshape(chips * nodes, -1).astype(BF16)
    send_ref[chips * nodes :] = weight_part.astype(BF16)
    keep_weight_ref[...] = weight_part.astype(BF16)


def add_kernel(a_ref, b_ref, out_ref):
    out_ref[...] = (a_ref[...] + b_ref[...].astype(F32)).astype(out_ref.dtype)


def order_kernel(order, *refs):
    pieces, out_ref = refs[:-1], refs[-1]
    part = pieces[0].shape[0]
    for j, piece in zip(order, pieces):
        target = lax.axis_index("rep") ^ j
        out_ref[pl.ds(pl.multiple_of(target * part, part), part), :] = piece[...]


def pair_kernel(keep_ref, keep_weight_ref, got_ref, own_ref, own_weight_ref, *outs):
    chips, nodes, _ = keep_ref.shape
    both = keep_weight_ref[...].astype(F32) + got_ref[chips * nodes :].astype(F32)
    both = both.astype(BF16)
    own_weight_ref[...] = both
    own_ref[...] = keep_ref[0] + got_ref[:nodes].astype(F32)
    for chip in range(1, chips):
        total = keep_ref[chip] + got_ref[chip * nodes : (chip + 1) * nodes].astype(F32)
        outs[chip - 1][:nodes] = total.astype(BF16)
        outs[chip - 1][nodes:] = both


def total_of(values):
    while len(values) > 1:
        values = [a + b for a, b in zip(values[::2], values[1::2])]
    return values[0]


def half_kernel(levels, *refs):
    for level in range(1, levels):
        first = 1 << level
        got = refs[: -levels + 1][::-1][first - 2 : 2 * first - 2]
        refs[level - levels][...] = total_of([g[...].astype(F32) for g in got])


def final_kernel(own_ref, own_weight_ref, got_ref, *refs):
    later, (feature_ref, weight_ref) = refs[:-2], refs[-2:]
    nodes = own_ref.shape[0]
    feature = own_ref[...] + got_ref[:nodes].astype(F32)
    weight = own_weight_ref[...].astype(F32) + got_ref[nodes:].astype(F32)
    for value in later:
        feature += value[:nodes]
        weight += value[nodes:]
    feature_ref[...] = feature
    weight_ref[...] = weight


def shape(dims, dtype):
    return jax.ShapeDtypeStruct(dims, dtype)


def body(cols, vals, features, weight, bias, cotangent):
    rows, count, size, _ = vals.shape
    nodes, width = features.shape
    dom, rep = lax.axis_size("dom"), lax.axis_size("rep")
    chips = dom // 2
    own_blocks = nodes // size
    quarter_blocks = own_blocks * dom
    part = rows * size // rep
    params = pltpu.CompilerParams(vmem_limit_bytes=(8 + dom // 2) * 1024 * 1024)

    def call(kernel, out_shape, in_specs, scratch=()):
        single = not isinstance(out_shape, list)
        return pl.pallas_call(
            kernel,
            out_shape=out_shape,
            in_specs=in_specs,
            out_specs=VMEM if single else [VMEM] * len(out_shape),
            scratch_shapes=scratch,
            compiler_params=params,
        )

    flipped, own = call(
        early_kernel,
        [shape((rows, count * size, size), BF16), shape(features.shape, BF16)],
        [VMEM] * 2,
    )(vals, features)

    def join(*values):
        nodes_in = sum(v.shape[0] for v in values)
        return call(join_kernel, shape((nodes_in, width), BF16), [VMEM] * len(values))(*values)

    across = [swap(features, "dom", 2 * chip) for chip in range(1, chips)]
    front = join(own, across[-1])
    middle = join(*across[chips // 2 - 1 : -1], front)
    mine = call(last_join_kernel, shape((chips * nodes, width), BF16), [VMEM] * (chips // 2))(
        *across[: chips // 2 - 1], middle
    )
    far = swap(mine, "dom", 1)
    place = call(
        functools.partial(place_kernel, own_blocks, dom),
        shape((rows * count, 128), jnp.int32),
        [VMEM] * 2,
    )(cols.T, mine)

    partials = call(
        functools.partial(aggregate_kernel, rep),
        [shape((part, width), BF16 if j else F32) for j in range(rep)],
        [VMEM] * 4,
    )(place, vals, mine, far)
    arrived = {j: swap(partials[j], "rep", j) if j else partials[j] for j in range(rep)}
    order = [*range(2, rep), 1]
    own_rows = arrived[0]
    for j in order:
        own_rows = call(add_kernel, shape((part, width), F32 if j > 1 else BF16), [VMEM] * 2)(
            own_rows, arrived[j]
        )
    pieces = {0: own_rows}
    for j in order:
        pieces[j] = swap(own_rows, "rep", j)

    outputs, carried = [], []
    for j, piece in pieces.items():
        if j != 1:
            outs = [shape((quarter_blocks, size, width), F32), shape((width, width), F32)]
            scratch = []
        else:
            outs = [
                shape((chips * nodes + width, width), BF16),
                shape((chips, nodes, width), F32),
                shape((width, width), BF16),
            ]
            scratch = [pltpu.VMEM((quarter_blocks, size, width), F32)]
        output, *carried = call(
            functools.partial(layer_kernel, rep, count, own_blocks, j),
            [shape((part, width), BF16)] + outs,
            [VMEM] * (6 + len(carried)),
            scratch,
        )(place, flipped, cotangent, weight, bias, piece, *carried)
        outputs.append(output)
    send, keep, keep_weight = carried

    own, own_weight, *sends = call(
        pair_kernel,
        [shape((nodes, width), F32), shape((width, width), BF16)]
        + [shape((nodes + width, width), BF16)] * (chips - 1),
        [VMEM] * 3,
    )(keep, keep_weight, swap(send, "dom", 1))
    got = {chip: swap(sends[chip - 1], "dom", 2 * chip) for chip in range(chips - 1, 0, -1)}
    output = call(
        functools.partial(order_kernel, list(pieces)), shape((rows * size, width), BF16), [VMEM] * rep
    )(*outputs)
    levels = chips.bit_length() - 1
    later = call(
        functools.partial(half_kernel, levels), [shape((nodes + width, width), F32)] * (levels - 1), [VMEM] * (chips - 2)
    )(*[got[chip] for chip in range(chips - 1, 1, -1)])
    feature_grad, weight_grad = call(
        final_kernel,
        [shape((nodes, width), F32), shape((width, width), F32)],
        [VMEM] * (levels + 2),
    )(own, own_weight, got[1], *later)
    return output, feature_grad, weight_grad


def solution(mesh):
    placed = (
        P("dom", "rep"),
        P("dom", "rep", None, None),
        P(("rep", "dom"), None),
        P(),
        P(),
        P("dom", None),
    )
    return jax.shard_map(
        body,
        mesh=mesh,
        in_specs=placed,
        out_specs=(P("dom", None), P(("rep", "dom"), None), P()),
        check_vma=False,
    )
```

```python
import functools

import jax
import jax.numpy as jnp
from jax import lax
from jax.experimental import pallas as pl
from jax.experimental.pallas import tpu as pltpu
from jax.sharding import PartitionSpec as P

BF16 = jnp.bfloat16
F32 = jnp.float32
VMEM = pl.BlockSpec(memory_space=pltpu.VMEM)


def swap(value, axis, distance):
    size = lax.axis_size(axis)
    return lax.ppermute(value, axis, [(i, i ^ distance) for i in range(size)])


def matmul(a, b, contract):
    return lax.dot_general(a, b, ((contract[:1], contract[1:]), ((), ())), preferred_element_type=F32)


def early_kernel(vals_ref, features_ref, flipped_ref, own_ref):
    rows, count, size, _ = vals_ref.shape
    own_ref[...] = features_ref[...]
    for row in range(rows):
        for k in range(count):
            flipped_ref[row, k * size : (k + 1) * size] = vals_ref[row, k].T


def place_kernel(own_blocks, dom, cols_ref, _, place_ref):
    count, rows = cols_ref.shape
    for row in range(rows):
        for k in range(count):
            col = cols_ref[k, row] - lax.axis_index("rep") * (own_blocks * dom)
            owner = lax.div(col, jnp.int32(own_blocks)) ^ lax.axis_index("dom")
            place = ((owner & 1) * (dom // 2) + (owner >> 1)) * own_blocks
            place += lax.rem(col, jnp.int32(own_blocks))
            place_ref[row * count + k : row * count + k + 1, :] = jnp.full((1, 128), place, jnp.int32)


def join_kernel(*refs):
    pieces, out_ref = refs[:-1], refs[-1]
    first = 0
    for piece in pieces:
        out_ref[first : first + piece.shape[0]] = piece[...]
        first += piece.shape[0]


def last_join_kernel(*refs):
    near, middle, out_ref = refs[:-2], refs[-2], refs[-1]
    nodes = near[0].shape[0]
    body = middle.shape[0] - 2 * nodes
    out_ref[:nodes] = middle[body : body + nodes]
    first = nodes
    for piece in near:
        out_ref[first : first + nodes] = piece[...]
        first += nodes
    out_ref[first : first + body] = middle[:body]
    out_ref[first + body :] = middle[body + nodes :]


def aggregate_kernel(rep, place_ref, vals_ref, mine_ref, far_ref, *outs):
    rows, count, size, _ = vals_ref.shape
    blocks = mine_ref.shape[0] // size
    share = rows // rep
    for j in (*range(2, rep), 1, 0):
        target = lax.axis_index("rep") ^ j
        for i in range(share):
            row = target * share + i
            total = None
            for k in range(count):
                place = place_ref[row * count + k, 0]
                beyond = place >= blocks
                index = jnp.where(beyond, place - blocks, place)
                here = pl.ds(pl.multiple_of(index * size, size), size)
                block = jnp.where(beyond, far_ref[here, :], mine_ref[here, :])
                term = matmul(vals_ref[row, k], block, (1, 0))
                total = term if total is None else total + term
            half, at = (0, i) if j == 1 else divmod(i, share // 2)
            out_ref = outs[-1] if j == 1 else outs[2 * max(j - 1, 0) + half]
            out_ref[at * size : (at + 1) * size] = total.astype(out_ref.dtype)


def layer_kernel(
    rep, count, own_blocks, segments, stage, place_ref, flipped_ref, cotangent_ref, weight_ref,
    bias_ref, *refs
):
    pieces, refs = refs[: len(segments)], refs[len(segments) :]
    if stage > 0:
        (contrib_in, sums_in), refs = refs[:2], refs[2:]
    if stage == 3:
        output_ref, send_ref, keep_ref, keep_weight_ref, contrib = refs
    else:
        output_ref, contrib, sums_out = refs
    rows, _, size = flipped_ref.shape
    part = rows * size // rep
    quarter_blocks = contrib.shape[0]
    nodes = own_blocks * size
    contrib[...] = contrib_in[...] if stage > 0 else jnp.zeros_like(contrib)

    def joined(values):
        return values[0] if len(values) == 1 else jnp.concatenate(values)

    starts = [(lax.axis_index("rep") ^ j) * part + first for j, first, _ in segments]
    aggregated = joined([piece[...] for piece in pieces])
    gradient = joined(
        [
            cotangent_ref[pl.ds(pl.multiple_of(start, size), length), :]
            for start, (_, _, length) in zip(starts, segments)
        ]
    ).astype(F32)
    hidden = matmul(aggregated, weight_ref[...], (1, 0)) + bias_ref[...]
    gate_prob = jax.nn.sigmoid(hidden)
    output_ref[...] = (hidden * gate_prob).astype(BF16)
    grad_hidden = (gradient * gate_prob * (1.0 + hidden * (1.0 - gate_prob))).astype(BF16)
    grad_agg = matmul(grad_hidden, weight_ref[...], (1, 1)).astype(BF16)

    sums, at = [None, None], 0
    for start, (_, first, length) in zip(starts, segments):
        for i in range(length // size):
            here = slice(at + i * size, at + (i + 1) * size)
            row = lax.div(start, jnp.int32(size)) + i
            terms = matmul(flipped_ref[row], grad_agg[here], (1, 0))
            for k in range(count):
                contrib[place_ref[row * count + k, 0]] += terms[k * size : (k + 1) * size]
        for half in range(first * 2 // part, (first + length) * 2 // part):
            skip = at + half * part // 2 - first
            here = slice(skip, skip + part // 2)
            part_sum = matmul(aggregated[here], grad_hidden[here], (0, 0))
            sums[half] = part_sum if sums[half] is None else sums[half] + part_sum
        at += length

    if stage == 0:
        sums_out[0] = sums_out[1] = jnp.zeros_like(sums[0])
        sums_out[2] = sums[0]
    elif stage == 1:
        sums_out[0], sums_out[1], sums_out[2] = sums[0], sums[1], sums_in[2]
    elif stage == 2:
        sums_out[0], sums_out[1] = sums_in[0] + sums[0], sums_in[1] + sums[1]
        sums_out[2] = sums_in[2]
    if stage < 3:
        return
    weight_part = ((sums_in[0] + sums_in[2]) + (sums_in[1] + sums[1])).astype(BF16)
    chips = keep_ref.shape[0]
    half = quarter_blocks // 2
    keep_ref[...] = contrib[:half].reshape(keep_ref.shape)
    send_ref[: chips * nodes] = contrib[half:].reshape(chips * nodes, -1).astype(BF16)
    send_ref[chips * nodes :] = weight_part
    keep_weight_ref[...] = weight_part


def add_kernel(first, a_ref, b_ref, *refs):
    out_ref = refs[-1]
    b = b_ref[first : first + a_ref.shape[0]]
    out_ref[...] = (a_ref[...] + b.astype(F32)).astype(out_ref.dtype)


def order_kernel(part, stages, *refs):
    pieces, out_ref = refs[:-1], refs[-1]
    for segments, piece in zip(stages, pieces):
        at = 0
        for j, first, length in segments:
            start = (lax.axis_index("rep") ^ j) * part + first
            out_ref[pl.ds(pl.multiple_of(start, 128), length), :] = piece[at : at + length]
            at += length


def pair_kernel(keep_ref, keep_weight_ref, got_ref, own_ref, own_weight_ref, *outs):
    chips, nodes, _ = keep_ref.shape
    both = keep_weight_ref[...].astype(F32) + got_ref[chips * nodes :].astype(F32)
    both = both.astype(BF16)
    own_weight_ref[...] = both
    own_ref[...] = keep_ref[0] + got_ref[:nodes].astype(F32)
    for chip in range(1, chips):
        total = keep_ref[chip] + got_ref[chip * nodes : (chip + 1) * nodes].astype(F32)
        outs[chip - 1][:nodes] = total.astype(BF16)
        outs[chip - 1][nodes:] = both


def total_of(values):
    while len(values) > 1:
        values = [a + b for a, b in zip(values[::2], values[1::2])]
    return values[0]


def half_kernel(levels, *refs):
    for level in range(1, levels):
        first = 1 << level
        got = refs[: -levels + 1][::-1][first - 2 : 2 * first - 2]
        refs[level - levels][...] = total_of([g[...].astype(F32) for g in got])


def final_kernel(own_ref, own_weight_ref, got_ref, *refs):
    later, (feature_ref, weight_ref) = refs[:-2], refs[-2:]
    nodes = own_ref.shape[0]
    feature = own_ref[...] + got_ref[:nodes].astype(F32)
    weight = own_weight_ref[...].astype(F32) + got_ref[nodes:].astype(F32)
    for value in later:
        feature += value[:nodes]
        weight += value[nodes:]
    feature_ref[...] = feature
    weight_ref[...] = weight


def shape(dims, dtype):
    return jax.ShapeDtypeStruct(dims, dtype)


def body(cols, vals, features, weight, bias, cotangent):
    rows, count, size, _ = vals.shape
    nodes, width = features.shape
    dom, rep = lax.axis_size("dom"), lax.axis_size("rep")
    chips = dom // 2
    own_blocks = nodes // size
    quarter_blocks = own_blocks * dom
    part = rows * size // rep
    params = pltpu.CompilerParams(vmem_limit_bytes=(8 + dom // 2) * 1024 * 1024)

    cost = pl.CostEstimate(flops=10**9, bytes_accessed=10**6, transcendentals=0)

    def call(kernel, out_shape, in_specs, scratch=(), cost=None):
        single = not isinstance(out_shape, list)
        return pl.pallas_call(
            kernel,
            out_shape=out_shape,
            in_specs=in_specs,
            out_specs=VMEM if single else [VMEM] * len(out_shape),
            scratch_shapes=scratch,
            compiler_params=params,
            cost_estimate=cost,
        )

    flipped, own = call(
        early_kernel,
        [shape((rows, count * size, size), BF16), shape(features.shape, BF16)],
        [VMEM] * 2,
    )(vals, features)

    def join(*values):
        nodes_in = sum(v.shape[0] for v in values)
        return call(join_kernel, shape((nodes_in, width), BF16), [VMEM] * len(values))(*values)

    across = [swap(features, "dom", 2 * chip) for chip in range(1, chips)]
    front = join(own, across[-1])
    middle = join(*across[chips // 2 - 1 : -1], front)
    mine = call(last_join_kernel, shape((chips * nodes, width), BF16), [VMEM] * (chips // 2))(
        *across[: chips // 2 - 1], middle
    )
    far = swap(mine, "dom", 1)
    place = call(
        functools.partial(place_kernel, own_blocks, dom),
        shape((rows * count, 128), jnp.int32),
        [VMEM] * 2,
    )(cols.T, mine)

    beyond, half = range(2, rep), part // 2
    halves = call(
        functools.partial(aggregate_kernel, rep),
        [shape((half, width), F32)] * 2
        + [shape((half, width), BF16)] * (2 * len(beyond))
        + [shape((part, width), BF16)],
        [VMEM] * 4,
    )(place, vals, mine, far)
    partials = {(j, h): halves[2 * max(j - 1, 0) + h] for j in (0, *beyond) for h in (0, 1)}
    arrived = {(j, 0): swap(partials[j, 0], "rep", j) for j in beyond}
    beside = swap(halves[-1], "rep", 1)
    arrived |= {(j, 1): swap(partials[j, 1], "rep", j) for j in beyond}

    def add(a, b, first, dtype, *after):
        kernel = functools.partial(add_kernel, first)
        return call(kernel, shape(a.shape, dtype), [VMEM] * (2 + len(after)), cost=cost)(a, b, *after)

    own_rows, pieces = {}, {}
    for h in (0, 1):
        total = partials[0, h]
        for j in beyond:
            after = [own_rows[0]] if h == 1 and j == 2 else []
            total = add(total, arrived[j, h], 0, F32, *after)
        own_rows[h] = add(total, beside, h * half, BF16)
        for j in beyond:
            pieces[j, h] = swap(own_rows[h], "rep", j)
    both = call(join_kernel, shape((part, width), BF16), [VMEM] * 2)(own_rows[0], own_rows[1])
    beside = swap(both, "rep", 1)

    stages = [
        [(j, 0, half) for j in beyond],
        [(0, 0, part)],
        [(1, 0, part)],
        [(j, half, half) for j in beyond],
    ]
    blocks = [[pieces[j, 0] for j in beyond], [both], [beside], [pieces[j, 1] for j in beyond]]
    outputs, carried = [], []
    for stage, (segments, values) in enumerate(zip(stages, blocks)):
        if stage < 3:
            outs = [shape((quarter_blocks, size, width), F32), shape((3, width, width), F32)]
            scratch = []
        else:
            outs = [
                shape((chips * nodes + width, width), BF16),
                shape((chips, nodes, width), F32),
                shape((width, width), BF16),
            ]
            scratch = [pltpu.VMEM((quarter_blocks, size, width), F32)]
        output, *carried = call(
            functools.partial(layer_kernel, rep, count, own_blocks, segments, stage),
            [shape((sum(length for _, _, length in segments), width), BF16)] + outs,
            [VMEM] * (5 + len(values) + len(carried)),
            scratch,
            cost=cost,
        )(place, flipped, cotangent, weight, bias.reshape(1, width), *values, *carried)
        outputs.append(output)
    send, keep, keep_weight = carried

    own, own_weight, *sends = call(
        pair_kernel,
        [shape((nodes, width), F32), shape((width, width), BF16)]
        + [shape((nodes + width, width), BF16)] * (chips - 1),
        [VMEM] * 3,
    )(keep, keep_weight, swap(send, "dom", 1))
    got = {chip: swap(sends[chip - 1], "dom", 2 * chip) for chip in range(chips - 1, 0, -1)}
    output = call(
        functools.partial(order_kernel, part, stages), shape((rows * size, width), BF16), [VMEM] * 4
    )(*outputs)
    levels = chips.bit_length() - 1
    later = call(
        functools.partial(half_kernel, levels), [shape((nodes + width, width), F32)] * (levels - 1), [VMEM] * (chips - 2)
    )(*[got[chip] for chip in range(chips - 1, 1, -1)])
    feature_grad, weight_grad = call(
        final_kernel,
        [shape((nodes, width), F32), shape((width, width), F32)],
        [VMEM] * (levels + 2),
    )(own, own_weight, got[1], *later)
    return output, feature_grad, weight_grad


def solution(mesh):
    placed = (
        P("dom", "rep"),
        P("dom", "rep", None, None),
        P(("rep", "dom"), None),
        P(),
        P(),
        P("dom", None),
    )
    return jax.shard_map(
        body,
        mesh=mesh,
        in_specs=placed,
        out_specs=(P("dom", None), P(("rep", "dom"), None), P()),
        check_vma=False,
    )
```

```python
import functools

import jax
import jax.numpy as jnp
from jax import lax
from jax.experimental import pallas as pl
from jax.experimental.pallas import tpu as pltpu
from jax.sharding import PartitionSpec as P

BF16 = jnp.bfloat16
F32 = jnp.float32
VMEM = pl.BlockSpec(memory_space=pltpu.VMEM)


def swap(value, axis, distance):
    size = lax.axis_size(axis)
    return lax.ppermute(value, axis, [(i, i ^ distance) for i in range(size)])


def matmul(a, b, contract):
    return lax.dot_general(a, b, ((contract[:1], contract[1:]), ((), ())), preferred_element_type=F32)


def early_kernel(vals_ref, features_ref, flipped_ref, own_ref):
    rows, count, size, _ = vals_ref.shape
    own_ref[...] = features_ref[...]
    for row in range(rows):
        for k in range(count):
            flipped_ref[row, k * size : (k + 1) * size] = vals_ref[row, k].T


def place_kernel(own_blocks, dom, cols_ref, _, place_ref):
    count, rows = cols_ref.shape
    for row in range(rows):
        for k in range(count):
            col = cols_ref[k, row] - lax.axis_index("rep") * (own_blocks * dom)
            owner = lax.div(col, jnp.int32(own_blocks)) ^ lax.axis_index("dom")
            place = ((owner & 1) * (dom // 2) + (owner >> 1)) * own_blocks
            place += lax.rem(col, jnp.int32(own_blocks))
            place_ref[row * count + k : row * count + k + 1, :] = jnp.full((1, 128), place, jnp.int32)


def join_kernel(*refs):
    pieces, out_ref = refs[:-1], refs[-1]
    first = 0
    for piece in pieces:
        out_ref[first : first + piece.shape[0]] = piece[...]
        first += piece.shape[0]


def last_join_kernel(*refs):
    near, middle, out_ref = refs[:-2], refs[-2], refs[-1]
    nodes = near[0].shape[0]
    body = middle.shape[0] - 2 * nodes
    out_ref[:nodes] = middle[body : body + nodes]
    first = nodes
    for piece in near:
        out_ref[first : first + nodes] = piece[...]
        first += nodes
    out_ref[first : first + body] = middle[:body]
    out_ref[first + body :] = middle[body + nodes :]


def aggregate_kernel(rep, place_ref, vals_ref, mine_ref, far_ref, *outs):
    rows, count, size, _ = vals_ref.shape
    half = mine_ref.shape[0] // size
    share = rows // rep
    for j in range(rep - 1, -1, -1):
        target = lax.axis_index("rep") ^ j
        for i in range(share):
            row = target * share + i
            total = None
            for k in range(count):
                place = place_ref[row * count + k, 0]
                beyond = place >= half
                index = jnp.where(beyond, place - half, place)
                here = pl.ds(pl.multiple_of(index * size, size), size)
                block = jnp.where(beyond, far_ref[here, :], mine_ref[here, :])
                term = matmul(vals_ref[row, k], block, (1, 0))
                total = term if total is None else total + term
            outs[j][i * size : (i + 1) * size] = total.astype(outs[j].dtype)


def layer_kernel(
    rep, count, own_blocks, j, place_ref, flipped_ref, cotangent_ref, weight_ref, bias_ref, *refs
):
    first, last = j == 0, j == 1
    piece_ref, refs = refs[0], refs[1:]
    if not first:
        (contrib_in, sums_in), refs = refs[:2], refs[2:]
    if last:
        output_ref, first_ref, rest_ref, keep_ref, contrib = refs
    else:
        output_ref, contrib, sums_out = refs
    rows, _, size = flipped_ref.shape
    share = rows // rep
    quarter_blocks = contrib.shape[0]
    nodes = own_blocks * size
    contrib[...] = jnp.zeros_like(contrib) if first else contrib_in[...]

    target = lax.axis_index("rep") ^ j
    aggregated = piece_ref[...]
    part = aggregated.shape[0]
    here = pl.ds(pl.multiple_of(target * part, part), part)
    hidden = matmul(aggregated, weight_ref[...], (1, 0)) + bias_ref[...]
    gate_prob = jax.nn.sigmoid(hidden)
    output_ref[...] = (hidden * gate_prob).astype(BF16)
    grad_hidden = (
        cotangent_ref[here, :].astype(F32) * gate_prob * (1.0 + hidden * (1.0 - gate_prob))
    ).astype(BF16)
    part_sum = matmul(aggregated, grad_hidden, (0, 0))
    grad_agg = matmul(grad_hidden, weight_ref[...], (1, 1)).astype(BF16)
    for i in range(share):
        row = target * share + i
        terms = matmul(flipped_ref[row], grad_agg[i * size : (i + 1) * size], (1, 0))
        for k in range(count):
            contrib[place_ref[row * count + k, 0]] += terms[k * size : (k + 1) * size]
    if first:
        sums_out[0] = part_sum
        sums_out[1] = jnp.zeros_like(part_sum)
    elif not last:
        sums_out[0] = sums_in[0]
        sums_out[1] = sums_in[1] + part_sum
    if not last:
        return
    half = quarter_blocks // 2
    keep_ref[...] = contrib[:half].reshape(keep_ref.shape)
    away = contrib[half:].reshape(half * size, -1).astype(BF16)
    rest_ref[...] = away[:-nodes]
    first_ref[:nodes] = away[-nodes:]
    first_ref[nodes:] = ((sums_in[0] + part_sum) + sums_in[1]).astype(BF16)


def add_kernel(a_ref, b_ref, out_ref):
    out_ref[...] = (a_ref[...] + b_ref[...].astype(F32)).astype(out_ref.dtype)


def order_kernel(order, *refs):
    pieces, out_ref = refs[:-1], refs[-1]
    part = pieces[0].shape[0]
    for j, piece in zip(order, pieces):
        target = lax.axis_index("rep") ^ j
        out_ref[pl.ds(pl.multiple_of(target * part, part), part), :] = piece[...]


def first_pair_kernel(keep_ref, sent_ref, got_ref, out_ref):
    chips, nodes, _ = keep_ref.shape
    out_ref[:nodes] = (keep_ref[chips - 1] + got_ref[:nodes].astype(F32)).astype(BF16)
    out_ref[nodes:] = (sent_ref[nodes:].astype(F32) + got_ref[nodes:].astype(F32)).astype(BF16)


def rest_pair_kernel(keep_ref, first_ref, got_ref, own_ref, *outs):
    chips, nodes, _ = keep_ref.shape
    own_ref[...] = keep_ref[0] + got_ref[:nodes].astype(F32)
    for chip in range(1, chips - 1):
        total = keep_ref[chip] + got_ref[chip * nodes : (chip + 1) * nodes].astype(F32)
        outs[chip - 1][:nodes] = total.astype(BF16)
        outs[chip - 1][nodes:] = first_ref[nodes:]


def total_of(values):
    while len(values) > 1:
        values = [a + b for a, b in zip(values[::2], values[1::2])]
    return values[0]


def lift_kernel(got_ref, out_ref):
    out_ref[...] = got_ref[...].astype(F32)


def half_kernel(levels, *refs):
    for level in range(1, levels):
        first = 1 << level
        got = refs[first - 2 : 2 * first - 2]
        refs[level - levels][...] = total_of([g[...].astype(F32) for g in got])


def final_kernel(own_ref, sent_ref, got_ref, *refs):
    later, (feature_ref, weight_ref) = refs[:-2], refs[-2:]
    nodes = own_ref.shape[0]
    feature = own_ref[...] + got_ref[:nodes].astype(F32)
    weight = sent_ref[nodes:].astype(F32) + got_ref[nodes:].astype(F32)
    for value in later:
        feature += value[:nodes]
        weight += value[nodes:]
    feature_ref[...] = feature
    weight_ref[...] = weight


def shape(dims, dtype):
    return jax.ShapeDtypeStruct(dims, dtype)


def body(cols, vals, features, weight, bias, cotangent):
    rows, count, size, _ = vals.shape
    nodes, width = features.shape
    dom, rep = lax.axis_size("dom"), lax.axis_size("rep")
    chips = dom // 2
    own_blocks = nodes // size
    quarter_blocks = own_blocks * dom
    part = rows * size // rep
    params = pltpu.CompilerParams(vmem_limit_bytes=(8 + dom // 2) * 1024 * 1024)

    def call(kernel, out_shape, in_specs, scratch=(), cost=0):
        single = not isinstance(out_shape, list)
        return pl.pallas_call(
            kernel,
            out_shape=out_shape,
            in_specs=in_specs,
            out_specs=VMEM if single else [VMEM] * len(out_shape),
            scratch_shapes=scratch,
            compiler_params=params,
            cost_estimate=pl.CostEstimate(flops=cost, bytes_accessed=0, transcendentals=0),
        )

    flipped, own = call(
        early_kernel,
        [shape((rows, count * size, size), BF16), shape(features.shape, BF16)],
        [VMEM] * 2,
    )(vals, features)

    def join(*values):
        nodes_in = sum(v.shape[0] for v in values)
        return call(join_kernel, shape((nodes_in, width), BF16), [VMEM] * len(values))(*values)

    across = [swap(features, "dom", 2 * chip) for chip in range(1, chips)]
    front = join(own, across[-1])
    middle = join(*across[chips // 2 - 1 : -1], front)
    mine = call(last_join_kernel, shape((chips * nodes, width), BF16), [VMEM] * (chips // 2))(
        *across[: chips // 2 - 1], middle
    )
    far = swap(mine, "dom", 1)
    place = call(
        functools.partial(place_kernel, own_blocks, dom),
        shape((rows * count, 128), jnp.int32),
        [VMEM] * 2,
    )(cols.T, mine)

    partials = call(
        functools.partial(aggregate_kernel, rep),
        [shape((part, width), BF16 if j else F32) for j in range(rep)],
        [VMEM] * 4,
    )(place, vals, mine, far)
    arrived = {j: swap(partials[j], "rep", j) if j else partials[j] for j in range(rep)}
    order = range(rep - 1, 0, -1)
    own_rows = arrived[0]
    for j in order:
        own_rows = call(add_kernel, shape((part, width), F32 if j > 1 else BF16), [VMEM] * 2)(
            own_rows, arrived[j]
        )
    pieces = {0: own_rows}
    for j in order:
        pieces[j] = swap(own_rows, "rep", j)

    outputs, carried = [], []
    for j, piece in pieces.items():
        if j != 1:
            outs = [shape((quarter_blocks, size, width), F32), shape((2, width, width), F32)]
            scratch = []
        else:
            outs = [
                shape((nodes + width, width), BF16),
                shape(((chips - 1) * nodes, width), BF16),
                shape((chips, nodes, width), F32),
            ]
            scratch = [pltpu.VMEM((quarter_blocks, size, width), F32)]
        output, *carried = call(
            functools.partial(layer_kernel, rep, count, own_blocks, j),
            [shape((part, width), BF16)] + outs,
            [VMEM] * (6 + len(carried)),
            scratch,
        )(place, flipped, cotangent, weight, bias, piece, *carried)
        outputs.append(output)
    first, rest, keep = carried

    message = shape((nodes + width, width), BF16)
    got_first, got_rest = swap(first, "dom", 1), swap(rest, "dom", 1)
    sends = [call(first_pair_kernel, message, [VMEM] * 3, cost=5000000000)(keep, first, got_first)]
    own, *others = call(
        rest_pair_kernel, [shape((nodes, width), F32)] + [message] * (chips - 2), [VMEM] * 3, cost=1000000000
    )(keep, sends[0], got_rest)
    sends = others + sends
    got = {chip: swap(sends[chip - 1], "dom", 2 * chip) for chip in range(chips - 1, 0, -1)}
    output = call(
        functools.partial(order_kernel, list(pieces)), shape((rows * size, width), BF16), [VMEM] * rep
    )(*outputs)
    levels = chips.bit_length() - 1
    total = shape(message.shape, F32)
    got[chips - 1] = call(lift_kernel, total, [VMEM], cost=1000000000)(got[chips - 1])
    later = call(
        functools.partial(half_kernel, levels), [total] * (levels - 1), [VMEM] * (chips - 2), cost=0
    )(*[got[chip] for chip in range(2, chips)])
    feature_grad, weight_grad = call(
        final_kernel,
        [shape((nodes, width), F32), shape((width, width), F32)],
        [VMEM] * (levels + 2),
    )(own, sends[-1], got[1], *later)
    return output, feature_grad, weight_grad


def solution(mesh):
    placed = (
        P("dom", "rep"),
        P("dom", "rep", None, None),
        P(("rep", "dom"), None),
        P(),
        P(),
        P("dom", None),
    )
    return jax.shard_map(
        body,
        mesh=mesh,
        in_specs=placed,
        out_specs=(P("dom", None), P(("rep", "dom"), None), P()),
        check_vma=False,
    )
```

```python
import functools

import jax
import jax.numpy as jnp
from jax import lax
from jax.experimental import pallas as pl
from jax.experimental.pallas import tpu as pltpu
from jax.sharding import PartitionSpec as P

BF16 = jnp.bfloat16
F32 = jnp.float32
VMEM = pl.BlockSpec(memory_space=pltpu.VMEM)


def swap(value, axis, distance):
    size = lax.axis_size(axis)
    return lax.ppermute(value, axis, [(i, i ^ distance) for i in range(size)])


def matmul(a, b, contract):
    return lax.dot_general(a, b, ((contract[:1], contract[1:]), ((), ())), preferred_element_type=F32)


def early_kernel(vals_ref, features_ref, flipped_ref, own_ref):
    rows, count, size, _ = vals_ref.shape
    own_ref[...] = features_ref[...]
    for row in range(rows):
        for k in range(count):
            flipped_ref[row, k * size : (k + 1) * size] = vals_ref[row, k].T


def place_kernel(own_blocks, dom, cols_ref, _, place_ref):
    count, rows = cols_ref.shape
    for row in range(rows):
        for k in range(count):
            col = cols_ref[k, row] - lax.axis_index("rep") * (own_blocks * dom)
            owner = lax.div(col, jnp.int32(own_blocks)) ^ lax.axis_index("dom")
            place = ((owner & 1) * (dom // 2) + (owner >> 1)) * own_blocks
            place += lax.rem(col, jnp.int32(own_blocks))
            place_ref[row * count + k : row * count + k + 1, :] = jnp.full((1, 128), place, jnp.int32)


def join_kernel(*refs):
    pieces, out_ref = refs[:-1], refs[-1]
    first = 0
    for piece in pieces:
        out_ref[first : first + piece.shape[0]] = piece[...]
        first += piece.shape[0]


def last_join_kernel(*refs):
    near, middle, out_ref = refs[:-2], refs[-2], refs[-1]
    nodes = near[0].shape[0]
    body = middle.shape[0] - 2 * nodes
    out_ref[:nodes] = middle[body : body + nodes]
    first = nodes
    for piece in near:
        out_ref[first : first + nodes] = piece[...]
        first += nodes
    out_ref[first : first + body] = middle[:body]
    out_ref[first + body :] = middle[body + nodes :]


def aggregate_kernel(rep, place_ref, vals_ref, mine_ref, far_ref, *outs):
    rows, count, size, _ = vals_ref.shape
    half = mine_ref.shape[0] // size
    share = rows // rep
    for j in range(rep - 1, -1, -1):
        target = lax.axis_index("rep") ^ j
        for i in range(share):
            row = target * share + i
            total = None
            for k in range(count):
                place = place_ref[row * count + k, 0]
                beyond = place >= half
                index = jnp.where(beyond, place - half, place)
                here = pl.ds(pl.multiple_of(index * size, size), size)
                block = jnp.where(beyond, far_ref[here, :], mine_ref[here, :])
                term = matmul(vals_ref[row, k], block, (1, 0))
                total = term if total is None else total + term
            outs[j][i * size : (i + 1) * size] = total.astype(outs[j].dtype)


def layer_kernel(
    rep, count, own_blocks, j, place_ref, flipped_ref, cotangent_ref, weight_ref, bias_ref, *refs
):
    first, last = j == 0, j == 3
    piece_ref, refs = refs[0], refs[1:]
    if not first:
        (contrib_in, sums_in), refs = refs[:2], refs[2:]
    if last:
        output_ref, first_ref, rest_ref, keep_ref, contrib = refs
    else:
        output_ref, contrib, sums_out = refs
    rows, _, size = flipped_ref.shape
    share = rows // rep
    quarter_blocks = contrib.shape[0]
    nodes = own_blocks * size
    contrib[...] = jnp.zeros_like(contrib) if first else contrib_in[...]

    target = lax.axis_index("rep") ^ j
    aggregated = piece_ref[...]
    part = aggregated.shape[0]
    here = pl.ds(pl.multiple_of(target * part, part), part)
    hidden = matmul(aggregated, weight_ref[...], (1, 0)) + bias_ref[...]
    gate_prob = jax.nn.sigmoid(hidden)
    output_ref[...] = (hidden * gate_prob).astype(BF16)
    grad_hidden = (
        cotangent_ref[here, :].astype(F32) * gate_prob * (1.0 + hidden * (1.0 - gate_prob))
    ).astype(BF16)
    part_sum = matmul(aggregated, grad_hidden, (0, 0))
    grad_agg = matmul(grad_hidden, weight_ref[...], (1, 1)).astype(BF16)
    for i in range(share):
        row = target * share + i
        terms = matmul(flipped_ref[row], grad_agg[i * size : (i + 1) * size], (1, 0))
        for k in range(count):
            contrib[place_ref[row * count + k, 0]] += terms[k * size : (k + 1) * size]
    if j == 0:
        sums_out[0] = part_sum
        sums_out[1] = jnp.zeros_like(part_sum)
    elif j == 2:
        sums_out[0] = sums_in[0]
        sums_out[1] = part_sum
    elif j == 1:
        sums_out[0] = sums_in[0] + part_sum
        sums_out[1] = sums_in[1]
    if not last:
        return
    half = quarter_blocks // 2
    keep_ref[...] = contrib[:half].reshape(keep_ref.shape)
    away = contrib[half:].reshape(half * size, -1).astype(BF16)
    rest_ref[...] = away[:-nodes]
    first_ref[:nodes] = away[-nodes:]
    first_ref[nodes:] = (sums_in[0] + (sums_in[1] + part_sum)).astype(BF16)


def add_kernel(a_ref, b_ref, out_ref):
    out_ref[...] = (a_ref[...] + b_ref[...].astype(F32)).astype(out_ref.dtype)


def order_kernel(order, *refs):
    pieces, out_ref = refs[:-1], refs[-1]
    part = pieces[0].shape[0]
    for j, piece in zip(order, pieces):
        target = lax.axis_index("rep") ^ j
        out_ref[pl.ds(pl.multiple_of(target * part, part), part), :] = piece[...]


def first_pair_kernel(keep_ref, sent_ref, got_ref, out_ref):
    chips, nodes, _ = keep_ref.shape
    out_ref[:nodes] = (keep_ref[chips - 1] + got_ref[:nodes].astype(F32)).astype(BF16)
    out_ref[nodes:] = (sent_ref[nodes:].astype(F32) + got_ref[nodes:].astype(F32)).astype(BF16)


def rest_pair_kernel(keep_ref, first_ref, got_ref, own_ref, *outs):
    chips, nodes, _ = keep_ref.shape
    own_ref[...] = keep_ref[0] + got_ref[:nodes].astype(F32)
    for chip in range(1, chips - 1):
        total = keep_ref[chip] + got_ref[chip * nodes : (chip + 1) * nodes].astype(F32)
        outs[chip - 1][:nodes] = total.astype(BF16)
        outs[chip - 1][nodes:] = first_ref[nodes:]


def total_of(values):
    while len(values) > 1:
        values = [a + b for a, b in zip(values[::2], values[1::2])]
    return values[0]


def lift_kernel(got_ref, out_ref):
    out_ref[...] = got_ref[...].astype(F32)


def half_kernel(levels, *refs):
    for level in range(1, levels):
        first = 1 << level
        got = refs[first - 2 : 2 * first - 2]
        refs[level - levels][...] = total_of([g[...].astype(F32) for g in got])


def final_kernel(own_ref, sent_ref, got_ref, *refs):
    later, (feature_ref, weight_ref) = refs[:-2], refs[-2:]
    nodes = own_ref.shape[0]
    feature = own_ref[...] + got_ref[:nodes].astype(F32)
    weight = sent_ref[nodes:].astype(F32) + got_ref[nodes:].astype(F32)
    for value in later:
        feature += value[:nodes]
        weight += value[nodes:]
    feature_ref[...] = feature
    weight_ref[...] = weight


def shape(dims, dtype):
    return jax.ShapeDtypeStruct(dims, dtype)


def body(cols, vals, features, weight, bias, cotangent):
    rows, count, size, _ = vals.shape
    nodes, width = features.shape
    dom, rep = lax.axis_size("dom"), lax.axis_size("rep")
    chips = dom // 2
    own_blocks = nodes // size
    quarter_blocks = own_blocks * dom
    part = rows * size // rep
    params = pltpu.CompilerParams(vmem_limit_bytes=(8 + dom // 2) * 1024 * 1024)

    def call(kernel, out_shape, in_specs, scratch=(), cost=0):
        single = not isinstance(out_shape, list)
        return pl.pallas_call(
            kernel,
            out_shape=out_shape,
            in_specs=in_specs,
            out_specs=VMEM if single else [VMEM] * len(out_shape),
            scratch_shapes=scratch,
            compiler_params=params,
            cost_estimate=pl.CostEstimate(flops=cost, bytes_accessed=0, transcendentals=0),
        )

    flipped, own = call(
        early_kernel,
        [shape((rows, count * size, size), BF16), shape(features.shape, BF16)],
        [VMEM] * 2,
    )(vals, features)

    def join(*values):
        nodes_in = sum(v.shape[0] for v in values)
        return call(join_kernel, shape((nodes_in, width), BF16), [VMEM] * len(values))(*values)

    across = [swap(features, "dom", 2 * chip) for chip in range(1, chips)]
    front = join(own, across[-1])
    middle = join(*across[chips // 2 - 1 : -1], front)
    mine = call(last_join_kernel, shape((chips * nodes, width), BF16), [VMEM] * (chips // 2))(
        *across[: chips // 2 - 1], middle
    )
    far = swap(mine, "dom", 1)
    place = call(
        functools.partial(place_kernel, own_blocks, dom),
        shape((rows * count, 128), jnp.int32),
        [VMEM] * 2,
    )(cols.T, mine)

    partials = call(
        functools.partial(aggregate_kernel, rep),
        [shape((part, width), BF16 if j % 2 else F32) for j in range(rep)],
        [VMEM] * 4,
    )(place, vals, mine, far)
    def add(a, b, dtype, cost=0):
        return call(add_kernel, shape((part, width), dtype), [VMEM] * 2, cost=cost)(a, b)

    passing = swap(partials[3], "rep", 1)
    beside = swap(partials[1], "rep", 1)
    crossing = swap(add(partials[2], passing, BF16), "rep", 2)
    own_rows = add(add(partials[0], beside, F32), crossing, BF16)
    pieces = {0: own_rows, 2: swap(own_rows, "rep", 2), 1: swap(own_rows, "rep", 1)}
    pieces[3] = swap(pieces[2], "rep", 1)

    outputs, carried = [], []
    for j, piece in pieces.items():
        if j != 3:
            outs = [shape((quarter_blocks, size, width), F32), shape((2, width, width), F32)]
            scratch = []
        else:
            outs = [
                shape((nodes + width, width), BF16),
                shape(((chips - 1) * nodes, width), BF16),
                shape((chips, nodes, width), F32),
            ]
            scratch = [pltpu.VMEM((quarter_blocks, size, width), F32)]
        output, *carried = call(
            functools.partial(layer_kernel, rep, count, own_blocks, j),
            [shape((part, width), BF16)] + outs,
            [VMEM] * (6 + len(carried)),
            scratch,
        )(place, flipped, cotangent, weight, bias, piece, *carried)
        outputs.append(output)
    first, rest, keep = carried

    message = shape((nodes + width, width), BF16)
    got_first, got_rest = swap(first, "dom", 1), swap(rest, "dom", 1)
    sends = [call(first_pair_kernel, message, [VMEM] * 3, cost=5000000000)(keep, first, got_first)]
    own, *others = call(
        rest_pair_kernel, [shape((nodes, width), F32)] + [message] * (chips - 2), [VMEM] * 3, cost=1000000000
    )(keep, sends[0], got_rest)
    sends = others + sends
    got = {chip: swap(sends[chip - 1], "dom", 2 * chip) for chip in range(chips - 1, 0, -1)}
    output = call(
        functools.partial(order_kernel, list(pieces)), shape((rows * size, width), BF16), [VMEM] * rep
    )(*outputs)
    levels = chips.bit_length() - 1
    total = shape(message.shape, F32)
    got[chips - 1] = call(lift_kernel, total, [VMEM], cost=1000000000)(got[chips - 1])
    later = call(
        functools.partial(half_kernel, levels), [total] * (levels - 1), [VMEM] * (chips - 2), cost=0
    )(*[got[chip] for chip in range(2, chips)])
    feature_grad, weight_grad = call(
        final_kernel,
        [shape((nodes, width), F32), shape((width, width), F32)],
        [VMEM] * (levels + 2),
    )(own, sends[-1], got[1], *later)
    return output, feature_grad, weight_grad


def solution(mesh):
    placed = (
        P("dom", "rep"),
        P("dom", "rep", None, None),
        P(("rep", "dom"), None),
        P(),
        P(),
        P("dom", None),
    )
    return jax.shard_map(
        body,
        mesh=mesh,
        in_specs=placed,
        out_specs=(P("dom", None), P(("rep", "dom"), None), P()),
        check_vma=False,
    )
```

```python
import functools

import jax
import jax.numpy as jnp
from jax import lax
from jax.experimental import pallas as pl
from jax.experimental.pallas import tpu as pltpu
from jax.sharding import PartitionSpec as P

BF16 = jnp.bfloat16
F32 = jnp.float32
VMEM = pl.BlockSpec(memory_space=pltpu.VMEM)


def swap(value, axis, distance):
    size = lax.axis_size(axis)
    return lax.ppermute(value, axis, [(i, i ^ distance) for i in range(size)])


def matmul(a, b, contract):
    return lax.dot_general(a, b, ((contract[:1], contract[1:]), ((), ())), preferred_element_type=F32)


def early_kernel(vals_ref, features_ref, flipped_ref, own_ref):
    rows, count, size, _ = vals_ref.shape
    own_ref[...] = features_ref[...]
    for row in range(rows):
        for k in range(count):
            flipped_ref[row, k * size : (k + 1) * size] = vals_ref[row, k].T


def place_kernel(own_blocks, dom, cols_ref, _, place_ref):
    count, rows = cols_ref.shape
    for row in range(rows):
        for k in range(count):
            col = cols_ref[k, row] - lax.axis_index("rep") * (own_blocks * dom)
            owner = lax.div(col, jnp.int32(own_blocks)) ^ lax.axis_index("dom")
            place = ((owner & 1) * (dom // 2) + (owner >> 1)) * own_blocks
            place += lax.rem(col, jnp.int32(own_blocks))
            place_ref[row * count + k : row * count + k + 1, :] = jnp.full((1, 128), place, jnp.int32)


def join_kernel(*refs):
    pieces, out_ref = refs[:-1], refs[-1]
    first = 0
    for piece in pieces:
        out_ref[first : first + piece.shape[0]] = piece[...]
        first += piece.shape[0]


def last_join_kernel(*refs):
    near, middle, out_ref = refs[:-2], refs[-2], refs[-1]
    nodes = near[0].shape[0]
    body = middle.shape[0] - 2 * nodes
    out_ref[:nodes] = middle[body : body + nodes]
    first = nodes
    for piece in near:
        out_ref[first : first + nodes] = piece[...]
        first += nodes
    out_ref[first : first + body] = middle[:body]
    out_ref[first + body :] = middle[body + nodes :]


def aggregate_kernel(rep, place_ref, vals_ref, mine_ref, far_ref, *outs):
    rows, count, size, _ = vals_ref.shape
    half = mine_ref.shape[0] // size
    share = rows // rep
    for j in range(rep - 1, -1, -1):
        target = lax.axis_index("rep") ^ j
        for i in range(share):
            row = target * share + i
            total = None
            for k in range(count):
                place = place_ref[row * count + k, 0]
                beyond = place >= half
                index = jnp.where(beyond, place - half, place)
                here = pl.ds(pl.multiple_of(index * size, size), size)
                block = jnp.where(beyond, far_ref[here, :], mine_ref[here, :])
                term = matmul(vals_ref[row, k], block, (1, 0))
                total = term if total is None else total + term
            outs[j][i * size : (i + 1) * size] = total.astype(outs[j].dtype)


def layer_kernel(
    rep, count, own_blocks, j, place_ref, flipped_ref, cotangent_ref, weight_ref, bias_ref, *refs
):
    first, last = j == 0, j == 3
    piece_ref, refs = refs[0], refs[1:]
    if not first:
        (contrib_in, sums_in), refs = refs[:2], refs[2:]
    if last:
        output_ref, first_ref, rest_ref, keep_ref, contrib = refs
    else:
        output_ref, contrib, sums_out = refs[:3]
    if first:
        refs[3][...] = piece_ref[...]
    rows, _, size = flipped_ref.shape
    share = rows // rep
    quarter_blocks = contrib.shape[0]
    nodes = own_blocks * size
    contrib[...] = jnp.zeros_like(contrib) if first else contrib_in[...]

    target = lax.axis_index("rep") ^ j
    aggregated = piece_ref[...]
    part = aggregated.shape[0]
    here = pl.ds(pl.multiple_of(target * part, part), part)
    hidden = matmul(aggregated, weight_ref[...], (1, 0)) + bias_ref[...]
    gate_prob = jax.nn.sigmoid(hidden)
    output_ref[...] = (hidden * gate_prob).astype(BF16)
    grad_hidden = (
        cotangent_ref[here, :].astype(F32) * gate_prob * (1.0 + hidden * (1.0 - gate_prob))
    ).astype(BF16)
    part_sum = matmul(aggregated, grad_hidden, (0, 0))
    grad_agg = matmul(grad_hidden, weight_ref[...], (1, 1)).astype(BF16)
    for i in range(share):
        row = target * share + i
        terms = matmul(flipped_ref[row], grad_agg[i * size : (i + 1) * size], (1, 0))
        for k in range(count):
            contrib[place_ref[row * count + k, 0]] += terms[k * size : (k + 1) * size]
    if j == 0:
        sums_out[0] = part_sum
        sums_out[1] = jnp.zeros_like(part_sum)
    elif j == 2:
        sums_out[0] = sums_in[0]
        sums_out[1] = part_sum
    elif j == 1:
        sums_out[0] = sums_in[0] + part_sum
        sums_out[1] = sums_in[1]
    if not last:
        return
    half = quarter_blocks // 2
    keep_ref[...] = contrib[:half].reshape(keep_ref.shape)
    away = contrib[half:].reshape(half * size, -1).astype(BF16)
    rest_ref[...] = away[:-nodes]
    first_ref[:nodes] = away[-nodes:]
    first_ref[nodes:] = (sums_in[0] + (sums_in[1] + part_sum)).astype(BF16)


def combine_kernel(partial_ref, passing_ref, staying_ref, combined_ref, out_ref):
    combined_ref[...] = (partial_ref[...] + passing_ref[...].astype(F32)).astype(BF16)
    out_ref[...] = staying_ref[...]


def add_kernel(a_ref, b_ref, out_ref):
    out_ref[...] = (a_ref[...] + b_ref[...].astype(F32)).astype(out_ref.dtype)


def order_kernel(order, *refs):
    pieces, out_ref = refs[:-1], refs[-1]
    part = pieces[0].shape[0]
    for j, piece in zip(order, pieces):
        target = lax.axis_index("rep") ^ j
        out_ref[pl.ds(pl.multiple_of(target * part, part), part), :] = piece[...]


def first_pair_kernel(keep_ref, sent_ref, got_ref, out_ref):
    chips, nodes, _ = keep_ref.shape
    out_ref[:nodes] = (keep_ref[chips - 1] + got_ref[:nodes].astype(F32)).astype(BF16)
    out_ref[nodes:] = (sent_ref[nodes:].astype(F32) + got_ref[nodes:].astype(F32)).astype(BF16)


def rest_pair_kernel(keep_ref, first_ref, got_ref, own_ref, *outs):
    chips, nodes, _ = keep_ref.shape
    own_ref[...] = keep_ref[0] + got_ref[:nodes].astype(F32)
    for chip in range(1, chips - 1):
        total = keep_ref[chip] + got_ref[chip * nodes : (chip + 1) * nodes].astype(F32)
        outs[chip - 1][:nodes] = total.astype(BF16)
        outs[chip - 1][nodes:] = first_ref[nodes:]


def total_of(values):
    while len(values) > 1:
        values = [a + b for a, b in zip(values[::2], values[1::2])]
    return values[0]


def lift_kernel(got_ref, out_ref):
    out_ref[...] = got_ref[...].astype(F32)


def half_kernel(levels, *refs):
    for level in range(1, levels):
        first = 1 << level
        got = refs[first - 2 : 2 * first - 2]
        refs[level - levels][...] = total_of([g[...].astype(F32) for g in got])


def final_kernel(own_ref, sent_ref, got_ref, *refs):
    later, (feature_ref, weight_ref) = refs[:-2], refs[-2:]
    nodes = own_ref.shape[0]
    feature = own_ref[...] + got_ref[:nodes].astype(F32)
    weight = sent_ref[nodes:].astype(F32) + got_ref[nodes:].astype(F32)
    for value in later:
        feature += value[:nodes]
        weight += value[nodes:]
    feature_ref[...] = feature
    weight_ref[...] = weight


def shape(dims, dtype):
    return jax.ShapeDtypeStruct(dims, dtype)


def body(cols, vals, features, weight, bias, cotangent):
    rows, count, size, _ = vals.shape
    nodes, width = features.shape
    dom, rep = lax.axis_size("dom"), lax.axis_size("rep")
    chips = dom // 2
    own_blocks = nodes // size
    quarter_blocks = own_blocks * dom
    part = rows * size // rep
    params = pltpu.CompilerParams(vmem_limit_bytes=(8 + dom // 2) * 1024 * 1024)

    def call(kernel, out_shape, in_specs, scratch=(), cost=0):
        single = not isinstance(out_shape, list)
        return pl.pallas_call(
            kernel,
            out_shape=out_shape,
            in_specs=in_specs,
            out_specs=VMEM if single else [VMEM] * len(out_shape),
            scratch_shapes=scratch,
            compiler_params=params,
            cost_estimate=pl.CostEstimate(flops=cost, bytes_accessed=0, transcendentals=0),
        )

    flipped, own = call(
        early_kernel,
        [shape((rows, count * size, size), BF16), shape(features.shape, BF16)],
        [VMEM] * 2,
    )(vals, features)

    def join(*values):
        nodes_in = sum(v.shape[0] for v in values)
        return call(join_kernel, shape((nodes_in, width), BF16), [VMEM] * len(values))(*values)

    across = [swap(features, "dom", 2 * chip) for chip in range(1, chips)]
    front = join(own, across[-1])
    middle = join(*across[chips // 2 - 1 : -1], front)
    mine = call(last_join_kernel, shape((chips * nodes, width), BF16), [VMEM] * (chips // 2))(
        *across[: chips // 2 - 1], middle
    )
    far = swap(mine, "dom", 1)
    place = call(
        functools.partial(place_kernel, own_blocks, dom),
        shape((rows * count, 128), jnp.int32),
        [VMEM] * 2,
    )(cols.T, mine)

    partials = call(
        functools.partial(aggregate_kernel, rep),
        [shape((part, width), BF16 if j % 2 else F32) for j in range(rep)],
        [VMEM] * 4,
    )(place, vals, mine, far)
    def add(a, b, dtype):
        return call(add_kernel, shape((part, width), dtype), [VMEM] * 2, cost=10**9)(a, b)

    passing = swap(partials[3], "rep", 1)
    combined, staying = call(
        combine_kernel, [shape((part, width), BF16)] * 2, [VMEM] * 3
    )(partials[2], passing, partials[1])
    crossing = swap(combined, "rep", 2)
    beside = swap(staying, "rep", 1)
    own_rows = add(add(partials[0], crossing, F32), beside, BF16)
    pieces = {0: own_rows, 2: swap(own_rows, "rep", 2)}
    pieces[1] = None
    pieces[3] = swap(pieces[2], "rep", 1)

    outputs, carried = [], []
    for j in pieces:
        if j != 3:
            outs = [shape((quarter_blocks, size, width), F32), shape((2, width, width), F32)]
            scratch = []
            if j == 0:
                outs += [shape((part, width), BF16)]
        else:
            outs = [
                shape((nodes + width, width), BF16),
                shape(((chips - 1) * nodes, width), BF16),
                shape((chips, nodes, width), F32),
            ]
            scratch = [pltpu.VMEM((quarter_blocks, size, width), F32)]
        output, *carried = call(
            functools.partial(layer_kernel, rep, count, own_blocks, j),
            [shape((part, width), BF16)] + outs,
            [VMEM] * (6 + len(carried)),
            scratch,
        )(place, flipped, cotangent, weight, bias, pieces[j], *carried)
        outputs.append(output)
        if j == 0:
            pieces[1] = swap(carried.pop(), "rep", 1)
    first, rest, keep = carried

    message = shape((nodes + width, width), BF16)
    got_first, got_rest = swap(first, "dom", 1), swap(rest, "dom", 1)
    sends = [call(first_pair_kernel, message, [VMEM] * 3, cost=5000000000)(keep, first, got_first)]
    own, *others = call(
        rest_pair_kernel, [shape((nodes, width), F32)] + [message] * (chips - 2), [VMEM] * 3, cost=1000000000
    )(keep, sends[0], got_rest)
    sends = others + sends
    got = {chip: swap(sends[chip - 1], "dom", 2 * chip) for chip in range(chips - 1, 0, -1)}
    output = call(
        functools.partial(order_kernel, list(pieces)), shape((rows * size, width), BF16), [VMEM] * rep
    )(*outputs)
    levels = chips.bit_length() - 1
    total = shape(message.shape, F32)
    got[chips - 1] = call(lift_kernel, total, [VMEM], cost=1000000000)(got[chips - 1])
    later = call(
        functools.partial(half_kernel, levels), [total] * (levels - 1), [VMEM] * (chips - 2), cost=0
    )(*[got[chip] for chip in range(2, chips)])
    feature_grad, weight_grad = call(
        final_kernel,
        [shape((nodes, width), F32), shape((width, width), F32)],
        [VMEM] * (levels + 2),
    )(own, sends[-1], got[1], *later)
    return output, feature_grad, weight_grad


def solution(mesh):
    placed = (
        P("dom", "rep"),
        P("dom", "rep", None, None),
        P(("rep", "dom"), None),
        P(),
        P(),
        P("dom", None),
    )
    return jax.shard_map(
        body,
        mesh=mesh,
        in_specs=placed,
        out_specs=(P("dom", None), P(("rep", "dom"), None), P()),
        check_vma=False,
    )
```

```python
import functools

import jax
import jax.numpy as jnp
from jax import lax
from jax.experimental import pallas as pl
from jax.experimental.pallas import tpu as pltpu
from jax.sharding import PartitionSpec as P

BF16 = jnp.bfloat16
F32 = jnp.float32
VMEM = pl.BlockSpec(memory_space=pltpu.VMEM)


def swap(value, axis, distance):
    size = lax.axis_size(axis)
    return lax.ppermute(value, axis, [(i, i ^ distance) for i in range(size)])


def matmul(a, b, contract):
    return lax.dot_general(a, b, ((contract[:1], contract[1:]), ((), ())), preferred_element_type=F32)


def early_kernel(vals_ref, features_ref, flipped_ref, own_ref):
    rows, count, size, _ = vals_ref.shape
    own_ref[...] = features_ref[...]
    for row in range(rows):
        for k in range(count):
            flipped_ref[row, k * size : (k + 1) * size] = vals_ref[row, k].T


def place_kernel(own_blocks, dom, cols_ref, _, place_ref):
    count, rows = cols_ref.shape
    for row in range(rows):
        for k in range(count):
            col = cols_ref[k, row] - lax.axis_index("rep") * (own_blocks * dom)
            owner = lax.div(col, jnp.int32(own_blocks)) ^ lax.axis_index("dom")
            place = ((owner & 1) * (dom // 2) + (owner >> 1)) * own_blocks
            place += lax.rem(col, jnp.int32(own_blocks))
            place_ref[row * count + k : row * count + k + 1, :] = jnp.full((1, 128), place, jnp.int32)


def join_kernel(*refs):
    pieces, out_ref = refs[:-1], refs[-1]
    first = 0
    for piece in pieces:
        out_ref[first : first + piece.shape[0]] = piece[...]
        first += piece.shape[0]


def last_join_kernel(*refs):
    near, middle, out_ref = refs[:-2], refs[-2], refs[-1]
    nodes = near[0].shape[0]
    body = middle.shape[0] - 2 * nodes
    out_ref[:nodes] = middle[body : body + nodes]
    first = nodes
    for piece in near:
        out_ref[first : first + nodes] = piece[...]
        first += nodes
    out_ref[first : first + body] = middle[:body]
    out_ref[first + body :] = middle[body + nodes :]


def aggregate_kernel(rep, place_ref, vals_ref, mine_ref, far_ref, *outs):
    rows, count, size, _ = vals_ref.shape
    half = mine_ref.shape[0] // size
    share = rows // rep
    for j in range(rep - 1, -1, -1):
        target = lax.axis_index("rep") ^ j
        for i in range(share):
            row = target * share + i
            total = None
            for k in range(count):
                place = place_ref[row * count + k, 0]
                beyond = place >= half
                index = jnp.where(beyond, place - half, place)
                here = pl.ds(pl.multiple_of(index * size, size), size)
                block = jnp.where(beyond, far_ref[here, :], mine_ref[here, :])
                term = matmul(vals_ref[row, k], block, (1, 0))
                total = term if total is None else total + term
            outs[j][i * size : (i + 1) * size] = total.astype(outs[j].dtype)


def layer_kernel(
    rep, place_ref, flipped_ref, cotangent_ref, weight_ref, bias_ref, aggregated_ref,
    output_ref, first_ref, rest_ref, keep_ref, contrib,
):
    rows, length, size = flipped_ref.shape
    count = length // size
    chips, nodes, _ = keep_ref.shape
    part = rows * size // rep
    contrib[...] = jnp.zeros_like(contrib)
    weight_part = None
    for piece in range(rep):
        here = slice(piece * part, (piece + 1) * part)
        aggregated = aggregated_ref[here, :]
        hidden = matmul(aggregated, weight_ref[...], (1, 0)) + bias_ref[...]
        gate_prob = jax.nn.sigmoid(hidden)
        output_ref[here, :] = (hidden * gate_prob).astype(BF16)
        grad_hidden = (
            cotangent_ref[here, :].astype(F32) * gate_prob * (1.0 + hidden * (1.0 - gate_prob))
        ).astype(BF16)
        part_sum = matmul(aggregated, grad_hidden, (0, 0))
        weight_part = part_sum if piece == 0 else weight_part + part_sum
        grad_agg = matmul(grad_hidden, weight_ref[...], (1, 1)).astype(BF16)
        for i in range(part // size):
            row = piece * (part // size) + i
            terms = matmul(flipped_ref[row], grad_agg[i * size : (i + 1) * size], (1, 0))
            for k in range(count):
                contrib[place_ref[row * count + k, 0]] += terms[k * size : (k + 1) * size]
    half = contrib.shape[0] // 2
    keep_ref[...] = contrib[:half].reshape(keep_ref.shape)
    away = contrib[half:].reshape(half * size, -1).astype(BF16)
    rest_ref[...] = away[:-nodes]
    first_ref[:nodes] = away[-nodes:]
    first_ref[nodes:] = weight_part.astype(BF16)


def add_kernel(a_ref, b_ref, out_ref):
    out_ref[...] = (a_ref[...] + b_ref[...].astype(F32)).astype(out_ref.dtype)


def copy_kernel(value_ref, out_ref):
    out_ref[...] = value_ref[...]


def first_pair_kernel(keep_ref, sent_ref, got_ref, out_ref):
    chips, nodes, _ = keep_ref.shape
    out_ref[:nodes] = (keep_ref[chips - 1] + got_ref[:nodes].astype(F32)).astype(BF16)
    out_ref[nodes:] = (sent_ref[nodes:].astype(F32) + got_ref[nodes:].astype(F32)).astype(BF16)


def rest_pair_kernel(keep_ref, first_ref, got_ref, own_ref, *outs):
    chips, nodes, _ = keep_ref.shape
    own_ref[...] = keep_ref[0] + got_ref[:nodes].astype(F32)
    for chip in range(1, chips - 1):
        total = keep_ref[chip] + got_ref[chip * nodes : (chip + 1) * nodes].astype(F32)
        outs[chip - 1][:nodes] = total.astype(BF16)
        outs[chip - 1][nodes:] = first_ref[nodes:]


def total_of(values):
    while len(values) > 1:
        values = [a + b for a, b in zip(values[::2], values[1::2])]
    return values[0]


def lift_kernel(got_ref, out_ref):
    out_ref[...] = got_ref[...].astype(F32)


def half_kernel(levels, *refs):
    for level in range(1, levels):
        first = 1 << level
        got = refs[first - 2 : 2 * first - 2]
        refs[level - levels][...] = total_of([g[...].astype(F32) for g in got])


def final_kernel(own_ref, sent_ref, got_ref, *refs):
    later, (feature_ref, weight_ref) = refs[:-2], refs[-2:]
    nodes = own_ref.shape[0]
    feature = own_ref[...] + got_ref[:nodes].astype(F32)
    weight = sent_ref[nodes:].astype(F32) + got_ref[nodes:].astype(F32)
    for value in later:
        feature += value[:nodes]
        weight += value[nodes:]
    feature_ref[...] = feature
    weight_ref[...] = weight


def shape(dims, dtype):
    return jax.ShapeDtypeStruct(dims, dtype)


def body(cols, vals, features, weight, bias, cotangent):
    rows, count, size, _ = vals.shape
    nodes, width = features.shape
    dom, rep = lax.axis_size("dom"), lax.axis_size("rep")
    chips = dom // 2
    own_blocks = nodes // size
    quarter_blocks = own_blocks * dom
    part = rows * size // rep
    params = pltpu.CompilerParams(vmem_limit_bytes=(8 + dom // 2) * 1024 * 1024)

    def call(kernel, out_shape, in_specs, scratch=(), cost=0):
        single = not isinstance(out_shape, list)
        return pl.pallas_call(
            kernel,
            out_shape=out_shape,
            in_specs=in_specs,
            out_specs=VMEM if single else [VMEM] * len(out_shape),
            scratch_shapes=scratch,
            compiler_params=params,
            cost_estimate=pl.CostEstimate(flops=cost, bytes_accessed=0, transcendentals=0),
        )

    flipped, own = call(
        early_kernel,
        [shape((rows, count * size, size), BF16), shape(features.shape, BF16)],
        [VMEM] * 2,
    )(vals, features)

    def join(*values):
        nodes_in = sum(v.shape[0] for v in values)
        return call(join_kernel, shape((nodes_in, width), BF16), [VMEM] * len(values))(*values)

    across = [swap(features, "dom", 2 * chip) for chip in range(1, chips)]
    front = join(own, across[-1])
    middle = join(*across[chips // 2 - 1 : -1], front)
    mine = call(last_join_kernel, shape((chips * nodes, width), BF16), [VMEM] * (chips // 2))(
        *across[: chips // 2 - 1], middle
    )
    far = swap(mine, "dom", 1)
    place = call(
        functools.partial(place_kernel, own_blocks, dom),
        shape((rows * count, 128), jnp.int32),
        [VMEM] * 2,
    )(cols.T, mine)

    partials = call(
        functools.partial(aggregate_kernel, rep),
        [shape((part, width), BF16 if j else F32) for j in range(rep)],
        [VMEM] * 4,
    )(place, vals, mine, far)
    arrived = {j: swap(partials[j], "rep", j) if j else partials[j] for j in range(rep)}
    order = range(rep - 1, 0, -1)
    own_rows = arrived[0]
    for j in order:
        own_rows = call(add_kernel, shape((part, width), F32 if j > 1 else BF16), [VMEM] * 2)(
            own_rows, arrived[j]
        )
    aggregated = lax.all_gather(own_rows, "rep", axis=0, tiled=True)

    output, first, rest, keep = call(
        functools.partial(layer_kernel, rep),
        [
            shape((rows * size, width), BF16),
            shape((nodes + width, width), BF16),
            shape(((chips - 1) * nodes, width), BF16),
            shape((chips, nodes, width), F32),
        ],
        [VMEM] * 6,
        [pltpu.VMEM((quarter_blocks, size, width), F32)],
    )(place, flipped, cotangent, weight, bias.reshape(1, width), aggregated)

    message = shape((nodes + width, width), BF16)
    got_first, got_rest = swap(first, "dom", 1), swap(rest, "dom", 1)
    sends = [call(first_pair_kernel, message, [VMEM] * 3, cost=5000000000)(keep, first, got_first)]
    own, *others = call(
        rest_pair_kernel, [shape((nodes, width), F32)] + [message] * (chips - 2), [VMEM] * 3, cost=1000000000
    )(keep, sends[0], got_rest)
    sends = others + sends
    got = {chip: swap(sends[chip - 1], "dom", 2 * chip) for chip in range(chips - 1, 0, -1)}
    output = call(copy_kernel, shape(output.shape, BF16), [VMEM])(output)
    levels = chips.bit_length() - 1
    total = shape(message.shape, F32)
    got[chips - 1] = call(lift_kernel, total, [VMEM], cost=1000000000)(got[chips - 1])
    later = call(
        functools.partial(half_kernel, levels), [total] * (levels - 1), [VMEM] * (chips - 2), cost=0
    )(*[got[chip] for chip in range(2, chips)])
    feature_grad, weight_grad = call(
        final_kernel,
        [shape((nodes, width), F32), shape((width, width), F32)],
        [VMEM] * (levels + 2),
    )(own, sends[-1], got[1], *later)
    return output, feature_grad, weight_grad


def solution(mesh):
    placed = (
        P("dom", "rep"),
        P("dom", "rep", None, None),
        P(("rep", "dom"), None),
        P(),
        P(),
        P("dom", None),
    )
    return jax.shard_map(
        body,
        mesh=mesh,
        in_specs=placed,
        out_specs=(P("dom", None), P(("rep", "dom"), None), P()),
        check_vma=False,
    )
```

```python
import functools

import jax
import jax.numpy as jnp
from jax import lax
from jax.experimental import pallas as pl
from jax.experimental.pallas import tpu as pltpu
from jax.sharding import PartitionSpec as P

BF16 = jnp.bfloat16
F32 = jnp.float32
VMEM = pl.BlockSpec(memory_space=pltpu.VMEM)


def swap(value, axis, distance):
    size = lax.axis_size(axis)
    return lax.ppermute(value, axis, [(i, i ^ distance) for i in range(size)])


def matmul(a, b, contract):
    return lax.dot_general(a, b, ((contract[:1], contract[1:]), ((), ())), preferred_element_type=F32)


def early_kernel(vals_ref, features_ref, flipped_ref, own_ref):
    rows, count, size, _ = vals_ref.shape
    own_ref[...] = features_ref[...]
    for row in range(rows):
        for k in range(count):
            flipped_ref[row, k * size : (k + 1) * size] = vals_ref[row, k].T


def place_kernel(own_blocks, dom, cols_ref, _, place_ref):
    count, rows = cols_ref.shape
    for row in range(rows):
        for k in range(count):
            col = cols_ref[k, row] - lax.axis_index("rep") * (own_blocks * dom)
            owner = lax.div(col, jnp.int32(own_blocks)) ^ lax.axis_index("dom")
            place = ((owner & 1) * (dom // 2) + (owner >> 1)) * own_blocks
            place += lax.rem(col, jnp.int32(own_blocks))
            place_ref[row * count + k : row * count + k + 1, :] = jnp.full((1, 128), place, jnp.int32)


def join_kernel(*refs):
    pieces, out_ref = refs[:-1], refs[-1]
    first = 0
    for piece in pieces:
        out_ref[first : first + piece.shape[0]] = piece[...]
        first += piece.shape[0]


def last_join_kernel(*refs):
    near, middle, out_ref = refs[:-2], refs[-2], refs[-1]
    nodes = near[0].shape[0]
    body = middle.shape[0] - 2 * nodes
    out_ref[:nodes] = middle[body : body + nodes]
    first = nodes
    for piece in near:
        out_ref[first : first + nodes] = piece[...]
        first += nodes
    out_ref[first : first + body] = middle[:body]
    out_ref[first + body :] = middle[body + nodes :]


def aggregate_kernel(rep, place_ref, vals_ref, mine_ref, far_ref, *outs):
    rows, count, size, _ = vals_ref.shape
    half = mine_ref.shape[0] // size
    share = rows // rep
    for j in range(rep - 1, -1, -1):
        target = lax.axis_index("rep") ^ j
        for i in range(share):
            row = target * share + i
            total = None
            for k in range(count):
                place = place_ref[row * count + k, 0]
                beyond = place >= half
                index = jnp.where(beyond, place - half, place)
                here = pl.ds(pl.multiple_of(index * size, size), size)
                block = jnp.where(beyond, far_ref[here, :], mine_ref[here, :])
                term = matmul(vals_ref[row, k], block, (1, 0))
                total = term if total is None else total + term
            outs[j][i * size : (i + 1) * size] = total.astype(outs[j].dtype)


def layer_kernel(
    rep, count, own_blocks, j, place_ref, flipped_ref, cotangent_ref, weight_ref, bias_ref, *refs
):
    first, last = j == 0, j == 1
    piece_ref, refs = refs[0], refs[1:]
    if not first:
        (_, sums_in), refs = refs[:2], refs[2:]
    output_ref, contrib, *refs = refs
    rows, _, size = flipped_ref.shape
    share = rows // rep
    quarter_blocks = contrib.shape[0]
    nodes = own_blocks * size
    if first:
        contrib[...] = jnp.zeros_like(contrib)

    target = lax.axis_index("rep") ^ j
    aggregated = piece_ref[...]
    part = aggregated.shape[0]
    here = pl.ds(pl.multiple_of(target * part, part), part)
    hidden = matmul(aggregated, weight_ref[...], (1, 0)) + bias_ref[...]
    gate_prob = jax.nn.sigmoid(hidden)
    output_ref[...] = (hidden * gate_prob).astype(BF16)
    grad_hidden = (
        cotangent_ref[here, :].astype(F32) * gate_prob * (1.0 + hidden * (1.0 - gate_prob))
    ).astype(BF16)
    part_sum = matmul(aggregated, grad_hidden, (0, 0))
    grad_agg = matmul(grad_hidden, weight_ref[...], (1, 1)).astype(BF16)
    for i in range(share):
        row = target * share + i
        terms = matmul(flipped_ref[row], grad_agg[i * size : (i + 1) * size], (1, 0))
        for k in range(count):
            contrib[place_ref[row * count + k, 0]] += terms[k * size : (k + 1) * size]
    if first:
        refs[0][0] = part_sum
        refs[0][1] = jnp.zeros_like(part_sum)
    elif not last:
        refs[0][0] = sums_in[0]
        refs[0][1] = sums_in[1] + part_sum
    else:
        first_ref, rest_ref = refs
        away = contrib[quarter_blocks // 2 :].reshape(quarter_blocks // 2 * size, -1).astype(BF16)
        rest_ref[...] = away[:-nodes]
        first_ref[:nodes] = away[-nodes:]
        first_ref[nodes:] = ((sums_in[0] + part_sum) + sums_in[1]).astype(BF16)


def add_kernel(a_ref, b_ref, out_ref):
    out_ref[...] = (a_ref[...] + b_ref[...].astype(F32)).astype(out_ref.dtype)


def order_kernel(order, *refs):
    pieces, out_ref = refs[:-1], refs[-1]
    part = pieces[0].shape[0]
    for j, piece in zip(order, pieces):
        target = lax.axis_index("rep") ^ j
        out_ref[pl.ds(pl.multiple_of(target * part, part), part), :] = piece[...]


def first_pair_kernel(contrib_ref, sent_ref, got_ref, out_ref):
    blocks, size, _ = contrib_ref.shape
    nodes = out_ref.shape[0] - sent_ref.shape[1]
    last = contrib_ref[blocks // 2 - nodes // size : blocks // 2].reshape(nodes, -1)
    out_ref[:nodes] = (last + got_ref[:nodes].astype(F32)).astype(BF16)
    out_ref[nodes:] = (sent_ref[nodes:].astype(F32) + got_ref[nodes:].astype(F32)).astype(BF16)


def rest_pair_kernel(contrib_ref, first_ref, got_ref, own_ref, *outs):
    size, nodes = contrib_ref.shape[1], own_ref.shape[0]
    for chip in range(len(outs) + 1):
        mine = contrib_ref[chip * nodes // size : (chip + 1) * nodes // size].reshape(nodes, -1)
        total = mine + got_ref[chip * nodes : (chip + 1) * nodes].astype(F32)
        if chip == 0:
            own_ref[...] = total
        else:
            outs[chip - 1][:nodes] = total.astype(BF16)
            outs[chip - 1][nodes:] = first_ref[nodes:]


def total_of(values):
    while len(values) > 1:
        values = [a + b for a, b in zip(values[::2], values[1::2])]
    return values[0]


def lift_kernel(got_ref, out_ref):
    out_ref[...] = got_ref[...].astype(F32)


def half_kernel(levels, *refs):
    for level in range(1, levels):
        first = 1 << level
        got = refs[first - 2 : 2 * first - 2]
        refs[level - levels][...] = total_of([g[...].astype(F32) for g in got])


def final_kernel(own_ref, sent_ref, got_ref, *refs):
    later, (feature_ref, weight_ref) = refs[:-2], refs[-2:]
    nodes = own_ref.shape[0]
    feature = own_ref[...] + got_ref[:nodes].astype(F32)
    weight = sent_ref[nodes:].astype(F32) + got_ref[nodes:].astype(F32)
    for value in later:
        feature += value[:nodes]
        weight += value[nodes:]
    feature_ref[...] = feature
    weight_ref[...] = weight


def shape(dims, dtype):
    return jax.ShapeDtypeStruct(dims, dtype)


def body(cols, vals, features, weight, bias, cotangent):
    rows, count, size, _ = vals.shape
    nodes, width = features.shape
    dom, rep = lax.axis_size("dom"), lax.axis_size("rep")
    chips = dom // 2
    own_blocks = nodes // size
    quarter_blocks = own_blocks * dom
    part = rows * size // rep
    params = pltpu.CompilerParams(vmem_limit_bytes=(8 + dom // 2) * 1024 * 1024)

    def call(kernel, out_shape, in_specs, aliases={}, cost=0):
        single = not isinstance(out_shape, list)
        return pl.pallas_call(
            kernel,
            out_shape=out_shape,
            in_specs=in_specs,
            out_specs=VMEM if single else [VMEM] * len(out_shape),
            input_output_aliases=aliases,
            compiler_params=params,
            cost_estimate=pl.CostEstimate(flops=cost, bytes_accessed=0, transcendentals=0),
        )

    flipped, own = call(
        early_kernel,
        [shape((rows, count * size, size), BF16), shape(features.shape, BF16)],
        [VMEM] * 2,
    )(vals, features)

    def join(*values):
        nodes_in = sum(v.shape[0] for v in values)
        return call(join_kernel, shape((nodes_in, width), BF16), [VMEM] * len(values))(*values)

    across = [swap(features, "dom", 2 * chip) for chip in range(1, chips)]
    front = join(own, across[-1])
    middle = join(*across[chips // 2 - 1 : -1], front)
    mine = call(last_join_kernel, shape((chips * nodes, width), BF16), [VMEM] * (chips // 2))(
        *across[: chips // 2 - 1], middle
    )
    far = swap(mine, "dom", 1)
    place = call(
        functools.partial(place_kernel, own_blocks, dom),
        shape((rows * count, 128), jnp.int32),
        [VMEM] * 2,
    )(cols.T, mine)

    partials = call(
        functools.partial(aggregate_kernel, rep),
        [shape((part, width), BF16 if j else F32) for j in range(rep)],
        [VMEM] * 4,
    )(place, vals, mine, far)
    arrived = {j: swap(partials[j], "rep", j) if j else partials[j] for j in range(rep)}
    order = [*range(2, rep), 1]
    own_rows = arrived[0]
    for j in order:
        own_rows = call(add_kernel, shape((part, width), F32 if j > 1 else BF16), [VMEM] * 2)(
            own_rows, arrived[j]
        )
    pieces = {0: own_rows}
    for j in order:
        pieces[j] = swap(own_rows, "rep", j)

    outputs, carried = [], []
    for j, piece in pieces.items():
        outs = [shape((part, width), BF16), shape((quarter_blocks, size, width), F32)]
        if j != 1:
            outs += [shape((2, width, width), F32)]
        else:
            outs += [
                shape((nodes + width, width), BF16),
                shape(((chips - 1) * nodes, width), BF16),
            ]
        output, *carried = call(
            functools.partial(layer_kernel, rep, count, own_blocks, j),
            outs,
            [VMEM] * (6 + len(carried)),
            aliases={6: 1} if carried else {},
        )(place, flipped, cotangent, weight, bias.reshape(1, width), piece, *carried)
        outputs.append(output)
    contrib, first, rest = carried

    message = shape((nodes + width, width), BF16)
    got_first, got_rest = swap(first, "dom", 1), swap(rest, "dom", 1)
    sends = [call(first_pair_kernel, message, [VMEM] * 3, cost=5000000000)(contrib, first, got_first)]
    own, *others = call(
        rest_pair_kernel, [shape((nodes, width), F32)] + [message] * (chips - 2), [VMEM] * 3, cost=1000000000
    )(contrib, sends[0], got_rest)
    sends = others + sends
    got = {chip: swap(sends[chip - 1], "dom", 2 * chip) for chip in range(chips - 1, 0, -1)}
    output = call(
        functools.partial(order_kernel, list(pieces)), shape((rows * size, width), BF16), [VMEM] * rep
    )(*outputs)
    levels = chips.bit_length() - 1
    total = shape(message.shape, F32)
    got[chips - 1] = call(lift_kernel, total, [VMEM], cost=1000000000)(got[chips - 1])
    later = call(
        functools.partial(half_kernel, levels), [total] * (levels - 1), [VMEM] * (chips - 2), cost=0
    )(*[got[chip] for chip in range(2, chips)])
    feature_grad, weight_grad = call(
        final_kernel,
        [shape((nodes, width), F32), shape((width, width), F32)],
        [VMEM] * (levels + 2),
    )(own, sends[-1], got[1], *later)
    return output, feature_grad, weight_grad


def solution(mesh):
    placed = (
        P("dom", "rep"),
        P("dom", "rep", None, None),
        P(("rep", "dom"), None),
        P(),
        P(),
        P("dom", None),
    )
    return jax.shard_map(
        body,
        mesh=mesh,
        in_specs=placed,
        out_specs=(P("dom", None), P(("rep", "dom"), None), P()),
        check_vma=False,
    )
```

```python
import functools

import jax
import jax.numpy as jnp
from jax import lax
from jax.experimental import pallas as pl
from jax.experimental.pallas import tpu as pltpu
from jax.sharding import PartitionSpec as P

BF16 = jnp.bfloat16
F32 = jnp.float32
VMEM = pl.BlockSpec(memory_space=pltpu.VMEM)


def swap(value, axis, distance):
    size = lax.axis_size(axis)
    return lax.ppermute(value, axis, [(i, i ^ distance) for i in range(size)])


def cross(value, turn, chips):
    def partner(i):
        chip = turn ^ (chips - 1) if i % 2 and turn != chips - 1 else turn
        return i ^ (2 * chip)

    return lax.ppermute(value, "dom", [(i, partner(i)) for i in range(2 * chips)])


def matmul(a, b, contract):
    return lax.dot_general(a, b, ((contract[:1], contract[1:]), ((), ())), preferred_element_type=F32)


def early_kernel(vals_ref, features_ref, flipped_ref, own_ref):
    rows, count, size, _ = vals_ref.shape
    own_ref[...] = features_ref[...]
    for row in range(rows):
        for k in range(count):
            flipped_ref[row, k * size : (k + 1) * size] = vals_ref[row, k].T


def place_kernel(own_blocks, chips, cols_ref, _, place_ref):
    count, rows = cols_ref.shape
    half = chips // 2 - 1
    me = lax.axis_index("dom")
    for row in range(rows):
        for k in range(count):
            col = cols_ref[k, row] - lax.axis_index("rep") * (own_blocks * 2 * chips)
            apart = lax.div(col, jnp.int32(own_blocks)) ^ me
            side, chip = apart & 1, apart >> 1
            inner = jnp.logical_and(chip > 0, chip < chips - 1)
            odd = ((me & 1) ^ side) == 1
            turn = jnp.where(jnp.logical_and(inner, odd), chip ^ (chips - 1), chip)
            turn = jnp.where(turn > half, turn + 1, turn)
            turn = jnp.where(chip == chips - 1, half + 1, turn)
            place = (side * chips + turn) * own_blocks + lax.rem(col, jnp.int32(own_blocks))
            place_ref[row * count + k : row * count + k + 1, :] = jnp.full((1, 128), place, jnp.int32)


def join_kernel(*refs):
    pieces, out_ref = refs[:-1], refs[-1]
    first = 0
    for piece in pieces:
        out_ref[first : first + piece.shape[0]] = piece[...]
        first += piece.shape[0]


def aggregate_kernel(rep, place_ref, vals_ref, mine_ref, far_ref, *outs):
    rows, count, size, _ = vals_ref.shape
    half = mine_ref.shape[0] // size
    share = rows // rep
    for j in range(rep - 1, -1, -1):
        target = lax.axis_index("rep") ^ j
        for i in range(share):
            row = target * share + i
            total = None
            for k in range(count):
                place = place_ref[row * count + k, 0]
                beyond = place >= half
                index = jnp.where(beyond, place - half, place)
                here = pl.ds(pl.multiple_of(index * size, size), size)
                block = jnp.where(beyond, far_ref[here, :], mine_ref[here, :])
                term = matmul(vals_ref[row, k], block, (1, 0))
                total = term if total is None else total + term
            outs[j][i * size : (i + 1) * size] = total.astype(outs[j].dtype)


def layer_kernel(
    rep, count, own_blocks, j, place_ref, flipped_ref, cotangent_ref, weight_ref, bias_ref, *refs
):
    first, last = j == 0, j == 1
    piece_ref, refs = refs[0], refs[1:]
    if not first:
        (_, sums_in), refs = refs[:2], refs[2:]
    output_ref, contrib, *refs = refs
    rows, _, size = flipped_ref.shape
    share = rows // rep
    quarter_blocks = contrib.shape[0]
    nodes = own_blocks * size
    if first:
        contrib[...] = jnp.zeros_like(contrib)

    target = lax.axis_index("rep") ^ j
    aggregated = piece_ref[...]
    part = aggregated.shape[0]
    here = pl.ds(pl.multiple_of(target * part, part), part)
    hidden = matmul(aggregated, weight_ref[...], (1, 0)) + bias_ref[...]
    gate_prob = jax.nn.sigmoid(hidden)
    output_ref[...] = (hidden * gate_prob).astype(BF16)
    grad_hidden = (
        cotangent_ref[here, :].astype(F32) * gate_prob * (1.0 + hidden * (1.0 - gate_prob))
    ).astype(BF16)
    part_sum = matmul(aggregated, grad_hidden, (0, 0))
    grad_agg = matmul(grad_hidden, weight_ref[...], (1, 1)).astype(BF16)
    for i in range(share):
        row = target * share + i
        terms = matmul(flipped_ref[row], grad_agg[i * size : (i + 1) * size], (1, 0))
        for k in range(count):
            contrib[place_ref[row * count + k, 0]] += terms[k * size : (k + 1) * size]
    if first:
        refs[0][0] = part_sum
        refs[0][1] = jnp.zeros_like(part_sum)
    elif not last:
        refs[0][0] = sums_in[0]
        refs[0][1] = sums_in[1] + part_sum
    else:
        first_ref, rest_ref = refs
        away = contrib[quarter_blocks // 2 :].reshape(quarter_blocks // 2 * size, -1).astype(BF16)
        rest_ref[:nodes] = away[:nodes]
        rest_ref[nodes:] = away[2 * nodes :]
        first_ref[:nodes] = away[nodes : 2 * nodes]
        first_ref[nodes:] = ((sums_in[0] + part_sum) + sums_in[1]).astype(BF16)


def add_kernel(a_ref, b_ref, out_ref):
    out_ref[...] = (a_ref[...] + b_ref[...].astype(F32)).astype(out_ref.dtype)


def order_kernel(order, *refs):
    pieces, out_ref = refs[:-1], refs[-1]
    part = pieces[0].shape[0]
    for j, piece in zip(order, pieces):
        target = lax.axis_index("rep") ^ j
        out_ref[pl.ds(pl.multiple_of(target * part, part), part), :] = piece[...]


def first_pair_kernel(contrib_ref, sent_ref, got_ref, out_ref):
    size = contrib_ref.shape[1]
    nodes = out_ref.shape[0] - sent_ref.shape[1]
    mine = contrib_ref[nodes // size : 2 * nodes // size].reshape(nodes, -1)
    out_ref[:nodes] = (mine + got_ref[:nodes].astype(F32)).astype(BF16)
    out_ref[nodes:] = (sent_ref[nodes:].astype(F32) + got_ref[nodes:].astype(F32)).astype(BF16)


def rest_pair_kernel(contrib_ref, first_ref, got_ref, own_ref, *outs):
    size, nodes = contrib_ref.shape[1], own_ref.shape[0]
    mine = contrib_ref[: nodes // size].reshape(nodes, -1)
    own_ref[...] = mine + got_ref[:nodes].astype(F32)
    for at, out_ref in enumerate(outs, 1):
        mine = contrib_ref[(at + 1) * nodes // size : (at + 2) * nodes // size].reshape(nodes, -1)
        total = mine + got_ref[at * nodes : (at + 1) * nodes].astype(F32)
        out_ref[:nodes] = total.astype(BF16)
        out_ref[nodes:] = first_ref[nodes:]


def total_of(values):
    while len(values) > 1:
        values = [a + b for a, b in zip(values[::2], values[1::2])]
    return values[0]


def lift_kernel(got_ref, out_ref):
    out_ref[...] = got_ref[...].astype(F32)


def early_sum_kernel(own_ref, sent_ref, lifted_ref, *refs):
    got, out_ref = refs[:-1], refs[-1]
    nodes = own_ref.shape[0]
    width = sent_ref.shape[1]
    total = own_ref[...] + lifted_ref[:nodes]
    for g in got:
        total += g[:nodes].astype(F32)
    out_ref[:nodes] = total
    weights = [sent_ref[nodes:].astype(F32) + got[-1][nodes:].astype(F32), lifted_ref[nodes:]]
    weights += [g[nodes:].astype(F32) for g in got[:-1]]
    for i, value in enumerate(weights):
        out_ref[nodes + i * width : nodes + (i + 1) * width] = value


def final_kernel(early_ref, *refs):
    got, (feature_ref, weight_ref) = refs[:-2], refs[-2:]
    nodes, width = feature_ref.shape
    total = early_ref[:nodes]
    weights = [early_ref[nodes : nodes + width]]
    for i, g in enumerate(got):
        total += g[:nodes].astype(F32)
        early = early_ref[nodes + (i + 1) * width : nodes + (i + 2) * width]
        weights.append(early + got[-1 - i][nodes:].astype(F32))
    feature_ref[...] = total
    weight_ref[...] = total_of(weights)


def shape(dims, dtype):
    return jax.ShapeDtypeStruct(dims, dtype)


def body(cols, vals, features, weight, bias, cotangent):
    rows, count, size, _ = vals.shape
    nodes, width = features.shape
    dom, rep = lax.axis_size("dom"), lax.axis_size("rep")
    chips = dom // 2
    own_blocks = nodes // size
    quarter_blocks = own_blocks * dom
    part = rows * size // rep
    params = pltpu.CompilerParams(vmem_limit_bytes=(8 + dom // 2) * 1024 * 1024)

    def call(kernel, out_shape, in_specs, aliases={}, cost=0):
        single = not isinstance(out_shape, list)
        return pl.pallas_call(
            kernel,
            out_shape=out_shape,
            in_specs=in_specs,
            out_specs=VMEM if single else [VMEM] * len(out_shape),
            input_output_aliases=aliases,
            compiler_params=params,
            cost_estimate=pl.CostEstimate(flops=cost, bytes_accessed=0, transcendentals=0),
        )

    flipped, own = call(
        early_kernel,
        [shape((rows, count * size, size), BF16), shape(features.shape, BF16)],
        [VMEM] * 2,
    )(vals, features)

    def join(*values):
        nodes_in = sum(v.shape[0] for v in values)
        return call(join_kernel, shape((nodes_in, width), BF16), [VMEM] * len(values))(*values)

    half = chips // 2 - 1
    turns = [*range(1, half + 1), chips - 1, *range(half + 1, chips - 1)]
    across = {turn: cross(features, turn, chips) for turn in turns}
    mine = join(own, *[across[turn] for turn in turns[:half]])
    mine = join(mine, across[chips - 1])
    mine = join(mine, *[across[turn] for turn in turns[half + 1 :]])
    far = swap(mine, "dom", 1)
    place = call(
        functools.partial(place_kernel, own_blocks, chips),
        shape((rows * count, 128), jnp.int32),
        [VMEM] * 2,
    )(cols.T, mine)

    partials = call(
        functools.partial(aggregate_kernel, rep),
        [shape((part, width), BF16 if j else F32) for j in range(rep)],
        [VMEM] * 4,
    )(place, vals, mine, far)
    arrived = {j: swap(partials[j], "rep", j) if j else partials[j] for j in range(rep)}
    order = [*range(2, rep), 1]
    own_rows = arrived[0]
    for j in order:
        own_rows = call(add_kernel, shape((part, width), F32 if j > 1 else BF16), [VMEM] * 2)(
            own_rows, arrived[j]
        )
    pieces = {0: own_rows}
    for j in order:
        pieces[j] = swap(own_rows, "rep", j)

    outputs, carried = [], []
    for j, piece in pieces.items():
        outs = [shape((part, width), BF16), shape((quarter_blocks, size, width), F32)]
        if j != 1:
            outs += [shape((2, width, width), F32)]
        else:
            outs += [
                shape((nodes + width, width), BF16),
                shape(((chips - 1) * nodes, width), BF16),
            ]
        output, *carried = call(
            functools.partial(layer_kernel, rep, count, own_blocks, j),
            outs,
            [VMEM] * (6 + len(carried)),
            aliases={6: 1} if carried else {},
        )(place, flipped, cotangent, weight, bias.reshape(1, width), piece, *carried)
        outputs.append(output)
    contrib, first, rest = carried

    message = shape((nodes + width, width), BF16)
    got_first, got_rest = swap(first, "dom", 1), swap(rest, "dom", 1)
    sent = call(first_pair_kernel, message, [VMEM] * 3, cost=5 * 10**9)(contrib, first, got_first)
    own, *sends = call(
        rest_pair_kernel,
        [shape((nodes, width), F32)] + [message] * (chips - 2),
        [VMEM] * 3,
        cost=10**9,
    )(contrib, sent, got_rest)
    got = [cross(value, turn, chips) for value, turn in zip([sent, *sends], turns)]
    output = call(
        functools.partial(order_kernel, list(pieces)), shape((rows * size, width), BF16), [VMEM] * rep
    )(*outputs)
    lifted = call(lift_kernel, shape(message.shape, F32), [VMEM], cost=10**9)(got[0])
    early = call(
        early_sum_kernel,
        shape((nodes + (half + 1) * width, width), F32),
        [VMEM] * (3 + half),
    )(own, sent, lifted, *got[1 : half + 1])
    feature_grad, weight_grad = call(
        final_kernel,
        [shape((nodes, width), F32), shape((width, width), F32)],
        [VMEM] * (1 + half),
    )(early, *got[half + 1 :])
    return output, feature_grad, weight_grad


def solution(mesh):
    placed = (
        P("dom", "rep"),
        P("dom", "rep", None, None),
        P(("rep", "dom"), None),
        P(),
        P(),
        P("dom", None),
    )
    return jax.shard_map(
        body,
        mesh=mesh,
        in_specs=placed,
        out_specs=(P("dom", None), P(("rep", "dom"), None), P()),
        check_vma=False,
    )
```

```python
import functools

import jax
import jax.numpy as jnp
from jax import lax
from jax.experimental import pallas as pl
from jax.experimental.pallas import tpu as pltpu
from jax.sharding import PartitionSpec as P

BF16 = jnp.bfloat16
F32 = jnp.float32
VMEM = pl.BlockSpec(memory_space=pltpu.VMEM)


def swap(value, axis, distance):
    size = lax.axis_size(axis)
    return lax.ppermute(value, axis, [(i, i ^ distance) for i in range(size)])


def matmul(a, b, contract):
    return lax.dot_general(a, b, ((contract[:1], contract[1:]), ((), ())), preferred_element_type=F32)


def early_kernel(vals_ref, features_ref, flipped_ref, own_ref):
    rows, count, size, _ = vals_ref.shape
    own_ref[...] = features_ref[...]
    for row in range(rows):
        for k in range(count):
            flipped_ref[row, k * size : (k + 1) * size] = vals_ref[row, k].T


def place_kernel(own_blocks, dom, cols_ref, _, place_ref):
    count, rows = cols_ref.shape
    for row in range(rows):
        for k in range(count):
            col = cols_ref[k, row] - lax.axis_index("rep") * (own_blocks * dom)
            owner = lax.div(col, jnp.int32(own_blocks)) ^ lax.axis_index("dom")
            side = jnp.where(owner > 1, 1 - (owner & 1), owner)
            place = (side * (dom // 2) + (owner >> 1)) * own_blocks
            place += lax.rem(col, jnp.int32(own_blocks))
            place_ref[row * count + k : row * count + k + 1, :] = jnp.full((1, 128), place, jnp.int32)


def join_kernel(*refs):
    pieces, out_ref = refs[:-1], refs[-1]
    first = 0
    for piece in pieces:
        out_ref[first : first + piece.shape[0]] = piece[...]
        first += piece.shape[0]


def last_join_kernel(*refs):
    near, middle, out_ref = refs[:-2], refs[-2], refs[-1]
    nodes = near[0].shape[0]
    body = middle.shape[0] - 2 * nodes
    out_ref[:nodes] = middle[body : body + nodes]
    first = nodes
    for piece in near:
        out_ref[first : first + nodes] = piece[...]
        first += nodes
    out_ref[first : first + body] = middle[:body]
    out_ref[first + body :] = middle[body + nodes :]


def aggregate_kernel(rep, place_ref, vals_ref, mine_ref, far_ref, *outs):
    rows, count, size, _ = vals_ref.shape
    half = mine_ref.shape[0] // size
    share = rows // rep
    for j in range(rep - 1, -1, -1):
        target = lax.axis_index("rep") ^ j
        for i in range(share):
            row = target * share + i
            total = None
            for k in range(count):
                place = place_ref[row * count + k, 0]
                beyond = place >= half
                index = jnp.where(beyond, place - half, place)
                here = pl.ds(pl.multiple_of(index * size, size), size)
                block = jnp.where(beyond, far_ref[here, :], mine_ref[here, :])
                term = matmul(vals_ref[row, k], block, (1, 0))
                total = term if total is None else total + term
            outs[j][i * size : (i + 1) * size] = total.astype(outs[j].dtype)


def layer_kernel(
    rep, count, own_blocks, j, place_ref, flipped_ref, cotangent_ref, weight_ref, bias_ref, *refs
):
    first, last = j == 0, j == 1
    piece_ref, refs = refs[0], refs[1:]
    if not first:
        (_, sums_in), refs = refs[:2], refs[2:]
    output_ref, contrib, *refs = refs
    rows, _, size = flipped_ref.shape
    share = rows // rep
    quarter_blocks = contrib.shape[0]
    nodes = own_blocks * size
    if first:
        contrib[...] = jnp.zeros_like(contrib)

    target = lax.axis_index("rep") ^ j
    aggregated = piece_ref[...]
    part = aggregated.shape[0]
    here = pl.ds(pl.multiple_of(target * part, part), part)
    hidden = matmul(aggregated, weight_ref[...], (1, 0)) + bias_ref[...]
    gate_prob = jax.nn.sigmoid(hidden)
    output_ref[...] = (hidden * gate_prob).astype(BF16)
    grad_hidden = (
        cotangent_ref[here, :].astype(F32) * gate_prob * (1.0 + hidden * (1.0 - gate_prob))
    ).astype(BF16)
    part_sum = matmul(aggregated, grad_hidden, (0, 0))
    grad_agg = matmul(grad_hidden, weight_ref[...], (1, 1)).astype(BF16)
    for i in range(share):
        row = target * share + i
        terms = matmul(flipped_ref[row], grad_agg[i * size : (i + 1) * size], (1, 0))
        for k in range(count):
            contrib[place_ref[row * count + k, 0]] += terms[k * size : (k + 1) * size]
    if first:
        refs[0][0] = part_sum
        refs[0][1] = jnp.zeros_like(part_sum)
    elif not last:
        refs[0][0] = sums_in[0]
        refs[0][1] = sums_in[1] + part_sum
    else:
        first_ref, rest_ref = refs
        away = contrib[quarter_blocks // 2 :].reshape(quarter_blocks // 2 * size, -1).astype(BF16)
        rest_ref[...] = away[:-nodes]
        first_ref[:nodes] = away[-nodes:]
        first_ref[nodes:] = ((sums_in[0] + part_sum) + sums_in[1]).astype(BF16)


def add_kernel(a_ref, b_ref, out_ref):
    out_ref[...] = (a_ref[...] + b_ref[...].astype(F32)).astype(out_ref.dtype)


def order_kernel(order, *refs):
    pieces, out_ref = refs[:-1], refs[-1]
    part = pieces[0].shape[0]
    for j, piece in zip(order, pieces):
        target = lax.axis_index("rep") ^ j
        out_ref[pl.ds(pl.multiple_of(target * part, part), part), :] = piece[...]


def first_pair_kernel(contrib_ref, sent_ref, got_ref, out_ref):
    blocks, size, _ = contrib_ref.shape
    nodes = out_ref.shape[0] - sent_ref.shape[1]
    last = contrib_ref[blocks // 2 - nodes // size : blocks // 2].reshape(nodes, -1)
    out_ref[:nodes] = (last + got_ref[:nodes].astype(F32)).astype(BF16)
    out_ref[nodes:] = (sent_ref[nodes:].astype(F32) + got_ref[nodes:].astype(F32)).astype(BF16)


def rest_pair_kernel(contrib_ref, first_ref, got_ref, own_ref, *outs):
    size, nodes = contrib_ref.shape[1], own_ref.shape[0]
    for chip in range(len(outs) + 1):
        mine = contrib_ref[chip * nodes // size : (chip + 1) * nodes // size].reshape(nodes, -1)
        total = mine + got_ref[chip * nodes : (chip + 1) * nodes].astype(F32)
        if chip == 0:
            own_ref[...] = total
        else:
            outs[chip - 1][:nodes] = total.astype(BF16)
            outs[chip - 1][nodes:] = first_ref[nodes:]


def total_of(values):
    while len(values) > 1:
        values = [a + b for a, b in zip(values[::2], values[1::2])]
    return values[0]


def lift_kernel(got_ref, out_ref):
    out_ref[...] = got_ref[...].astype(F32)


def half_kernel(levels, *refs):
    for level in range(1, levels):
        first = 1 << level
        got = refs[first - 2 : 2 * first - 2]
        refs[level - levels][...] = total_of([g[...].astype(F32) for g in got])


def final_kernel(own_ref, sent_ref, got_ref, *refs):
    later, (feature_ref, weight_ref) = refs[:-2], refs[-2:]
    nodes = own_ref.shape[0]
    feature = own_ref[...] + got_ref[:nodes].astype(F32)
    weight = sent_ref[nodes:].astype(F32) + got_ref[nodes:].astype(F32)
    for value in later:
        feature += value[:nodes]
        weight += value[nodes:]
    feature_ref[...] = feature
    weight_ref[...] = weight


def shape(dims, dtype):
    return jax.ShapeDtypeStruct(dims, dtype)


def body(cols, vals, features, weight, bias, cotangent):
    rows, count, size, _ = vals.shape
    nodes, width = features.shape
    dom, rep = lax.axis_size("dom"), lax.axis_size("rep")
    chips = dom // 2
    own_blocks = nodes // size
    quarter_blocks = own_blocks * dom
    part = rows * size // rep
    params = pltpu.CompilerParams(vmem_limit_bytes=(8 + dom // 2) * 1024 * 1024)

    def call(kernel, out_shape, in_specs, aliases={}, cost=0):
        single = not isinstance(out_shape, list)
        return pl.pallas_call(
            kernel,
            out_shape=out_shape,
            in_specs=in_specs,
            out_specs=VMEM if single else [VMEM] * len(out_shape),
            input_output_aliases=aliases,
            compiler_params=params,
            cost_estimate=pl.CostEstimate(flops=cost, bytes_accessed=0, transcendentals=0),
        )

    flipped, own = call(
        early_kernel,
        [shape((rows, count * size, size), BF16), shape(features.shape, BF16)],
        [VMEM] * 2,
    )(vals, features)

    def join(*values):
        nodes_in = sum(v.shape[0] for v in values)
        return call(join_kernel, shape((nodes_in, width), BF16), [VMEM] * len(values))(*values)

    across = [swap(features, "dom", 2 * chip + 1) for chip in range(1, chips)]
    front = join(own, across[-1])
    middle = join(*across[chips // 2 - 1 : -1], front)
    mine = call(last_join_kernel, shape((chips * nodes, width), BF16), [VMEM] * (chips // 2))(
        *across[: chips // 2 - 1], middle
    )
    far = swap(mine, "dom", 1)
    place = call(
        functools.partial(place_kernel, own_blocks, dom),
        shape((rows * count, 128), jnp.int32),
        [VMEM] * 2,
    )(cols.T, mine)

    partials = call(
        functools.partial(aggregate_kernel, rep),
        [shape((part, width), BF16 if j else F32) for j in range(rep)],
        [VMEM] * 4,
    )(place, vals, mine, far)
    arrived = {j: swap(partials[j], "rep", j) if j else partials[j] for j in range(rep)}
    order = [*range(2, rep), 1]
    own_rows = arrived[0]
    for j in order:
        own_rows = call(add_kernel, shape((part, width), F32 if j > 1 else BF16), [VMEM] * 2)(
            own_rows, arrived[j]
        )
    pieces = {0: own_rows}
    for j in order:
        pieces[j] = swap(own_rows, "rep", j)

    outputs, carried = [], []
    for j, piece in pieces.items():
        outs = [shape((part, width), BF16), shape((quarter_blocks, size, width), F32)]
        if j != 1:
            outs += [shape((2, width, width), F32)]
        else:
            outs += [
                shape((nodes + width, width), BF16),
                shape(((chips - 1) * nodes, width), BF16),
            ]
        output, *carried = call(
            functools.partial(layer_kernel, rep, count, own_blocks, j),
            outs,
            [VMEM] * (6 + len(carried)),
            aliases={6: 1} if carried else {},
        )(place, flipped, cotangent, weight, bias.reshape(1, width), piece, *carried)
        outputs.append(output)
    contrib, first, rest = carried

    message = shape((nodes + width, width), BF16)
    got_first, got_rest = swap(first, "dom", 1), swap(rest, "dom", 1)
    sends = [call(first_pair_kernel, message, [VMEM] * 3, cost=5000000000)(contrib, first, got_first)]
    own, *others = call(
        rest_pair_kernel, [shape((nodes, width), F32)] + [message] * (chips - 2), [VMEM] * 3, cost=1000000000
    )(contrib, sends[0], got_rest)
    sends = others + sends
    got = {chip: swap(sends[chip - 1], "dom", 2 * chip + 1) for chip in range(chips - 1, 0, -1)}
    output = call(
        functools.partial(order_kernel, list(pieces)), shape((rows * size, width), BF16), [VMEM] * rep
    )(*outputs)
    levels = chips.bit_length() - 1
    total = shape(message.shape, F32)
    got[chips - 1] = call(lift_kernel, total, [VMEM], cost=1000000000)(got[chips - 1])
    later = call(
        functools.partial(half_kernel, levels), [total] * (levels - 1), [VMEM] * (chips - 2), cost=0
    )(*[got[chip] for chip in range(2, chips)])
    feature_grad, weight_grad = call(
        final_kernel,
        [shape((nodes, width), F32), shape((width, width), F32)],
        [VMEM] * (levels + 2),
    )(own, sends[-1], got[1], *later)
    return output, feature_grad, weight_grad


def solution(mesh):
    placed = (
        P("dom", "rep"),
        P("dom", "rep", None, None),
        P(("rep", "dom"), None),
        P(),
        P(),
        P("dom", None),
    )
    return jax.shard_map(
        body,
        mesh=mesh,
        in_specs=placed,
        out_specs=(P("dom", None), P(("rep", "dom"), None), P()),
        check_vma=False,
    )
```

```python
import functools

import jax
import jax.numpy as jnp
from jax import lax
from jax.experimental import pallas as pl
from jax.experimental.pallas import tpu as pltpu
from jax.sharding import PartitionSpec as P

BF16 = jnp.bfloat16
F32 = jnp.float32
VMEM = pl.BlockSpec(memory_space=pltpu.VMEM)


def swap(value, axis, distance):
    size = lax.axis_size(axis)
    return lax.ppermute(value, axis, [(i, i ^ distance) for i in range(size)])


def matmul(a, b, contract):
    return lax.dot_general(a, b, ((contract[:1], contract[1:]), ((), ())), preferred_element_type=F32)


def early_kernel(vals_ref, features_ref, flipped_ref, own_ref):
    rows, count, size, _ = vals_ref.shape
    own_ref[...] = features_ref[...]
    for row in range(rows):
        for k in range(count):
            flipped_ref[row, k * size : (k + 1) * size] = vals_ref[row, k].T


def place_kernel(own_blocks, dom, cols_ref, _, place_ref):
    count, rows = cols_ref.shape
    for row in range(rows):
        for k in range(count):
            col = cols_ref[k, row] - lax.axis_index("rep") * (own_blocks * dom)
            owner = lax.div(col, jnp.int32(own_blocks)) ^ lax.axis_index("dom")
            side = jnp.where(owner > 1, 1 - (owner & 1), owner)
            place = (side * (dom // 2) + (owner >> 1)) * own_blocks
            place += lax.rem(col, jnp.int32(own_blocks))
            place_ref[row * count + k : row * count + k + 1, :] = jnp.full((1, 128), place, jnp.int32)


def join_kernel(*refs):
    pieces, out_ref = refs[:-1], refs[-1]
    first = 0
    for piece in pieces:
        out_ref[first : first + piece.shape[0]] = piece[...]
        first += piece.shape[0]


def last_join_kernel(*refs):
    near, middle, out_ref = refs[:-2], refs[-2], refs[-1]
    nodes = near[0].shape[0]
    body = middle.shape[0] - 2 * nodes
    out_ref[:nodes] = middle[body : body + nodes]
    first = nodes
    for piece in near:
        out_ref[first : first + nodes] = piece[...]
        first += nodes
    out_ref[first : first + body] = middle[:body]
    out_ref[first + body :] = middle[body + nodes :]


def aggregate_kernel(rep, place_ref, vals_ref, mine_ref, far_ref, *outs):
    rows, count, size, _ = vals_ref.shape
    half = mine_ref.shape[0] // size
    share = rows // rep
    for j in range(rep - 1, -1, -1):
        target = lax.axis_index("rep") ^ j
        for i in range(share):
            row = target * share + i
            total = None
            for k in range(count):
                place = place_ref[row * count + k, 0]
                beyond = place >= half
                index = jnp.where(beyond, place - half, place)
                here = pl.ds(pl.multiple_of(index * size, size), size)
                block = jnp.where(beyond, far_ref[here, :], mine_ref[here, :])
                term = matmul(vals_ref[row, k], block, (1, 0))
                total = term if total is None else total + term
            outs[j][i * size : (i + 1) * size] = total.astype(outs[j].dtype)


def layer_kernel(
    rep, count, own_blocks, j, place_ref, flipped_ref, cotangent_ref, weight_ref, bias_ref, *refs
):
    first, last = j == 0, j == 3
    piece_ref, refs = refs[0], refs[1:]
    if not first:
        (_, sums_in), refs = refs[:2], refs[2:]
    output_ref, contrib, *refs = refs
    rows, _, size = flipped_ref.shape
    share = rows // rep
    quarter_blocks = contrib.shape[0]
    nodes = own_blocks * size
    if first:
        contrib[...] = jnp.zeros_like(contrib)

    target = lax.axis_index("rep") ^ j
    aggregated = piece_ref[...]
    part = aggregated.shape[0]
    here = pl.ds(pl.multiple_of(target * part, part), part)
    hidden = matmul(aggregated, weight_ref[...], (1, 0)) + bias_ref[...]
    gate_prob = jax.nn.sigmoid(hidden)
    output_ref[...] = (hidden * gate_prob).astype(BF16)
    grad_hidden = (
        cotangent_ref[here, :].astype(F32) * gate_prob * (1.0 + hidden * (1.0 - gate_prob))
    ).astype(BF16)
    part_sum = matmul(aggregated, grad_hidden, (0, 0))
    grad_agg = matmul(grad_hidden, weight_ref[...], (1, 1)).astype(BF16)
    for i in range(share):
        row = target * share + i
        terms = matmul(flipped_ref[row], grad_agg[i * size : (i + 1) * size], (1, 0))
        for k in range(count):
            contrib[place_ref[row * count + k, 0]] += terms[k * size : (k + 1) * size]
    if j == 0:
        refs[0][0] = part_sum
        refs[0][1] = jnp.zeros_like(part_sum)
    elif j == 2:
        refs[0][0] = sums_in[0]
        refs[0][1] = part_sum
    elif j == 1:
        refs[0][0] = sums_in[0] + part_sum
        refs[0][1] = sums_in[1]
    else:
        first_ref, rest_ref = refs
        away = contrib[quarter_blocks // 2 :].reshape(quarter_blocks // 2 * size, -1).astype(BF16)
        rest_ref[...] = away[:-nodes]
        first_ref[:nodes] = away[-nodes:]
        first_ref[nodes:] = (sums_in[0] + (sums_in[1] + part_sum)).astype(BF16)


def add_kernel(a_ref, b_ref, out_ref):
    out_ref[...] = (a_ref[...] + b_ref[...].astype(F32)).astype(out_ref.dtype)


def order_kernel(order, *refs):
    pieces, out_ref = refs[:-1], refs[-1]
    part = pieces[0].shape[0]
    for j, piece in zip(order, pieces):
        target = lax.axis_index("rep") ^ j
        out_ref[pl.ds(pl.multiple_of(target * part, part), part), :] = piece[...]


def first_pair_kernel(contrib_ref, sent_ref, got_ref, out_ref):
    blocks, size, _ = contrib_ref.shape
    nodes = out_ref.shape[0] - sent_ref.shape[1]
    last = contrib_ref[blocks // 2 - nodes // size : blocks // 2].reshape(nodes, -1)
    out_ref[:nodes] = (last + got_ref[:nodes].astype(F32)).astype(BF16)
    out_ref[nodes:] = (sent_ref[nodes:].astype(F32) + got_ref[nodes:].astype(F32)).astype(BF16)


def rest_pair_kernel(contrib_ref, first_ref, got_ref, own_ref, *outs):
    size, nodes = contrib_ref.shape[1], own_ref.shape[0]
    for chip in range(len(outs) + 1):
        mine = contrib_ref[chip * nodes // size : (chip + 1) * nodes // size].reshape(nodes, -1)
        total = mine + got_ref[chip * nodes : (chip + 1) * nodes].astype(F32)
        if chip == 0:
            own_ref[...] = total
        else:
            outs[chip - 1][:nodes] = total.astype(BF16)
            outs[chip - 1][nodes:] = first_ref[nodes:]


def total_of(values):
    while len(values) > 1:
        values = [a + b for a, b in zip(values[::2], values[1::2])]
    return values[0]


def lift_kernel(got_ref, out_ref):
    out_ref[...] = got_ref[...].astype(F32)


def half_kernel(levels, *refs):
    for level in range(1, levels):
        first = 1 << level
        got = refs[first - 2 : 2 * first - 2]
        refs[level - levels][...] = total_of([g[...].astype(F32) for g in got])


def final_kernel(own_ref, sent_ref, got_ref, *refs):
    later, (feature_ref, weight_ref) = refs[:-2], refs[-2:]
    nodes = own_ref.shape[0]
    feature = own_ref[...] + got_ref[:nodes].astype(F32)
    weight = sent_ref[nodes:].astype(F32) + got_ref[nodes:].astype(F32)
    for value in later:
        feature += value[:nodes]
        weight += value[nodes:]
    feature_ref[...] = feature
    weight_ref[...] = weight


def shape(dims, dtype):
    return jax.ShapeDtypeStruct(dims, dtype)


def body(cols, vals, features, weight, bias, cotangent):
    rows, count, size, _ = vals.shape
    nodes, width = features.shape
    dom, rep = lax.axis_size("dom"), lax.axis_size("rep")
    chips = dom // 2
    own_blocks = nodes // size
    quarter_blocks = own_blocks * dom
    part = rows * size // rep
    params = pltpu.CompilerParams(vmem_limit_bytes=(8 + dom // 2) * 1024 * 1024)

    def call(kernel, out_shape, in_specs, aliases={}, cost=0):
        single = not isinstance(out_shape, list)
        return pl.pallas_call(
            kernel,
            out_shape=out_shape,
            in_specs=in_specs,
            out_specs=VMEM if single else [VMEM] * len(out_shape),
            input_output_aliases=aliases,
            compiler_params=params,
            cost_estimate=pl.CostEstimate(flops=cost, bytes_accessed=0, transcendentals=0),
        )

    flipped, own = call(
        early_kernel,
        [shape((rows, count * size, size), BF16), shape(features.shape, BF16)],
        [VMEM] * 2,
    )(vals, features)

    def join(*values):
        nodes_in = sum(v.shape[0] for v in values)
        return call(join_kernel, shape((nodes_in, width), BF16), [VMEM] * len(values))(*values)

    across = [swap(features, "dom", 2 * chip + 1) for chip in range(1, chips)]
    front = join(own, across[-1])
    middle = join(*across[chips // 2 - 1 : -1], front)
    mine = call(last_join_kernel, shape((chips * nodes, width), BF16), [VMEM] * (chips // 2))(
        *across[: chips // 2 - 1], middle
    )
    far = swap(mine, "dom", 1)
    place = call(
        functools.partial(place_kernel, own_blocks, dom),
        shape((rows * count, 128), jnp.int32),
        [VMEM] * 2,
    )(cols.T, mine)

    partials = call(
        functools.partial(aggregate_kernel, rep),
        [shape((part, width), BF16 if j else F32) for j in range(rep)],
        [VMEM] * 4,
    )(place, vals, mine, far)
    arrived = {j: swap(partials[j], "rep", j) if j else partials[j] for j in range(rep)}
    order = [2, 1, 3]
    own_rows = arrived[0]
    for j in order:
        own_rows = call(add_kernel, shape((part, width), F32 if j != 3 else BF16), [VMEM] * 2)(
            own_rows, arrived[j]
        )
    pieces = {0: own_rows}
    for j in order:
        pieces[j] = swap(own_rows, "rep", j)

    outputs, carried = [], []
    for j, piece in pieces.items():
        outs = [shape((part, width), BF16), shape((quarter_blocks, size, width), F32)]
        if j != 3:
            outs += [shape((2, width, width), F32)]
        else:
            outs += [
                shape((nodes + width, width), BF16),
                shape(((chips - 1) * nodes, width), BF16),
            ]
        output, *carried = call(
            functools.partial(layer_kernel, rep, count, own_blocks, j),
            outs,
            [VMEM] * (6 + len(carried)),
            aliases={6: 1} if carried else {},
        )(place, flipped, cotangent, weight, bias.reshape(1, width), piece, *carried)
        outputs.append(output)
    contrib, first, rest = carried

    message = shape((nodes + width, width), BF16)
    got_first, got_rest = swap(first, "dom", 1), swap(rest, "dom", 1)
    sends = [call(first_pair_kernel, message, [VMEM] * 3, cost=5000000000)(contrib, first, got_first)]
    own, *others = call(
        rest_pair_kernel, [shape((nodes, width), F32)] + [message] * (chips - 2), [VMEM] * 3, cost=1000000000
    )(contrib, sends[0], got_rest)
    sends = others + sends
    got = {chip: swap(sends[chip - 1], "dom", 2 * chip + 1) for chip in range(chips - 1, 0, -1)}
    output = call(
        functools.partial(order_kernel, list(pieces)), shape((rows * size, width), BF16), [VMEM] * rep
    )(*outputs)
    levels = chips.bit_length() - 1
    total = shape(message.shape, F32)
    got[chips - 1] = call(lift_kernel, total, [VMEM], cost=1000000000)(got[chips - 1])
    later = call(
        functools.partial(half_kernel, levels), [total] * (levels - 1), [VMEM] * (chips - 2), cost=0
    )(*[got[chip] for chip in range(2, chips)])
    feature_grad, weight_grad = call(
        final_kernel,
        [shape((nodes, width), F32), shape((width, width), F32)],
        [VMEM] * (levels + 2),
    )(own, sends[-1], got[1], *later)
    return output, feature_grad, weight_grad


def solution(mesh):
    placed = (
        P("dom", "rep"),
        P("dom", "rep", None, None),
        P(("rep", "dom"), None),
        P(),
        P(),
        P("dom", None),
    )
    return jax.shard_map(
        body,
        mesh=mesh,
        in_specs=placed,
        out_specs=(P("dom", None), P(("rep", "dom"), None), P()),
        check_vma=False,
    )
```

```python
import functools

import jax
import jax.numpy as jnp
from jax import lax
from jax.experimental import pallas as pl
from jax.experimental.pallas import tpu as pltpu
from jax.sharding import PartitionSpec as P

BF16 = jnp.bfloat16
F32 = jnp.float32
VMEM = pl.BlockSpec(memory_space=pltpu.VMEM)


def swap(value, axis, distance):
    size = lax.axis_size(axis)
    return lax.ppermute(value, axis, [(i, i ^ distance) for i in range(size)])


def matmul(a, b, contract):
    return lax.dot_general(a, b, ((contract[:1], contract[1:]), ((), ())), preferred_element_type=F32)


def early_kernel(vals_ref, features_ref, flipped_ref, own_ref):
    rows, count, size, _ = vals_ref.shape
    own_ref[...] = features_ref[...]
    for row in range(rows):
        for k in range(count):
            flipped_ref[row, k * size : (k + 1) * size] = vals_ref[row, k].T


def place_kernel(own_blocks, dom, cols_ref, _, place_ref):
    count, rows = cols_ref.shape
    for row in range(rows):
        for k in range(count):
            col = cols_ref[k, row] - lax.axis_index("rep") * (own_blocks * dom)
            owner = lax.div(col, jnp.int32(own_blocks)) ^ lax.axis_index("dom")
            side = jnp.where(owner > 1, 1 - (owner & 1), owner)
            place = (side * (dom // 2) + (owner >> 1)) * own_blocks
            place += lax.rem(col, jnp.int32(own_blocks))
            place_ref[row * count + k : row * count + k + 1, :] = jnp.full((1, 128), place, jnp.int32)


def join_kernel(*refs):
    pieces, out_ref = refs[:-1], refs[-1]
    first = 0
    for piece in pieces:
        out_ref[first : first + piece.shape[0]] = piece[...]
        first += piece.shape[0]


def last_join_kernel(*refs):
    near, middle, out_ref = refs[:-2], refs[-2], refs[-1]
    nodes = near[0].shape[0]
    body = middle.shape[0] - 2 * nodes
    out_ref[:nodes] = middle[body : body + nodes]
    first = nodes
    for piece in near:
        out_ref[first : first + nodes] = piece[...]
        first += nodes
    out_ref[first : first + body] = middle[:body]
    out_ref[first + body :] = middle[body + nodes :]


def aggregate_kernel(rep, place_ref, vals_ref, mine_ref, far_ref, *outs):
    rows, count, size, _ = vals_ref.shape
    half = mine_ref.shape[0] // size
    share = rows // rep
    for j in range(rep - 1, -1, -1):
        target = lax.axis_index("rep") ^ j
        for i in range(share):
            row = target * share + i
            total = None
            for k in range(count):
                place = place_ref[row * count + k, 0]
                beyond = place >= half
                index = jnp.where(beyond, place - half, place)
                here = pl.ds(pl.multiple_of(index * size, size), size)
                block = jnp.where(beyond, far_ref[here, :], mine_ref[here, :])
                term = matmul(vals_ref[row, k], block, (1, 0))
                total = term if total is None else total + term
            outs[j][i * size : (i + 1) * size] = total.astype(outs[j].dtype)


def layer_kernel(
    rep, count, own_blocks, j, place_ref, flipped_ref, cotangent_ref, weight_ref, bias_ref, *refs
):
    first, last = j == 0, j == 2
    piece_ref, refs = refs[0], refs[1:]
    if not first:
        (_, sums_in), refs = refs[:2], refs[2:]
    output_ref, contrib, *refs = refs
    rows, _, size = flipped_ref.shape
    share = rows // rep
    quarter_blocks = contrib.shape[0]
    nodes = own_blocks * size
    if first:
        contrib[...] = jnp.zeros_like(contrib)

    target = lax.axis_index("rep") ^ j
    aggregated = piece_ref[...]
    part = aggregated.shape[0]
    here = pl.ds(pl.multiple_of(target * part, part), part)
    hidden = matmul(aggregated, weight_ref[...], (1, 0)) + bias_ref[...]
    gate_prob = jax.nn.sigmoid(hidden)
    output_ref[...] = (hidden * gate_prob).astype(BF16)
    grad_hidden = (
        cotangent_ref[here, :].astype(F32) * gate_prob * (1.0 + hidden * (1.0 - gate_prob))
    ).astype(BF16)
    part_sum = matmul(aggregated, grad_hidden, (0, 0))
    grad_agg = matmul(grad_hidden, weight_ref[...], (1, 1)).astype(BF16)
    for i in range(share):
        row = target * share + i
        terms = matmul(flipped_ref[row], grad_agg[i * size : (i + 1) * size], (1, 0))
        for k in range(count):
            contrib[place_ref[row * count + k, 0]] += terms[k * size : (k + 1) * size]
    if j == 0:
        refs[0][0] = part_sum
        refs[0][1] = jnp.zeros_like(part_sum)
    elif j == 3:
        refs[0][0] = sums_in[0]
        refs[0][1] = part_sum
    elif j == 1:
        refs[0][0] = sums_in[0] + part_sum
        refs[0][1] = sums_in[1]
    else:
        first_ref, rest_ref = refs
        away = contrib[quarter_blocks // 2 :].reshape(quarter_blocks // 2 * size, -1).astype(BF16)
        rest_ref[...] = away[:-nodes]
        first_ref[:nodes] = away[-nodes:]
        first_ref[nodes:] = (sums_in[0] + (sums_in[1] + part_sum)).astype(BF16)


def add_kernel(a_ref, b_ref, out_ref):
    out_ref[...] = (a_ref[...] + b_ref[...].astype(F32)).astype(out_ref.dtype)


def order_kernel(order, *refs):
    pieces, out_ref = refs[:-1], refs[-1]
    part = pieces[0].shape[0]
    for j, piece in zip(order, pieces):
        target = lax.axis_index("rep") ^ j
        out_ref[pl.ds(pl.multiple_of(target * part, part), part), :] = piece[...]


def first_pair_kernel(contrib_ref, sent_ref, got_ref, out_ref):
    blocks, size, _ = contrib_ref.shape
    nodes = out_ref.shape[0] - sent_ref.shape[1]
    last = contrib_ref[blocks // 2 - nodes // size : blocks // 2].reshape(nodes, -1)
    out_ref[:nodes] = (last + got_ref[:nodes].astype(F32)).astype(BF16)
    out_ref[nodes:] = (sent_ref[nodes:].astype(F32) + got_ref[nodes:].astype(F32)).astype(BF16)


def rest_pair_kernel(contrib_ref, first_ref, got_ref, own_ref, *outs):
    size, nodes = contrib_ref.shape[1], own_ref.shape[0]
    for chip in range(len(outs) + 1):
        mine = contrib_ref[chip * nodes // size : (chip + 1) * nodes // size].reshape(nodes, -1)
        total = mine + got_ref[chip * nodes : (chip + 1) * nodes].astype(F32)
        if chip == 0:
            own_ref[...] = total
        else:
            outs[chip - 1][:nodes] = total.astype(BF16)
            outs[chip - 1][nodes:] = first_ref[nodes:]


def total_of(values):
    while len(values) > 1:
        values = [a + b for a, b in zip(values[::2], values[1::2])]
    return values[0]


def lift_kernel(got_ref, out_ref):
    out_ref[...] = got_ref[...].astype(F32)


def half_kernel(levels, *refs):
    for level in range(1, levels):
        first = 1 << level
        got = refs[first - 2 : 2 * first - 2]
        refs[level - levels][...] = total_of([g[...].astype(F32) for g in got])


def final_kernel(own_ref, sent_ref, got_ref, *refs):
    later, (feature_ref, weight_ref) = refs[:-2], refs[-2:]
    nodes = own_ref.shape[0]
    feature = own_ref[...] + got_ref[:nodes].astype(F32)
    weight = sent_ref[nodes:].astype(F32) + got_ref[nodes:].astype(F32)
    for value in later:
        feature += value[:nodes]
        weight += value[nodes:]
    feature_ref[...] = feature
    weight_ref[...] = weight


def shape(dims, dtype):
    return jax.ShapeDtypeStruct(dims, dtype)


def body(cols, vals, features, weight, bias, cotangent):
    rows, count, size, _ = vals.shape
    nodes, width = features.shape
    dom, rep = lax.axis_size("dom"), lax.axis_size("rep")
    chips = dom // 2
    own_blocks = nodes // size
    quarter_blocks = own_blocks * dom
    part = rows * size // rep
    params = pltpu.CompilerParams(vmem_limit_bytes=(8 + dom // 2) * 1024 * 1024)

    def call(kernel, out_shape, in_specs, aliases={}, cost=0):
        single = not isinstance(out_shape, list)
        return pl.pallas_call(
            kernel,
            out_shape=out_shape,
            in_specs=in_specs,
            out_specs=VMEM if single else [VMEM] * len(out_shape),
            input_output_aliases=aliases,
            compiler_params=params,
            cost_estimate=pl.CostEstimate(flops=cost, bytes_accessed=0, transcendentals=0),
        )

    flipped, own = call(
        early_kernel,
        [shape((rows, count * size, size), BF16), shape(features.shape, BF16)],
        [VMEM] * 2,
    )(vals, features)

    def join(*values):
        nodes_in = sum(v.shape[0] for v in values)
        return call(join_kernel, shape((nodes_in, width), BF16), [VMEM] * len(values))(*values)

    across = [swap(features, "dom", 2 * chip + 1) for chip in range(1, chips)]
    front = join(own, across[-1])
    middle = join(*across[chips // 2 - 1 : -1], front)
    mine = call(last_join_kernel, shape((chips * nodes, width), BF16), [VMEM] * (chips // 2))(
        *across[: chips // 2 - 1], middle
    )
    far = swap(mine, "dom", 1)
    place = call(
        functools.partial(place_kernel, own_blocks, dom),
        shape((rows * count, 128), jnp.int32),
        [VMEM] * 2,
    )(cols.T, mine)

    partials = call(
        functools.partial(aggregate_kernel, rep),
        [shape((part, width), BF16 if j else F32) for j in range(rep)],
        [VMEM] * 4,
    )(place, vals, mine, far)
    arrived = {j: swap(partials[j], "rep", j) if j else partials[j] for j in range(rep)}
    order = [3, 1, 2]
    own_rows = arrived[0]
    for j in order:
        own_rows = call(add_kernel, shape((part, width), F32 if j != 2 else BF16), [VMEM] * 2)(
            own_rows, arrived[j]
        )
    pieces = {0: own_rows}
    for j in order:
        pieces[j] = swap(own_rows, "rep", j)

    outputs, carried = [], []
    for j, piece in pieces.items():
        outs = [shape((part, width), BF16), shape((quarter_blocks, size, width), F32)]
        if j != 2:
            outs += [shape((2, width, width), F32)]
        else:
            outs += [
                shape((nodes + width, width), BF16),
                shape(((chips - 1) * nodes, width), BF16),
            ]
        output, *carried = call(
            functools.partial(layer_kernel, rep, count, own_blocks, j),
            outs,
            [VMEM] * (6 + len(carried)),
            aliases={6: 1} if carried else {},
        )(place, flipped, cotangent, weight, bias.reshape(1, width), piece, *carried)
        outputs.append(output)
    contrib, first, rest = carried

    message = shape((nodes + width, width), BF16)
    got_first, got_rest = swap(first, "dom", 1), swap(rest, "dom", 1)
    sends = [call(first_pair_kernel, message, [VMEM] * 3, cost=5000000000)(contrib, first, got_first)]
    own, *others = call(
        rest_pair_kernel, [shape((nodes, width), F32)] + [message] * (chips - 2), [VMEM] * 3, cost=1000000000
    )(contrib, sends[0], got_rest)
    sends = others + sends
    got = {chip: swap(sends[chip - 1], "dom", 2 * chip + 1) for chip in range(chips - 1, 0, -1)}
    output = call(
        functools.partial(order_kernel, list(pieces)), shape((rows * size, width), BF16), [VMEM] * rep
    )(*outputs)
    levels = chips.bit_length() - 1
    total = shape(message.shape, F32)
    got[chips - 1] = call(lift_kernel, total, [VMEM], cost=1000000000)(got[chips - 1])
    later = call(
        functools.partial(half_kernel, levels), [total] * (levels - 1), [VMEM] * (chips - 2), cost=0
    )(*[got[chip] for chip in range(2, chips)])
    feature_grad, weight_grad = call(
        final_kernel,
        [shape((nodes, width), F32), shape((width, width), F32)],
        [VMEM] * (levels + 2),
    )(own, sends[-1], got[1], *later)
    return output, feature_grad, weight_grad


def solution(mesh):
    placed = (
        P("dom", "rep"),
        P("dom", "rep", None, None),
        P(("rep", "dom"), None),
        P(),
        P(),
        P("dom", None),
    )
    return jax.shard_map(
        body,
        mesh=mesh,
        in_specs=placed,
        out_specs=(P("dom", None), P(("rep", "dom"), None), P()),
        check_vma=False,
    )
```

```python
import functools

import jax
import jax.numpy as jnp
from jax import lax
from jax.experimental import pallas as pl
from jax.experimental.pallas import tpu as pltpu
from jax.sharding import PartitionSpec as P

BF16 = jnp.bfloat16
F32 = jnp.float32
VMEM = pl.BlockSpec(memory_space=pltpu.VMEM)


def swap(value, axis, distance):
    size = lax.axis_size(axis)
    return lax.ppermute(value, axis, [(i, i ^ distance) for i in range(size)])


def lift(value, distance):
    rep, dom = lax.axis_size("rep"), lax.axis_size("dom")
    pairs = [(r * dom + d, (r ^ distance) * dom + (d ^ 1)) for r in range(rep) for d in range(dom)]
    return lax.ppermute(value, ("rep", "dom"), pairs)


def matmul(a, b, contract):
    return lax.dot_general(a, b, ((contract[:1], contract[1:]), ((), ())), preferred_element_type=F32)


def early_kernel(vals_ref, features_ref, flipped_ref, own_ref):
    rows, count, size, _ = vals_ref.shape
    own_ref[...] = features_ref[...]
    for row in range(rows):
        for k in range(count):
            flipped_ref[row, k * size : (k + 1) * size] = vals_ref[row, k].T


def place_kernel(own_blocks, dom, cols_ref, _, place_ref):
    count, rows = cols_ref.shape
    for row in range(rows):
        for k in range(count):
            col = cols_ref[k, row] - lax.axis_index("rep") * (own_blocks * dom)
            owner = lax.div(col, jnp.int32(own_blocks)) ^ lax.axis_index("dom")
            side = jnp.where(owner > 1, 1 - (owner & 1), owner)
            place = (side * (dom // 2) + (owner >> 1)) * own_blocks
            place += lax.rem(col, jnp.int32(own_blocks))
            place_ref[row * count + k : row * count + k + 1, :] = jnp.full((1, 128), place, jnp.int32)


def join_kernel(*refs):
    pieces, out_ref = refs[:-1], refs[-1]
    first = 0
    for piece in pieces:
        out_ref[first : first + piece.shape[0]] = piece[...]
        first += piece.shape[0]


def last_join_kernel(*refs):
    near, middle, out_ref = refs[:-2], refs[-2], refs[-1]
    nodes = near[0].shape[0]
    body = middle.shape[0] - 2 * nodes
    out_ref[:nodes] = middle[body : body + nodes]
    first = nodes
    for piece in near:
        out_ref[first : first + nodes] = piece[...]
        first += nodes
    out_ref[first : first + body] = middle[:body]
    out_ref[first + body :] = middle[body + nodes :]


def aggregate_kernel(rep, place_ref, vals_ref, mine_ref, far_ref, *outs):
    rows, count, size, _ = vals_ref.shape
    half = mine_ref.shape[0] // size
    share = rows // rep
    for j in range(rep - 1, -1, -1):
        target = lax.axis_index("rep") ^ j
        for i in range(share):
            row = target * share + i
            total = None
            for k in range(count):
                place = place_ref[row * count + k, 0]
                beyond = place >= half
                index = jnp.where(beyond, place - half, place)
                here = pl.ds(pl.multiple_of(index * size, size), size)
                block = jnp.where(beyond, far_ref[here, :], mine_ref[here, :])
                term = matmul(vals_ref[row, k], block, (1, 0))
                total = term if total is None else total + term
            outs[j][i * size : (i + 1) * size] = total.astype(outs[j].dtype)


def layer_kernel(
    rep, count, own_blocks, j, place_ref, flipped_ref, cotangent_ref, weight_ref, bias_ref, *refs
):
    first, last = j == 3, j == 2
    piece_ref, refs = refs[0], refs[1:]
    if not first:
        (_, sums_in), refs = refs[:2], refs[2:]
    output_ref, contrib, *refs = refs
    rows, _, size = flipped_ref.shape
    share = rows // rep
    quarter_blocks = contrib.shape[0]
    nodes = own_blocks * size
    if first:
        contrib[...] = jnp.zeros_like(contrib)

    target = lax.axis_index("rep") ^ j
    aggregated = piece_ref[...]
    part = aggregated.shape[0]
    here = pl.ds(pl.multiple_of(target * part, part), part)
    hidden = matmul(aggregated, weight_ref[...], (1, 0)) + bias_ref[...]
    gate_prob = jax.nn.sigmoid(hidden)
    output_ref[...] = (hidden * gate_prob).astype(BF16)
    grad_hidden = (
        cotangent_ref[here, :].astype(F32) * gate_prob * (1.0 + hidden * (1.0 - gate_prob))
    ).astype(BF16)
    part_sum = matmul(aggregated, grad_hidden, (0, 0))
    grad_agg = matmul(grad_hidden, weight_ref[...], (1, 1)).astype(BF16)
    for i in range(share):
        row = target * share + i
        terms = matmul(flipped_ref[row], grad_agg[i * size : (i + 1) * size], (1, 0))
        for k in range(count):
            contrib[place_ref[row * count + k, 0]] += terms[k * size : (k + 1) * size]
    if j == 3:
        refs[0][0] = jnp.zeros_like(part_sum)
        refs[0][1] = part_sum
    elif not last:
        refs[0][0] = sums_in[0] + part_sum
        refs[0][1] = sums_in[1]
    else:
        first_ref, rest_ref = refs
        away = contrib[quarter_blocks // 2 :].reshape(quarter_blocks // 2 * size, -1).astype(BF16)
        rest_ref[...] = away[:-nodes]
        first_ref[:nodes] = away[-nodes:]
        first_ref[nodes:] = (sums_in[0] + (sums_in[1] + part_sum)).astype(BF16)


def add_kernel(a_ref, b_ref, out_ref):
    out_ref[...] = (a_ref[...].astype(F32) + b_ref[...].astype(F32)).astype(out_ref.dtype)


def order_kernel(order, *refs):
    pieces, out_ref = refs[:-1], refs[-1]
    part = pieces[0].shape[0]
    for j, piece in zip(order, pieces):
        target = lax.axis_index("rep") ^ j
        out_ref[pl.ds(pl.multiple_of(target * part, part), part), :] = piece[...]


def first_pair_kernel(contrib_ref, sent_ref, got_ref, out_ref):
    blocks, size, _ = contrib_ref.shape
    nodes = out_ref.shape[0] - sent_ref.shape[1]
    last = contrib_ref[blocks // 2 - nodes // size : blocks // 2].reshape(nodes, -1)
    out_ref[:nodes] = (last + got_ref[:nodes].astype(F32)).astype(BF16)
    out_ref[nodes:] = (sent_ref[nodes:].astype(F32) + got_ref[nodes:].astype(F32)).astype(BF16)


def rest_pair_kernel(contrib_ref, first_ref, got_ref, own_ref, *outs):
    size, nodes = contrib_ref.shape[1], own_ref.shape[0]
    for chip in range(len(outs) + 1):
        mine = contrib_ref[chip * nodes // size : (chip + 1) * nodes // size].reshape(nodes, -1)
        total = mine + got_ref[chip * nodes : (chip + 1) * nodes].astype(F32)
        if chip == 0:
            own_ref[...] = total
        else:
            outs[chip - 1][:nodes] = total.astype(BF16)
            outs[chip - 1][nodes:] = first_ref[nodes:]


def total_of(values):
    while len(values) > 1:
        values = [a + b for a, b in zip(values[::2], values[1::2])]
    return values[0]


def lift_kernel(got_ref, out_ref):
    out_ref[...] = got_ref[...].astype(F32)


def half_kernel(levels, *refs):
    for level in range(1, levels):
        first = 1 << level
        got = refs[first - 2 : 2 * first - 2]
        refs[level - levels][...] = total_of([g[...].astype(F32) for g in got])


def final_kernel(own_ref, sent_ref, got_ref, *refs):
    later, (feature_ref, weight_ref) = refs[:-2], refs[-2:]
    nodes = own_ref.shape[0]
    feature = own_ref[...] + got_ref[:nodes].astype(F32)
    weight = sent_ref[nodes:].astype(F32) + got_ref[nodes:].astype(F32)
    for value in later:
        feature += value[:nodes]
        weight += value[nodes:]
    feature_ref[...] = feature
    weight_ref[...] = weight


def shape(dims, dtype):
    return jax.ShapeDtypeStruct(dims, dtype)


def body(cols, vals, features, weight, bias, cotangent):
    rows, count, size, _ = vals.shape
    nodes, width = features.shape
    dom, rep = lax.axis_size("dom"), lax.axis_size("rep")
    chips = dom // 2
    own_blocks = nodes // size
    quarter_blocks = own_blocks * dom
    part = rows * size // rep
    params = pltpu.CompilerParams(vmem_limit_bytes=(8 + dom // 2) * 1024 * 1024)

    def call(kernel, out_shape, in_specs, aliases={}, cost=0):
        single = not isinstance(out_shape, list)
        return pl.pallas_call(
            kernel,
            out_shape=out_shape,
            in_specs=in_specs,
            out_specs=VMEM if single else [VMEM] * len(out_shape),
            input_output_aliases=aliases,
            compiler_params=params,
            cost_estimate=pl.CostEstimate(flops=cost, bytes_accessed=0, transcendentals=0),
        )

    flipped, own = call(
        early_kernel,
        [shape((rows, count * size, size), BF16), shape(features.shape, BF16)],
        [VMEM] * 2,
    )(vals, features)

    def join(*values):
        nodes_in = sum(v.shape[0] for v in values)
        return call(join_kernel, shape((nodes_in, width), BF16), [VMEM] * len(values))(*values)

    across = [swap(features, "dom", 2 * chip + 1) for chip in range(1, chips)]
    front = join(own, across[-1])
    middle = join(*across[chips // 2 - 1 : -1], front)
    mine = call(last_join_kernel, shape((chips * nodes, width), BF16), [VMEM] * (chips // 2))(
        *across[: chips // 2 - 1], middle
    )
    far = swap(mine, "dom", 1)
    place = call(
        functools.partial(place_kernel, own_blocks, dom),
        shape((rows * count, 128), jnp.int32),
        [VMEM] * 2,
    )(cols.T, mine)

    partials = call(
        functools.partial(aggregate_kernel, rep),
        [shape((part, width), BF16 if j else F32) for j in range(rep)],
        [VMEM] * 4,
    )(place, vals, mine, far)
    def add(a, b, dtype):
        return call(add_kernel, shape((part, width), dtype), [VMEM] * 2, cost=10**9)(a, b)

    arrived = {j: lift(partials[j], j) for j in (3, 1, 2)}
    total = add(arrived[3], arrived[1], F32)
    total = add(total, arrived[2], F32)
    own_rows = add(total, swap(partials[0], "dom", 1), BF16)
    pieces = {3: lift(own_rows, 3), 1: lift(own_rows, 1)}
    pieces |= {0: swap(own_rows, "dom", 1), 2: lift(own_rows, 2)}

    outputs, carried = [], []
    for j, piece in pieces.items():
        outs = [shape((part, width), BF16), shape((quarter_blocks, size, width), F32)]
        if j != 2:
            outs += [shape((2, width, width), F32)]
        else:
            outs += [
                shape((nodes + width, width), BF16),
                shape(((chips - 1) * nodes, width), BF16),
            ]
        output, *carried = call(
            functools.partial(layer_kernel, rep, count, own_blocks, j),
            outs,
            [VMEM] * (6 + len(carried)),
            aliases={6: 1} if carried else {},
        )(place, flipped, cotangent, weight, bias.reshape(1, width), piece, *carried)
        outputs.append(output)
    contrib, first, rest = carried

    message = shape((nodes + width, width), BF16)
    got_first, got_rest = swap(first, "dom", 1), swap(rest, "dom", 1)
    sends = [call(first_pair_kernel, message, [VMEM] * 3, cost=5000000000)(contrib, first, got_first)]
    own, *others = call(
        rest_pair_kernel, [shape((nodes, width), F32)] + [message] * (chips - 2), [VMEM] * 3, cost=1000000000
    )(contrib, sends[0], got_rest)
    sends = others + sends
    got = {chip: swap(sends[chip - 1], "dom", 2 * chip + 1) for chip in range(chips - 1, 0, -1)}
    output = call(
        functools.partial(order_kernel, list(pieces)), shape((rows * size, width), BF16), [VMEM] * rep
    )(*outputs)
    levels = chips.bit_length() - 1
    total = shape(message.shape, F32)
    got[chips - 1] = call(lift_kernel, total, [VMEM], cost=1000000000)(got[chips - 1])
    later = call(
        functools.partial(half_kernel, levels), [total] * (levels - 1), [VMEM] * (chips - 2), cost=0
    )(*[got[chip] for chip in range(2, chips)])
    feature_grad, weight_grad = call(
        final_kernel,
        [shape((nodes, width), F32), shape((width, width), F32)],
        [VMEM] * (levels + 2),
    )(own, sends[-1], got[1], *later)
    return output, feature_grad, weight_grad


def solution(mesh):
    placed = (
        P("dom", "rep"),
        P("dom", "rep", None, None),
        P(("rep", "dom"), None),
        P(),
        P(),
        P("dom", None),
    )
    return jax.shard_map(
        body,
        mesh=mesh,
        in_specs=placed,
        out_specs=(P("dom", None), P(("rep", "dom"), None), P()),
        check_vma=False,
    )
```

```python
import functools

import jax
import jax.numpy as jnp
from jax import lax
from jax.experimental import pallas as pl
from jax.experimental.pallas import tpu as pltpu
from jax.sharding import PartitionSpec as P

BF16 = jnp.bfloat16
F32 = jnp.float32
VMEM = pl.BlockSpec(memory_space=pltpu.VMEM)


def swap(value, axis, distance):
    size = lax.axis_size(axis)
    return lax.ppermute(value, axis, [(i, i ^ distance) for i in range(size)])


def matmul(a, b, contract):
    return lax.dot_general(a, b, ((contract[:1], contract[1:]), ((), ())), preferred_element_type=F32)


def early_kernel(vals_ref, features_ref, flipped_ref, own_ref):
    rows, count, size, _ = vals_ref.shape
    own_ref[...] = features_ref[...]
    for row in range(rows):
        for k in range(count):
            flipped_ref[row, k * size : (k + 1) * size] = vals_ref[row, k].T


def place_kernel(own_blocks, dom, cols_ref, _, place_ref):
    count, rows = cols_ref.shape
    for row in range(rows):
        for k in range(count):
            col = cols_ref[k, row] - lax.axis_index("rep") * (own_blocks * dom)
            owner = lax.div(col, jnp.int32(own_blocks)) ^ lax.axis_index("dom")
            side = jnp.where(owner > 1, 1 - (owner & 1), owner)
            place = (side * (dom // 2) + (owner >> 1)) * own_blocks
            place += lax.rem(col, jnp.int32(own_blocks))
            place_ref[row * count + k : row * count + k + 1, :] = jnp.full((1, 128), place, jnp.int32)


def join_kernel(*refs):
    pieces, out_ref = refs[:-1], refs[-1]
    first = 0
    for piece in pieces:
        out_ref[first : first + piece.shape[0]] = piece[...]
        first += piece.shape[0]


def wrap_kernel(ends_ref, *refs):
    out_ref = refs[-1]
    nodes = ends_ref.shape[0] // 2
    out_ref[:nodes] = ends_ref[:nodes]
    for at, piece in enumerate(refs[:-1], 1):
        out_ref[at * nodes : (at + 1) * nodes] = piece[...]
    out_ref[out_ref.shape[0] - nodes :] = ends_ref[nodes:]


def aggregate_kernel(rep, place_ref, vals_ref, mine_ref, far_ref, *outs):
    rows, count, size, _ = vals_ref.shape
    half = mine_ref.shape[0] // size
    share = rows // rep
    for j in range(rep - 1, -1, -1):
        target = lax.axis_index("rep") ^ j
        for i in range(share):
            row = target * share + i
            total = None
            for k in range(count):
                place = place_ref[row * count + k, 0]
                beyond = place >= half
                index = jnp.where(beyond, place - half, place)
                here = pl.ds(pl.multiple_of(index * size, size), size)
                block = jnp.where(beyond, far_ref[here, :], mine_ref[here, :])
                term = matmul(vals_ref[row, k], block, (1, 0))
                total = term if total is None else total + term
            outs[j][i * size : (i + 1) * size] = total.astype(outs[j].dtype)


def layer_kernel(
    rep, count, own_blocks, j, place_ref, flipped_ref, cotangent_ref, weight_ref, bias_ref, *refs
):
    first, last = j == 0, j == 2
    piece_ref, refs = refs[0], refs[1:]
    if not first:
        (_, sums_in), refs = refs[:2], refs[2:]
    output_ref, contrib, *refs = refs
    rows, _, size = flipped_ref.shape
    share = rows // rep
    quarter_blocks = contrib.shape[0]
    nodes = own_blocks * size
    if first:
        contrib[...] = jnp.zeros_like(contrib)

    target = lax.axis_index("rep") ^ j
    aggregated = piece_ref[...]
    part = aggregated.shape[0]
    here = pl.ds(pl.multiple_of(target * part, part), part)
    hidden = matmul(aggregated, weight_ref[...], (1, 0)) + bias_ref[...]
    gate_prob = jax.nn.sigmoid(hidden)
    output_ref[...] = (hidden * gate_prob).astype(BF16)
    grad_hidden = (
        cotangent_ref[here, :].astype(F32) * gate_prob * (1.0 + hidden * (1.0 - gate_prob))
    ).astype(BF16)
    part_sum = matmul(aggregated, grad_hidden, (0, 0))
    grad_agg = matmul(grad_hidden, weight_ref[...], (1, 1)).astype(BF16)
    for i in range(share):
        row = target * share + i
        terms = matmul(flipped_ref[row], grad_agg[i * size : (i + 1) * size], (1, 0))
        for k in range(count):
            contrib[place_ref[row * count + k, 0]] += terms[k * size : (k + 1) * size]
    if j == 0:
        refs[0][0] = part_sum
        refs[0][1] = jnp.zeros_like(part_sum)
    elif j == 3:
        refs[0][0] = sums_in[0]
        refs[0][1] = part_sum
    elif j == 1:
        refs[0][0] = sums_in[0] + part_sum
        refs[0][1] = sums_in[1]
    else:
        first_ref, rest_ref = refs
        away = contrib[quarter_blocks // 2 :].reshape(quarter_blocks // 2 * size, -1).astype(BF16)
        rest_ref[...] = away[:-nodes]
        first_ref[:nodes] = away[-nodes:]
        first_ref[nodes:] = (sums_in[0] + (sums_in[1] + part_sum)).astype(BF16)


def add_kernel(a_ref, b_ref, out_ref):
    out_ref[...] = (a_ref[...] + b_ref[...].astype(F32)).astype(out_ref.dtype)


def order_kernel(order, *refs):
    pieces, out_ref = refs[:-1], refs[-1]
    part = pieces[0].shape[0]
    for j, piece in zip(order, pieces):
        target = lax.axis_index("rep") ^ j
        out_ref[pl.ds(pl.multiple_of(target * part, part), part), :] = piece[...]


def first_pair_kernel(contrib_ref, sent_ref, got_ref, out_ref):
    blocks, size, _ = contrib_ref.shape
    nodes = out_ref.shape[0] - sent_ref.shape[1]
    last = contrib_ref[blocks // 2 - nodes // size : blocks // 2].reshape(nodes, -1)
    out_ref[:nodes] = (last + got_ref[:nodes].astype(F32)).astype(BF16)
    out_ref[nodes:] = (sent_ref[nodes:].astype(F32) + got_ref[nodes:].astype(F32)).astype(BF16)


def rest_pair_kernel(contrib_ref, first_ref, got_ref, own_ref, *outs):
    size, nodes = contrib_ref.shape[1], own_ref.shape[0]
    for chip in range(len(outs) + 1):
        mine = contrib_ref[chip * nodes // size : (chip + 1) * nodes // size].reshape(nodes, -1)
        total = mine + got_ref[chip * nodes : (chip + 1) * nodes].astype(F32)
        if chip == 0:
            own_ref[...] = total
        else:
            outs[chip - 1][:nodes] = total.astype(BF16)
            outs[chip - 1][nodes:] = first_ref[nodes:]


def total_of(values):
    while len(values) > 1:
        values = [a + b for a, b in zip(values[::2], values[1::2])]
    return values[0]


def lift_kernel(got_ref, out_ref):
    out_ref[...] = got_ref[...].astype(F32)


def half_kernel(levels, *refs):
    for level in range(1, levels):
        first = 1 << level
        got = refs[first - 2 : 2 * first - 2]
        refs[level - levels][...] = total_of([g[...].astype(F32) for g in got])


def final_kernel(own_ref, sent_ref, got_ref, *refs):
    later, (feature_ref, weight_ref) = refs[:-2], refs[-2:]
    nodes = own_ref.shape[0]
    feature = own_ref[...] + got_ref[:nodes].astype(F32)
    weight = sent_ref[nodes:].astype(F32) + got_ref[nodes:].astype(F32)
    for value in later:
        feature += value[:nodes]
        weight += value[nodes:]
    feature_ref[...] = feature
    weight_ref[...] = weight


def shape(dims, dtype):
    return jax.ShapeDtypeStruct(dims, dtype)


def body(cols, vals, features, weight, bias, cotangent):
    rows, count, size, _ = vals.shape
    nodes, width = features.shape
    dom, rep = lax.axis_size("dom"), lax.axis_size("rep")
    chips = dom // 2
    own_blocks = nodes // size
    quarter_blocks = own_blocks * dom
    part = rows * size // rep
    params = pltpu.CompilerParams(vmem_limit_bytes=(8 + dom // 2) * 1024 * 1024)

    def call(kernel, out_shape, in_specs, aliases={}, cost=0):
        single = not isinstance(out_shape, list)
        return pl.pallas_call(
            kernel,
            out_shape=out_shape,
            in_specs=in_specs,
            out_specs=VMEM if single else [VMEM] * len(out_shape),
            input_output_aliases=aliases,
            compiler_params=params,
            cost_estimate=pl.CostEstimate(flops=cost, bytes_accessed=0, transcendentals=0),
        )

    flipped, own = call(
        early_kernel,
        [shape((rows, count * size, size), BF16), shape(features.shape, BF16)],
        [VMEM] * 2,
    )(vals, features)

    def join(*values):
        nodes_in = sum(v.shape[0] for v in values)
        return call(join_kernel, shape((nodes_in, width), BF16), [VMEM] * len(values))(*values)

    across = [swap(features, "dom", 2 * chip + 1) for chip in range(1, chips)]
    ends = join(own, across[-1])
    far_ends = swap(ends, "dom", 1)
    half = chips // 2 - 1
    beyond = [swap(piece, "dom", 1) for piece in across[half:-1]]
    beyond = [swap(piece, "dom", 1) for piece in across[:half]] + beyond

    def wrap(*values):
        return call(wrap_kernel, shape((chips * nodes, width), BF16), [VMEM] * (chips - 1))(*values)

    mine, far = wrap(ends, *across[:-1]), wrap(far_ends, *beyond)
    place = call(
        functools.partial(place_kernel, own_blocks, dom),
        shape((rows * count, 128), jnp.int32),
        [VMEM] * 2,
    )(cols.T, ends)

    partials = call(
        functools.partial(aggregate_kernel, rep),
        [shape((part, width), BF16 if j else F32) for j in range(rep)],
        [VMEM] * 4,
    )(place, vals, mine, far)
    arrived = {j: swap(partials[j], "rep", j) if j else partials[j] for j in range(rep)}
    order = [3, 1, 2]
    own_rows = arrived[0]
    for j in order:
        own_rows = call(add_kernel, shape((part, width), F32 if j != 2 else BF16), [VMEM] * 2)(
            own_rows, arrived[j]
        )
    pieces = {0: own_rows}
    for j in order:
        pieces[j] = swap(own_rows, "rep", j)

    outputs, carried = [], []
    for j, piece in pieces.items():
        outs = [shape((part, width), BF16), shape((quarter_blocks, size, width), F32)]
        if j != 2:
            outs += [shape((2, width, width), F32)]
        else:
            outs += [
                shape((nodes + width, width), BF16),
                shape(((chips - 1) * nodes, width), BF16),
            ]
        output, *carried = call(
            functools.partial(layer_kernel, rep, count, own_blocks, j),
            outs,
            [VMEM] * (6 + len(carried)),
            aliases={6: 1} if carried else {},
        )(place, flipped, cotangent, weight, bias.reshape(1, width), piece, *carried)
        outputs.append(output)
    contrib, first, rest = carried

    message = shape((nodes + width, width), BF16)
    got_first, got_rest = swap(first, "dom", 1), swap(rest, "dom", 1)
    sends = [call(first_pair_kernel, message, [VMEM] * 3, cost=5000000000)(contrib, first, got_first)]
    own, *others = call(
        rest_pair_kernel, [shape((nodes, width), F32)] + [message] * (chips - 2), [VMEM] * 3, cost=1000000000
    )(contrib, sends[0], got_rest)
    sends = others + sends
    got = {chip: swap(sends[chip - 1], "dom", 2 * chip + 1) for chip in range(chips - 1, 0, -1)}
    output = call(
        functools.partial(order_kernel, list(pieces)), shape((rows * size, width), BF16), [VMEM] * rep
    )(*outputs)
    levels = chips.bit_length() - 1
    total = shape(message.shape, F32)
    got[chips - 1] = call(lift_kernel, total, [VMEM], cost=1000000000)(got[chips - 1])
    later = call(
        functools.partial(half_kernel, levels), [total] * (levels - 1), [VMEM] * (chips - 2), cost=0
    )(*[got[chip] for chip in range(2, chips)])
    feature_grad, weight_grad = call(
        final_kernel,
        [shape((nodes, width), F32), shape((width, width), F32)],
        [VMEM] * (levels + 2),
    )(own, sends[-1], got[1], *later)
    return output, feature_grad, weight_grad


def solution(mesh):
    placed = (
        P("dom", "rep"),
        P("dom", "rep", None, None),
        P(("rep", "dom"), None),
        P(),
        P(),
        P("dom", None),
    )
    return jax.shard_map(
        body,
        mesh=mesh,
        in_specs=placed,
        out_specs=(P("dom", None), P(("rep", "dom"), None), P()),
        check_vma=False,
    )
```

```python
import functools

import jax
import jax.numpy as jnp
from jax import lax
from jax.experimental import pallas as pl
from jax.experimental.pallas import tpu as pltpu
from jax.sharding import PartitionSpec as P

BF16 = jnp.bfloat16
F32 = jnp.float32
VMEM = pl.BlockSpec(memory_space=pltpu.VMEM)


def swap(value, axis, distance):
    size = lax.axis_size(axis)
    return lax.ppermute(value, axis, [(i, i ^ distance) for i in range(size)])


def matmul(a, b, contract):
    return lax.dot_general(a, b, ((contract[:1], contract[1:]), ((), ())), preferred_element_type=F32)


def early_kernel(vals_ref, features_ref, flipped_ref, own_ref):
    rows, count, size, _ = vals_ref.shape
    own_ref[...] = features_ref[...]
    for row in range(rows):
        for k in range(count):
            flipped_ref[row, k * size : (k + 1) * size] = vals_ref[row, k].T


def place_kernel(own_blocks, dom, cols_ref, _, place_ref):
    count, rows = cols_ref.shape
    for row in range(rows):
        for k in range(count):
            col = cols_ref[k, row] - lax.axis_index("rep") * (own_blocks * dom)
            owner = lax.div(col, jnp.int32(own_blocks)) ^ lax.axis_index("dom")
            side = jnp.where(owner > 1, 1 - (owner & 1), owner)
            place = (side * (dom // 2) + (owner >> 1)) * own_blocks
            place += lax.rem(col, jnp.int32(own_blocks))
            place_ref[row * count + k : row * count + k + 1, :] = jnp.full((1, 128), place, jnp.int32)


def join_kernel(*refs):
    pieces, out_ref = refs[:-1], refs[-1]
    first = 0
    for piece in pieces:
        out_ref[first : first + piece.shape[0]] = piece[...]
        first += piece.shape[0]


def wrap_kernel(ends_ref, *refs):
    out_ref = refs[-1]
    nodes = ends_ref.shape[0] // 2
    out_ref[:nodes] = ends_ref[:nodes]
    for at, piece in enumerate(refs[:-1], 1):
        out_ref[at * nodes : (at + 1) * nodes] = piece[...]
    out_ref[out_ref.shape[0] - nodes :] = ends_ref[nodes:]


def aggregate_kernel(rep, place_ref, vals_ref, mine_ref, far_ref, *outs):
    rows, count, size, _ = vals_ref.shape
    half = mine_ref.shape[0] // size
    share = rows // rep
    for j in range(rep - 1, -1, -1):
        target = lax.axis_index("rep") ^ j
        for i in range(share):
            row = target * share + i
            total = None
            for k in range(count):
                place = place_ref[row * count + k, 0]
                beyond = place >= half
                index = jnp.where(beyond, place - half, place)
                here = pl.ds(pl.multiple_of(index * size, size), size)
                block = jnp.where(beyond, far_ref[here, :], mine_ref[here, :])
                term = matmul(vals_ref[row, k], block, (1, 0))
                total = term if total is None else total + term
            outs[j][i * size : (i + 1) * size] = total.astype(outs[j].dtype)


def layer_kernel(
    rep, count, own_blocks, j, place_ref, flipped_ref, cotangent_ref, weight_ref, bias_ref, *refs
):
    first, last = j == 0, j == 2
    piece_ref, refs = refs[0], refs[1:]
    if not first:
        (_, sums_in), refs = refs[:2], refs[2:]
    output_ref, contrib, *refs = refs
    rows, _, size = flipped_ref.shape
    share = rows // rep
    quarter_blocks = contrib.shape[0]
    nodes = own_blocks * size
    if first:
        contrib[...] = jnp.zeros_like(contrib)

    target = lax.axis_index("rep") ^ j
    aggregated = piece_ref[...]
    part = aggregated.shape[0]
    here = pl.ds(pl.multiple_of(target * part, part), part)
    hidden = matmul(aggregated, weight_ref[...], (1, 0)) + bias_ref[...]
    gate_prob = jax.nn.sigmoid(hidden)
    output_ref[...] = (hidden * gate_prob).astype(BF16)
    grad_hidden = (
        cotangent_ref[here, :].astype(F32) * gate_prob * (1.0 + hidden * (1.0 - gate_prob))
    ).astype(BF16)
    part_sum = matmul(aggregated, grad_hidden, (0, 0))
    grad_agg = matmul(grad_hidden, weight_ref[...], (1, 1)).astype(BF16)
    for i in range(share):
        row = target * share + i
        terms = matmul(flipped_ref[row], grad_agg[i * size : (i + 1) * size], (1, 0))
        for k in range(count):
            contrib[place_ref[row * count + k, 0]] += terms[k * size : (k + 1) * size]
    if j == 0:
        refs[0][0] = part_sum
        refs[0][1] = jnp.zeros_like(part_sum)
    elif j == 3:
        refs[0][0] = sums_in[0]
        refs[0][1] = part_sum
    elif j == 1:
        refs[0][0] = sums_in[0] + part_sum
        refs[0][1] = sums_in[1]
    else:
        first_ref, rest_ref = refs
        away = contrib[quarter_blocks // 2 :].reshape(quarter_blocks // 2 * size, -1).astype(BF16)
        rest_ref[...] = away[:-nodes]
        first_ref[:nodes] = away[-nodes:]
        first_ref[nodes:] = (sums_in[0] + (sums_in[1] + part_sum)).astype(BF16)


def add_kernel(a_ref, b_ref, out_ref):
    out_ref[...] = (a_ref[...] + b_ref[...].astype(F32)).astype(out_ref.dtype)


def order_kernel(order, *refs):
    pieces, out_ref = refs[:-1], refs[-1]
    part = pieces[0].shape[0]
    for j, piece in zip(order, pieces):
        target = lax.axis_index("rep") ^ j
        out_ref[pl.ds(pl.multiple_of(target * part, part), part), :] = piece[...]


def first_pair_kernel(contrib_ref, sent_ref, got_ref, out_ref):
    blocks, size, _ = contrib_ref.shape
    nodes = out_ref.shape[0] - sent_ref.shape[1]
    last = contrib_ref[blocks // 2 - nodes // size : blocks // 2].reshape(nodes, -1)
    weight = (sent_ref[nodes:].astype(F32) + got_ref[nodes:].astype(F32)).astype(BF16)
    out_ref[:nodes] = (last + got_ref[:nodes].astype(F32)).astype(BF16)
    out_ref[nodes:] = weight


def rest_pair_kernel(contrib_ref, got_ref, first_ref, weight_ref, own_ref, *outs):
    size, nodes = contrib_ref.shape[1], own_ref.shape[0]
    weight_ref[...] = first_ref[nodes:]
    for chip, out_ref in enumerate([own_ref, *outs]):
        mine = contrib_ref[chip * nodes // size : (chip + 1) * nodes // size].reshape(nodes, -1)
        total = mine + got_ref[chip * nodes : (chip + 1) * nodes].astype(F32)
        out_ref[...] = total.astype(out_ref.dtype)


def total_of(values):
    while len(values) > 1:
        values = [a + b for a, b in zip(values[::2], values[1::2])]
    return values[0]


def lift_kernel(got_ref, out_ref):
    out_ref[...] = got_ref[...].astype(F32)


def early_sum_kernel(own_ref, lifted_ref, *refs):
    got, out_ref = refs[:-1], refs[-1]
    nodes = own_ref.shape[0]
    total = own_ref[...] + lifted_ref[:nodes]
    for g in got:
        total += g[...].astype(F32)
    out_ref[...] = total


def final_kernel(early_ref, lifted_ref, got_ref, *refs):
    weights, (feature_ref, weight_ref) = refs[:-2], refs[-2:]
    feature_ref[...] = early_ref[...] + got_ref[...].astype(F32)
    across = lifted_ref[feature_ref.shape[0] :]
    weight_ref[...] = total_of([w[...].astype(F32) for w in weights] + [across])


def shape(dims, dtype):
    return jax.ShapeDtypeStruct(dims, dtype)


def body(cols, vals, features, weight, bias, cotangent):
    rows, count, size, _ = vals.shape
    nodes, width = features.shape
    dom, rep = lax.axis_size("dom"), lax.axis_size("rep")
    chips = dom // 2
    own_blocks = nodes // size
    quarter_blocks = own_blocks * dom
    part = rows * size // rep
    params = pltpu.CompilerParams(vmem_limit_bytes=(8 + dom // 2) * 1024 * 1024)

    def call(kernel, out_shape, in_specs, aliases={}, cost=0):
        single = not isinstance(out_shape, list)
        return pl.pallas_call(
            kernel,
            out_shape=out_shape,
            in_specs=in_specs,
            out_specs=VMEM if single else [VMEM] * len(out_shape),
            input_output_aliases=aliases,
            compiler_params=params,
            cost_estimate=pl.CostEstimate(flops=cost, bytes_accessed=0, transcendentals=0),
        )

    flipped, own = call(
        early_kernel,
        [shape((rows, count * size, size), BF16), shape(features.shape, BF16)],
        [VMEM] * 2,
    )(vals, features)

    def join(*values):
        nodes_in = sum(v.shape[0] for v in values)
        return call(join_kernel, shape((nodes_in, width), BF16), [VMEM] * len(values))(*values)

    across = [swap(features, "dom", 2 * chip + 1) for chip in range(1, chips)]
    ends = join(own, across[-1])
    far_ends = swap(ends, "dom", 1)
    half = chips // 2 - 1
    beyond = [swap(piece, "dom", 1) for piece in across[half:-1]]
    beyond = [swap(piece, "dom", 1) for piece in across[:half]] + beyond

    def wrap(*values):
        return call(wrap_kernel, shape((chips * nodes, width), BF16), [VMEM] * (chips - 1))(*values)

    mine, far = wrap(ends, *across[:-1]), wrap(far_ends, *beyond)
    place = call(
        functools.partial(place_kernel, own_blocks, dom),
        shape((rows * count, 128), jnp.int32),
        [VMEM] * 2,
    )(cols.T, ends)

    partials = call(
        functools.partial(aggregate_kernel, rep),
        [shape((part, width), BF16 if j else F32) for j in range(rep)],
        [VMEM] * 4,
    )(place, vals, mine, far)
    arrived = {j: swap(partials[j], "rep", j) if j else partials[j] for j in range(rep)}
    order = [3, 1, 2]
    own_rows = arrived[0]
    for j in order:
        own_rows = call(add_kernel, shape((part, width), F32 if j != 2 else BF16), [VMEM] * 2)(
            own_rows, arrived[j]
        )
    pieces = {0: own_rows}
    for j in order:
        pieces[j] = swap(own_rows, "rep", j)

    outputs, carried = [], []
    for j, piece in pieces.items():
        outs = [shape((part, width), BF16), shape((quarter_blocks, size, width), F32)]
        if j != 2:
            outs += [shape((2, width, width), F32)]
        else:
            outs += [
                shape((nodes + width, width), BF16),
                shape(((chips - 1) * nodes, width), BF16),
            ]
        output, *carried = call(
            functools.partial(layer_kernel, rep, count, own_blocks, j),
            outs,
            [VMEM] * (6 + len(carried)),
            aliases={6: 1} if carried else {},
        )(place, flipped, cotangent, weight, bias.reshape(1, width), piece, *carried)
        outputs.append(output)
    contrib, first, rest = carried

    message = shape((nodes + width, width), BF16)
    got_first, got_rest = swap(first, "dom", 1), swap(rest, "dom", 1)
    first = call(first_pair_kernel, message, [VMEM] * 3, cost=5 * 10**9)(contrib, first, got_first)
    pair_weight, own, *rest = call(
        rest_pair_kernel,
        [shape((width, width), BF16), shape((nodes, width), F32)]
        + [shape((nodes, width), BF16)] * (chips - 2),
        [VMEM] * 3,
        cost=10**9,
    )(contrib, got_rest, first)
    last = chips - 1
    got = {last: swap(first, "dom", 2 * last + 1)}
    got |= {chip: swap(rest[chip - 1], "dom", 2 * chip + 1) for chip in range(last - 1, 0, -1)}
    weights = {chip: swap(pair_weight, "dom", 2 * chip + 1) for chip in range(last - 1, 0, -1)}
    weights[0] = pair_weight
    output = call(
        functools.partial(order_kernel, list(pieces)), shape((rows * size, width), BF16), [VMEM] * rep
    )(*outputs)
    lifted = call(lift_kernel, shape(message.shape, F32), [VMEM], cost=0)(got[last])
    early = call(early_sum_kernel, shape((nodes, width), F32), [VMEM] * last, cost=0)(
        own, lifted, *[got[chip] for chip in range(last - 1, 1, -1)]
    )
    feature_grad, weight_grad = call(
        final_kernel,
        [shape((nodes, width), F32), shape((width, width), F32)],
        [VMEM] * (chips + 2),
    )(early, lifted, got[1], *[weights[chip] for chip in range(last)])
    return output, feature_grad, weight_grad


def solution(mesh):
    placed = (
        P("dom", "rep"),
        P("dom", "rep", None, None),
        P(("rep", "dom"), None),
        P(),
        P(),
        P("dom", None),
    )
    return jax.shard_map(
        body,
        mesh=mesh,
        in_specs=placed,
        out_specs=(P("dom", None), P(("rep", "dom"), None), P()),
        check_vma=False,
    )
```

```python
import functools

import jax
import jax.numpy as jnp
from jax import lax
from jax.experimental import pallas as pl
from jax.experimental.pallas import tpu as pltpu
from jax.sharding import PartitionSpec as P

BF16 = jnp.bfloat16
F32 = jnp.float32
VMEM = pl.BlockSpec(memory_space=pltpu.VMEM)


def swap(value, axis, distance):
    size = lax.axis_size(axis)
    return lax.ppermute(value, axis, [(i, i ^ distance) for i in range(size)])


def matmul(a, b, contract):
    return lax.dot_general(a, b, ((contract[:1], contract[1:]), ((), ())), preferred_element_type=F32)


def early_kernel(vals_ref, features_ref, flipped_ref, own_ref, near_ref):
    rows, count, size, _ = vals_ref.shape
    near_ref[...] = vals_ref[...]
    own_ref[...] = features_ref[...]
    for row in range(rows):
        for k in range(count):
            flipped_ref[row, k * size : (k + 1) * size] = vals_ref[row, k].T


def place_kernel(own_blocks, dom, cols_ref, _, place_ref):
    count, rows = cols_ref.shape
    for row in range(rows):
        for k in range(count):
            col = cols_ref[k, row] - lax.axis_index("rep") * (own_blocks * dom)
            owner = lax.div(col, jnp.int32(own_blocks)) ^ lax.axis_index("dom")
            place = ((owner & 1) * (dom // 2) + (owner >> 1)) * own_blocks
            place += lax.rem(col, jnp.int32(own_blocks))
            place_ref[row * count + k : row * count + k + 1, :] = jnp.full((1, 128), place, jnp.int32)


def join_kernel(*refs):
    pieces, out_ref = refs[:-1], refs[-1]
    first = 0
    for piece in pieces:
        out_ref[first : first + piece.shape[0]] = piece[...]
        first += piece.shape[0]


def wrap_kernel(ends_ref, *refs):
    out_ref = refs[-1]
    nodes = ends_ref.shape[0] // 2
    out_ref[:nodes] = ends_ref[:nodes]
    for at, piece in enumerate(refs[:-1], 1):
        out_ref[at * nodes : (at + 1) * nodes] = piece[...]
    out_ref[out_ref.shape[0] - nodes :] = ends_ref[nodes:]


def aggregate_kernel(rep, place_ref, vals_ref, mine_ref, far_ref, *outs):
    rows, count, size, _ = vals_ref.shape
    half = mine_ref.shape[0] // size
    share = rows // rep
    for j in range(rep - 1, -1, -1):
        target = lax.axis_index("rep") ^ j
        for i in range(share):
            row = target * share + i
            total = None
            for k in range(count):
                place = place_ref[row * count + k, 0]
                beyond = place >= half
                index = jnp.where(beyond, place - half, place)
                here = pl.ds(pl.multiple_of(index * size, size), size)
                block = jnp.where(beyond, far_ref[here, :], mine_ref[here, :])
                term = matmul(vals_ref[row, k], block, (1, 0))
                total = term if total is None else total + term
            outs[j][i * size : (i + 1) * size] = total.astype(outs[j].dtype)


def layer_kernel(
    rep, count, own_blocks, j, place_ref, flipped_ref, cotangent_ref, weight_ref, bias_ref, *refs
):
    first, last = j == 0, j == 2
    piece_ref, refs = refs[0], refs[1:]
    if not first:
        (_, sums_in), refs = refs[:2], refs[2:]
    output_ref, contrib, *refs = refs
    rows, _, size = flipped_ref.shape
    share = rows // rep
    quarter_blocks = contrib.shape[0]
    nodes = own_blocks * size
    if first:
        contrib[...] = jnp.zeros_like(contrib)

    target = lax.axis_index("rep") ^ j
    aggregated = piece_ref[...]
    part = aggregated.shape[0]
    here = pl.ds(pl.multiple_of(target * part, part), part)
    hidden = matmul(aggregated, weight_ref[...], (1, 0)) + bias_ref[...]
    gate_prob = jax.nn.sigmoid(hidden)
    output_ref[...] = (hidden * gate_prob).astype(BF16)
    grad_hidden = (
        cotangent_ref[here, :].astype(F32) * gate_prob * (1.0 + hidden * (1.0 - gate_prob))
    ).astype(BF16)
    part_sum = matmul(aggregated, grad_hidden, (0, 0))
    grad_agg = matmul(grad_hidden, weight_ref[...], (1, 1)).astype(BF16)
    for i in range(share):
        row = target * share + i
        terms = matmul(flipped_ref[row], grad_agg[i * size : (i + 1) * size], (1, 0))
        for k in range(count):
            contrib[place_ref[row * count + k, 0]] += terms[k * size : (k + 1) * size]
    if j == 0:
        refs[0][0] = part_sum
        refs[0][1] = jnp.zeros_like(part_sum)
    elif j == 3:
        refs[0][0] = sums_in[0]
        refs[0][1] = part_sum
    elif j == 1:
        refs[0][0] = sums_in[0] + part_sum
        refs[0][1] = sums_in[1]
    else:
        first_ref, rest_ref = refs
        away = contrib[quarter_blocks // 2 :].reshape(quarter_blocks // 2 * size, -1).astype(BF16)
        rest_ref[...] = away[:-nodes]
        first_ref[:nodes] = away[-nodes:]
        first_ref[nodes:] = (sums_in[0] + (sums_in[1] + part_sum)).astype(BF16)


def add_kernel(a_ref, b_ref, out_ref):
    out_ref[...] = (a_ref[...] + b_ref[...].astype(F32)).astype(out_ref.dtype)


def order_kernel(order, *refs):
    pieces, out_ref = refs[:-1], refs[-1]
    part = pieces[0].shape[0]
    for j, piece in zip(order, pieces):
        target = lax.axis_index("rep") ^ j
        out_ref[pl.ds(pl.multiple_of(target * part, part), part), :] = piece[...]


def first_pair_kernel(contrib_ref, sent_ref, got_ref, out_ref):
    blocks, size, _ = contrib_ref.shape
    nodes = out_ref.shape[0] - sent_ref.shape[1]
    last = contrib_ref[blocks // 2 - nodes // size : blocks // 2].reshape(nodes, -1)
    weight = (sent_ref[nodes:].astype(F32) + got_ref[nodes:].astype(F32)).astype(BF16)
    out_ref[:nodes] = (last + got_ref[:nodes].astype(F32)).astype(BF16)
    out_ref[nodes:] = weight


def rest_pair_kernel(contrib_ref, got_ref, first_ref, weight_ref, own_ref, *outs):
    size, nodes = contrib_ref.shape[1], own_ref.shape[0]
    weight_ref[...] = first_ref[nodes:]
    for chip, out_ref in enumerate([own_ref, *outs]):
        mine = contrib_ref[chip * nodes // size : (chip + 1) * nodes // size].reshape(nodes, -1)
        total = mine + got_ref[chip * nodes : (chip + 1) * nodes].astype(F32)
        out_ref[...] = total.astype(out_ref.dtype)


def total_of(values):
    while len(values) > 1:
        values = [a + b for a, b in zip(values[::2], values[1::2])]
    return values[0]


def lift_kernel(got_ref, out_ref):
    out_ref[...] = got_ref[...].astype(F32)


def early_sum_kernel(own_ref, lifted_ref, *refs):
    got, out_ref = refs[:-1], refs[-1]
    nodes = own_ref.shape[0]
    total = own_ref[...] + lifted_ref[:nodes]
    for g in got:
        total += g[...].astype(F32)
    out_ref[...] = total


def final_kernel(early_ref, lifted_ref, got_ref, *refs):
    weights, (feature_ref, weight_ref) = refs[:-2], refs[-2:]
    feature_ref[...] = early_ref[...] + got_ref[...].astype(F32)
    across = lifted_ref[feature_ref.shape[0] :]
    weight_ref[...] = total_of([w[...].astype(F32) for w in weights] + [across])


def shape(dims, dtype):
    return jax.ShapeDtypeStruct(dims, dtype)


def body(cols, vals, features, weight, bias, cotangent):
    rows, count, size, _ = vals.shape
    nodes, width = features.shape
    dom, rep = lax.axis_size("dom"), lax.axis_size("rep")
    chips = dom // 2
    own_blocks = nodes // size
    quarter_blocks = own_blocks * dom
    part = rows * size // rep
    params = pltpu.CompilerParams(vmem_limit_bytes=(8 + dom // 2) * 1024 * 1024)

    def call(kernel, out_shape, in_specs, aliases={}, cost=0):
        single = not isinstance(out_shape, list)
        return pl.pallas_call(
            kernel,
            out_shape=out_shape,
            in_specs=in_specs,
            out_specs=VMEM if single else [VMEM] * len(out_shape),
            input_output_aliases=aliases,
            compiler_params=params,
            cost_estimate=pl.CostEstimate(flops=cost, bytes_accessed=0, transcendentals=0),
        )

    flipped, own, vals = call(
        early_kernel,
        [shape((rows, count * size, size), BF16), shape(features.shape, BF16), shape(vals.shape, BF16)],
        [VMEM] * 2,
    )(vals, features)

    def join(*values):
        nodes_in = sum(v.shape[0] for v in values)
        return call(join_kernel, shape((nodes_in, width), BF16), [VMEM] * len(values))(*values)

    across = [swap(features, "dom", 2 * chip) for chip in range(1, chips)]
    ends = join(own, across[-1])
    far_ends = swap(ends, "dom", 1)
    half = chips // 2 - 1
    beyond = [swap(piece, "dom", 1) for piece in across[half:-1]]
    beyond = [swap(piece, "dom", 1) for piece in across[:half]] + beyond

    def wrap(*values):
        return call(wrap_kernel, shape((chips * nodes, width), BF16), [VMEM] * (chips - 1))(*values)

    mine, far = wrap(ends, *across[:-1]), wrap(far_ends, *beyond)
    place = call(
        functools.partial(place_kernel, own_blocks, dom),
        shape((rows * count, 128), jnp.int32),
        [VMEM] * 2,
    )(cols.T, ends)

    partials = call(
        functools.partial(aggregate_kernel, rep),
        [shape((part, width), BF16 if j else F32) for j in range(rep)],
        [VMEM] * 4,
    )(place, vals, mine, far)
    arrived = {j: swap(partials[j], "rep", j) if j else partials[j] for j in range(rep)}
    order = [3, 1, 2]
    own_rows = arrived[0]
    for j in order:
        own_rows = call(add_kernel, shape((part, width), F32 if j != 2 else BF16), [VMEM] * 2)(
            own_rows, arrived[j]
        )
    pieces = {0: own_rows}
    for j in order:
        pieces[j] = swap(own_rows, "rep", j)

    outputs, carried = [], []
    for j, piece in pieces.items():
        outs = [shape((part, width), BF16), shape((quarter_blocks, size, width), F32)]
        if j != 2:
            outs += [shape((2, width, width), F32)]
        else:
            outs += [
                shape((nodes + width, width), BF16),
                shape(((chips - 1) * nodes, width), BF16),
            ]
        output, *carried = call(
            functools.partial(layer_kernel, rep, count, own_blocks, j),
            outs,
            [VMEM] * (6 + len(carried)),
            aliases={6: 1} if carried else {},
        )(place, flipped, cotangent, weight, bias.reshape(1, width), piece, *carried)
        outputs.append(output)
    contrib, first, rest = carried

    message = shape((nodes + width, width), BF16)
    got_first, got_rest = swap(first, "dom", 1), swap(rest, "dom", 1)
    first = call(first_pair_kernel, message, [VMEM] * 3, cost=5 * 10**9)(contrib, first, got_first)
    pair_weight, own, *rest = call(
        rest_pair_kernel,
        [shape((width, width), BF16), shape((nodes, width), F32)]
        + [shape((nodes, width), BF16)] * (chips - 2),
        [VMEM] * 3,
        cost=10**9,
    )(contrib, got_rest, first)
    last = chips - 1
    got = {last: swap(first, "dom", 2 * last)}
    got |= {chip: swap(rest[chip - 1], "dom", 2 * chip) for chip in range(last - 1, 0, -1)}
    weights = {chip: swap(pair_weight, "dom", 2 * chip) for chip in range(last - 1, 0, -1)}
    weights[0] = pair_weight
    output = call(
        functools.partial(order_kernel, list(pieces)), shape((rows * size, width), BF16), [VMEM] * rep
    )(*outputs)
    lifted = call(lift_kernel, shape(message.shape, F32), [VMEM], cost=0)(got[last])
    early = call(early_sum_kernel, shape((nodes, width), F32), [VMEM] * last, cost=0)(
        own, lifted, *[got[chip] for chip in range(last - 1, 1, -1)]
    )
    feature_grad, weight_grad = call(
        final_kernel,
        [shape((nodes, width), F32), shape((width, width), F32)],
        [VMEM] * (chips + 2),
    )(early, lifted, got[1], *[weights[chip] for chip in range(last)])
    return output, feature_grad, weight_grad


def solution(mesh):
    placed = (
        P("dom", "rep"),
        P("dom", "rep", None, None),
        P(("rep", "dom"), None),
        P(),
        P(),
        P("dom", None),
    )
    return jax.shard_map(
        body,
        mesh=mesh,
        in_specs=placed,
        out_specs=(P("dom", None), P(("rep", "dom"), None), P()),
        check_vma=False,
    )
```

```python
import functools

import jax
import jax.numpy as jnp
from jax import lax
from jax.experimental import pallas as pl
from jax.experimental.pallas import tpu as pltpu
from jax.sharding import PartitionSpec as P

BF16 = jnp.bfloat16
F32 = jnp.float32
VMEM = pl.BlockSpec(memory_space=pltpu.VMEM)


def swap(value, axis, distance):
    size = lax.axis_size(axis)
    return lax.ppermute(value, axis, [(i, i ^ distance) for i in range(size)])


def matmul(a, b, contract):
    return lax.dot_general(a, b, ((contract[:1], contract[1:]), ((), ())), preferred_element_type=F32)


def early_kernel(vals_ref, features_ref, flipped_ref, own_ref, near_ref):
    rows, count, size, _ = vals_ref.shape
    near_ref[...] = vals_ref[...]
    own_ref[...] = features_ref[...]
    for row in range(rows):
        for k in range(count):
            flipped_ref[row, k * size : (k + 1) * size] = vals_ref[row, k].T


def place_kernel(own_blocks, dom, cols_ref, _, place_ref):
    count, rows = cols_ref.shape
    for row in range(rows):
        for k in range(count):
            col = cols_ref[k, row] - lax.axis_index("rep") * (own_blocks * dom)
            owner = lax.div(col, jnp.int32(own_blocks)) ^ lax.axis_index("dom")
            side = jnp.where(owner > 1, 1 - (owner & 1), owner)
            place = (side * (dom // 2) + (owner >> 1)) * own_blocks
            place += lax.rem(col, jnp.int32(own_blocks))
            place_ref[row * count + k : row * count + k + 1, :] = jnp.full((1, 128), place, jnp.int32)


def join_kernel(*refs):
    pieces, out_ref = refs[:-1], refs[-1]
    first = 0
    for piece in pieces:
        out_ref[first : first + piece.shape[0]] = piece[...]
        first += piece.shape[0]


def wrap_kernel(ends_ref, *refs):
    out_ref = refs[-1]
    nodes = ends_ref.shape[0] // 2
    out_ref[:nodes] = ends_ref[:nodes]
    for at, piece in enumerate(refs[:-1], 1):
        out_ref[at * nodes : (at + 1) * nodes] = piece[...]
    out_ref[out_ref.shape[0] - nodes :] = ends_ref[nodes:]


def aggregate_kernel(rep, place_ref, vals_ref, mine_ref, far_ref, *outs):
    rows, count, size, _ = vals_ref.shape
    half = mine_ref.shape[0] // size
    share = rows // rep
    for j in range(rep - 1, -1, -1):
        target = lax.axis_index("rep") ^ j
        for i in range(share):
            row = target * share + i
            total = None
            for k in range(count):
                place = place_ref[row * count + k, 0]
                beyond = place >= half
                index = jnp.where(beyond, place - half, place)
                here = pl.ds(pl.multiple_of(index * size, size), size)
                block = jnp.where(beyond, far_ref[here, :], mine_ref[here, :])
                term = matmul(vals_ref[row, k], block, (1, 0))
                total = term if total is None else total + term
            outs[j][i * size : (i + 1) * size] = total.astype(outs[j].dtype)


def layer_kernel(
    rep, count, own_blocks, j, place_ref, flipped_ref, cotangent_ref, weight_ref, bias_ref, *refs
):
    first, last = j == 0, j == 2
    piece_ref, refs = refs[0], refs[1:]
    if not first:
        (_, sums_in), refs = refs[:2], refs[2:]
    output_ref, contrib, *refs = refs
    rows, _, size = flipped_ref.shape
    share = rows // rep
    quarter_blocks = contrib.shape[0]
    nodes = own_blocks * size
    if first:
        contrib[...] = jnp.zeros_like(contrib)

    target = lax.axis_index("rep") ^ j
    aggregated = piece_ref[...]
    part = aggregated.shape[0]
    here = pl.ds(pl.multiple_of(target * part, part), part)
    hidden = matmul(aggregated, weight_ref[...], (1, 0)) + bias_ref[...]
    gate_prob = jax.nn.sigmoid(hidden)
    output_ref[...] = (hidden * gate_prob).astype(BF16)
    grad_hidden = (
        cotangent_ref[here, :].astype(F32) * gate_prob * (1.0 + hidden * (1.0 - gate_prob))
    ).astype(BF16)
    part_sum = matmul(aggregated, grad_hidden, (0, 0))
    grad_agg = matmul(grad_hidden, weight_ref[...], (1, 1)).astype(BF16)
    for i in range(share):
        row = target * share + i
        terms = matmul(flipped_ref[row], grad_agg[i * size : (i + 1) * size], (1, 0))
        for k in range(count):
            contrib[place_ref[row * count + k, 0]] += terms[k * size : (k + 1) * size]
    if j == 0:
        refs[0][0] = part_sum
        refs[0][1] = jnp.zeros_like(part_sum)
    elif j == 3:
        refs[0][0] = sums_in[0]
        refs[0][1] = part_sum
    elif j == 1:
        refs[0][0] = sums_in[0] + part_sum
        refs[0][1] = sums_in[1]
    else:
        across_ref, beside_ref = refs
        half = quarter_blocks // 2
        rest = quarter_blocks * size // 2 - nodes
        weight = (sums_in[0] + (sums_in[1] + part_sum)).astype(BF16)
        across_ref[:nodes] = contrib[half - own_blocks : half].reshape(nodes, -1).astype(BF16)
        across_ref[2 * nodes :] = weight
        beside_ref[rest:] = weight
        away = contrib[half:].reshape(half * size, -1).astype(BF16)
        across_ref[nodes : 2 * nodes] = away[rest:]
        beside_ref[:rest] = away[:rest]


def add_kernel(a_ref, b_ref, out_ref):
    out_ref[...] = (a_ref[...] + b_ref[...].astype(F32)).astype(out_ref.dtype)


def order_kernel(order, *refs):
    pieces, out_ref = refs[:-1], refs[-1]
    part = pieces[0].shape[0]
    for j, piece in zip(order, pieces):
        target = lax.axis_index("rep") ^ j
        out_ref[pl.ds(pl.multiple_of(target * part, part), part), :] = piece[...]


def pair_kernel(contrib_ref, sent_ref, got_ref, own_ref, *outs):
    size, nodes = contrib_ref.shape[1], own_ref.shape[0]
    rest = nodes * len(outs)
    weight = (sent_ref[rest:].astype(F32) + got_ref[rest:].astype(F32)).astype(BF16)
    for chip in range(len(outs)):
        mine = contrib_ref[chip * nodes // size : (chip + 1) * nodes // size].reshape(nodes, -1)
        total = mine + got_ref[chip * nodes : (chip + 1) * nodes].astype(F32)
        if chip == 0:
            own_ref[...] = total
        else:
            outs[chip - 1][:nodes] = total.astype(BF16)
            outs[chip - 1][nodes:] = weight
    outs[-1][...] = weight


def pass_kernel(got_ref, out_ref):
    out_ref[...] = got_ref[got_ref.shape[0] - out_ref.shape[0] :]


def total_of(values):
    while len(values) > 1:
        values = [a + b for a, b in zip(values[::2], values[1::2])]
    return values[0]


def early_sum_kernel(own_ref, across_ref, *refs):
    got, out_ref = refs[:-1], refs[-1]
    nodes = own_ref.shape[0]
    total = own_ref[...] + across_ref[:nodes].astype(F32)
    for g in got:
        total += g[:nodes].astype(F32)
    out_ref[...] = total


def final_kernel(early_ref, weight_ref, across_ref, passed_ref, *refs):
    got, (feature_ref, grad_ref) = refs[:-2], refs[-2:]
    nodes = feature_ref.shape[0]
    feature_ref[...] = early_ref[...] + passed_ref[:nodes].astype(F32)
    weights = [weight_ref[...].astype(F32)] + [g[nodes:].astype(F32) for g in got]
    across = across_ref[2 * nodes :].astype(F32) + passed_ref[nodes:].astype(F32)
    grad_ref[...] = total_of(weights + [across.astype(BF16).astype(F32)])


def shape(dims, dtype):
    return jax.ShapeDtypeStruct(dims, dtype)


def body(cols, vals, features, weight, bias, cotangent):
    rows, count, size, _ = vals.shape
    nodes, width = features.shape
    dom, rep = lax.axis_size("dom"), lax.axis_size("rep")
    chips = dom // 2
    own_blocks = nodes // size
    quarter_blocks = own_blocks * dom
    part = rows * size // rep
    params = pltpu.CompilerParams(vmem_limit_bytes=(8 + dom // 2) * 1024 * 1024)

    def call(kernel, out_shape, in_specs, aliases={}, cost=0):
        single = not isinstance(out_shape, list)
        return pl.pallas_call(
            kernel,
            out_shape=out_shape,
            in_specs=in_specs,
            out_specs=VMEM if single else [VMEM] * len(out_shape),
            input_output_aliases=aliases,
            compiler_params=params,
            cost_estimate=pl.CostEstimate(flops=cost, bytes_accessed=0, transcendentals=0),
        )

    flipped, own, vals = call(
        early_kernel,
        [shape((rows, count * size, size), BF16), shape(features.shape, BF16), shape(vals.shape, BF16)],
        [VMEM] * 2,
    )(vals, features)

    def join(*values):
        nodes_in = sum(v.shape[0] for v in values)
        return call(join_kernel, shape((nodes_in, width), BF16), [VMEM] * len(values))(*values)

    across = [swap(features, "dom", 2 * chip + 1) for chip in range(1, chips)]
    ends = join(own, across[-1])
    far_ends = swap(ends, "dom", 1)
    half = chips // 2 - 1
    beyond = [swap(piece, "dom", 1) for piece in across[half:-1]]
    beyond = [swap(piece, "dom", 1) for piece in across[:half]] + beyond

    def wrap(*values):
        return call(wrap_kernel, shape((chips * nodes, width), BF16), [VMEM] * (chips - 1))(*values)

    mine, far = wrap(ends, *across[:-1]), wrap(far_ends, *beyond)
    place = call(
        functools.partial(place_kernel, own_blocks, dom),
        shape((rows * count, 128), jnp.int32),
        [VMEM] * 2,
    )(cols.T, ends)

    partials = call(
        functools.partial(aggregate_kernel, rep),
        [shape((part, width), BF16 if j else F32) for j in range(rep)],
        [VMEM] * 4,
    )(place, vals, mine, far)
    arrived = {j: swap(partials[j], "rep", j) if j else partials[j] for j in range(rep)}
    order = [3, 1, 2]
    own_rows = arrived[0]
    for j in order:
        own_rows = call(add_kernel, shape((part, width), F32 if j != 2 else BF16), [VMEM] * 2)(
            own_rows, arrived[j]
        )
    pieces = {0: own_rows}
    for j in order:
        pieces[j] = swap(own_rows, "rep", j)

    outputs, carried = [], []
    for j, piece in pieces.items():
        outs = [shape((part, width), BF16), shape((quarter_blocks, size, width), F32)]
        if j != 2:
            outs += [shape((2, width, width), F32)]
        else:
            outs += [
                shape((2 * nodes + width, width), BF16),
                shape(((chips - 1) * nodes + width, width), BF16),
            ]
        output, *carried = call(
            functools.partial(layer_kernel, rep, count, own_blocks, j),
            outs,
            [VMEM] * (6 + len(carried)),
            aliases={6: 1} if carried else {},
        )(place, flipped, cotangent, weight, bias.reshape(1, width), piece, *carried)
        outputs.append(output)
    contrib, across, beside = carried

    last = chips - 1
    message = shape((nodes + width, width), BF16)
    got_across = swap(across, "dom", 2 * last + 1)
    own, *sends, pair_weight = call(
        pair_kernel,
        [shape((nodes, width), F32)] + [message] * (last - 1) + [shape((width, width), BF16)],
        [VMEM] * 3,
    )(contrib, beside, swap(beside, "dom", 1))
    got = {chip: swap(sends[chip - 1], "dom", 2 * chip + 1) for chip in range(last - 1, 0, -1)}
    passed = swap(call(pass_kernel, message, [VMEM])(got_across), "dom", 1)
    output = call(
        functools.partial(order_kernel, list(pieces)), shape((rows * size, width), BF16), [VMEM] * rep
    )(*outputs)
    early = call(early_sum_kernel, shape((nodes, width), F32), [VMEM] * chips)(
        own, got_across, *[got[chip] for chip in range(last - 1, 0, -1)]
    )
    feature_grad, weight_grad = call(
        final_kernel,
        [shape((nodes, width), F32), shape((width, width), F32)],
        [VMEM] * (chips + 2),
    )(early, pair_weight, got_across, passed, *[got[chip] for chip in range(1, last)])
    return output, feature_grad, weight_grad


def solution(mesh):
    placed = (
        P("dom", "rep"),
        P("dom", "rep", None, None),
        P(("rep", "dom"), None),
        P(),
        P(),
        P("dom", None),
    )
    return jax.shard_map(
        body,
        mesh=mesh,
        in_specs=placed,
        out_specs=(P("dom", None), P(("rep", "dom"), None), P()),
        check_vma=False,
    )
```

```python
import functools

import jax
import jax.numpy as jnp
from jax import lax
from jax.experimental import pallas as pl
from jax.experimental.pallas import tpu as pltpu
from jax.sharding import PartitionSpec as P

BF16 = jnp.bfloat16
F32 = jnp.float32
VMEM = pl.BlockSpec(memory_space=pltpu.VMEM)


def swap(value, axis, distance):
    size = lax.axis_size(axis)
    return lax.ppermute(value, axis, [(i, i ^ distance) for i in range(size)])


def matmul(a, b, contract):
    return lax.dot_general(a, b, ((contract[:1], contract[1:]), ((), ())), preferred_element_type=F32)


def early_kernel(vals_ref, features_ref, flipped_ref, own_ref, near_ref):
    rows, count, size, _ = vals_ref.shape
    near_ref[...] = vals_ref[...]
    own_ref[...] = features_ref[...]
    for row in range(rows):
        for k in range(count):
            flipped_ref[row, k * size : (k + 1) * size] = vals_ref[row, k].T


def place_kernel(own_blocks, dom, cols_ref, _, place_ref):
    count, rows = cols_ref.shape
    for row in range(rows):
        for k in range(count):
            col = cols_ref[k, row] - lax.axis_index("rep") * (own_blocks * dom)
            owner = lax.div(col, jnp.int32(own_blocks)) ^ lax.axis_index("dom")
            side = jnp.where(owner > 1, 1 - (owner & 1), owner)
            place = (side * (dom // 2) + (owner >> 1)) * own_blocks
            place += lax.rem(col, jnp.int32(own_blocks))
            place_ref[row * count + k : row * count + k + 1, :] = jnp.full((1, 128), place, jnp.int32)


def join_kernel(*refs):
    pieces, out_ref = refs[:-1], refs[-1]
    first = 0
    for piece in pieces:
        out_ref[first : first + piece.shape[0]] = piece[...]
        first += piece.shape[0]


def wrap_kernel(ends_ref, *refs):
    out_ref = refs[-1]
    nodes = ends_ref.shape[0] // 2
    out_ref[:nodes] = ends_ref[:nodes]
    for at, piece in enumerate(refs[:-1], 1):
        out_ref[at * nodes : (at + 1) * nodes] = piece[...]
    out_ref[out_ref.shape[0] - nodes :] = ends_ref[nodes:]


def aggregate_kernel(rep, place_ref, vals_ref, mine_ref, far_ref, *outs):
    rows, count, size, _ = vals_ref.shape
    half = mine_ref.shape[0] // size
    share = rows // rep
    for j in range(rep - 1, -1, -1):
        target = lax.axis_index("rep") ^ j
        for i in range(share):
            row = target * share + i
            total = None
            for k in range(count):
                place = place_ref[row * count + k, 0]
                beyond = place >= half
                index = jnp.where(beyond, place - half, place)
                here = pl.ds(pl.multiple_of(index * size, size), size)
                block = jnp.where(beyond, far_ref[here, :], mine_ref[here, :])
                term = matmul(vals_ref[row, k], block, (1, 0))
                total = term if total is None else total + term
            outs[j][i * size : (i + 1) * size] = total.astype(outs[j].dtype)


def layer_kernel(
    rep, count, own_blocks, j, place_ref, flipped_ref, cotangent_ref, weight_ref, bias_ref, *refs
):
    first, last = j == 0, j == 2
    piece_ref, refs = refs[0], refs[1:]
    if not first:
        (_, sums_in), refs = refs[:2], refs[2:]
    output_ref, contrib, *refs = refs
    rows, _, size = flipped_ref.shape
    share = rows // rep
    quarter_blocks = contrib.shape[0]
    nodes = own_blocks * size
    if first:
        contrib[...] = jnp.zeros_like(contrib)

    target = lax.axis_index("rep") ^ j
    aggregated = piece_ref[...]
    part = aggregated.shape[0]
    here = pl.ds(pl.multiple_of(target * part, part), part)
    hidden = matmul(aggregated, weight_ref[...], (1, 0)) + bias_ref[...]
    gate_prob = jax.nn.sigmoid(hidden)
    output_ref[...] = (hidden * gate_prob).astype(BF16)
    grad_hidden = (
        cotangent_ref[here, :].astype(F32) * gate_prob * (1.0 + hidden * (1.0 - gate_prob))
    ).astype(BF16)
    part_sum = matmul(aggregated, grad_hidden, (0, 0))
    grad_agg = matmul(grad_hidden, weight_ref[...], (1, 1)).astype(BF16)
    for i in range(share):
        row = target * share + i
        terms = matmul(flipped_ref[row], grad_agg[i * size : (i + 1) * size], (1, 0))
        for k in range(count):
            contrib[place_ref[row * count + k, 0]] += terms[k * size : (k + 1) * size]
    if j == 0:
        refs[0][0] = part_sum
        refs[0][1] = jnp.zeros_like(part_sum)
    elif j == 3:
        refs[0][0] = sums_in[0]
        refs[0][1] = part_sum
    elif j == 1:
        refs[0][0] = sums_in[0] + part_sum
        refs[0][1] = sums_in[1]
    else:
        across_ref, beside_ref, others_ref = refs
        half = quarter_blocks // 2
        rest = quarter_blocks * size // 2 - nodes
        weight = (sums_in[0] + (sums_in[1] + part_sum)).astype(BF16)
        away = contrib[half:].reshape(half * size, -1).astype(BF16)
        across_ref[:nodes] = away[rest:]
        across_ref[nodes : 2 * nodes] = contrib[half - own_blocks : half].reshape(nodes, -1).astype(BF16)
        across_ref[2 * nodes :] = weight
        beside_ref[:nodes] = away[:nodes]
        beside_ref[nodes:] = weight
        others_ref[...] = away[nodes:rest]


def add_kernel(a_ref, b_ref, out_ref):
    out_ref[...] = (a_ref[...] + b_ref[...].astype(F32)).astype(out_ref.dtype)


def order_kernel(order, *refs):
    pieces, out_ref = refs[:-1], refs[-1]
    part = pieces[0].shape[0]
    for j, piece in zip(order, pieces):
        target = lax.axis_index("rep") ^ j
        out_ref[pl.ds(pl.multiple_of(target * part, part), part), :] = piece[...]


def pair_kernel(contrib_ref, sent_ref, got_ref, others_ref, own_ref, *outs):
    size, nodes = contrib_ref.shape[1], own_ref.shape[0]
    weight = (sent_ref[nodes:].astype(F32) + got_ref[nodes:].astype(F32)).astype(BF16)
    own_ref[...] = contrib_ref[: nodes // size].reshape(nodes, -1) + got_ref[:nodes].astype(F32)
    for chip in range(1, len(outs)):
        mine = contrib_ref[chip * nodes // size : (chip + 1) * nodes // size].reshape(nodes, -1)
        total = mine + others_ref[(chip - 1) * nodes : chip * nodes].astype(F32)
        outs[chip - 1][:nodes] = total.astype(BF16)
        outs[chip - 1][nodes:] = weight
    outs[-1][...] = weight


def pass_kernel(got_ref, out_ref):
    out_ref[...] = got_ref[got_ref.shape[0] - out_ref.shape[0] :]


def total_of(values):
    while len(values) > 1:
        values = [a + b for a, b in zip(values[::2], values[1::2])]
    return values[0]


def early_sum_kernel(own_ref, across_ref, *refs):
    got, out_ref = refs[:-1], refs[-1]
    nodes = own_ref.shape[0]
    total = own_ref[...] + across_ref[:nodes].astype(F32)
    for g in got:
        total += g[:nodes].astype(F32)
    out_ref[...] = total


def final_kernel(early_ref, weight_ref, across_ref, passed_ref, *refs):
    got, (feature_ref, grad_ref) = refs[:-2], refs[-2:]
    nodes = feature_ref.shape[0]
    feature_ref[...] = early_ref[...] + passed_ref[:nodes].astype(F32)
    weights = [weight_ref[...].astype(F32)] + [g[nodes:].astype(F32) for g in got]
    across = across_ref[2 * nodes :].astype(F32) + passed_ref[nodes:].astype(F32)
    grad_ref[...] = total_of(weights + [across.astype(BF16).astype(F32)])


def shape(dims, dtype):
    return jax.ShapeDtypeStruct(dims, dtype)


def body(cols, vals, features, weight, bias, cotangent):
    rows, count, size, _ = vals.shape
    nodes, width = features.shape
    dom, rep = lax.axis_size("dom"), lax.axis_size("rep")
    chips = dom // 2
    own_blocks = nodes // size
    quarter_blocks = own_blocks * dom
    part = rows * size // rep
    params = pltpu.CompilerParams(vmem_limit_bytes=(8 + dom // 2) * 1024 * 1024)

    def call(kernel, out_shape, in_specs, aliases={}, cost=0):
        single = not isinstance(out_shape, list)
        return pl.pallas_call(
            kernel,
            out_shape=out_shape,
            in_specs=in_specs,
            out_specs=VMEM if single else [VMEM] * len(out_shape),
            input_output_aliases=aliases,
            compiler_params=params,
            cost_estimate=pl.CostEstimate(flops=cost, bytes_accessed=0, transcendentals=0),
        )

    flipped, own, vals = call(
        early_kernel,
        [shape((rows, count * size, size), BF16), shape(features.shape, BF16), shape(vals.shape, BF16)],
        [VMEM] * 2,
    )(vals, features)

    def join(*values):
        nodes_in = sum(v.shape[0] for v in values)
        return call(join_kernel, shape((nodes_in, width), BF16), [VMEM] * len(values))(*values)

    across = [swap(features, "dom", 2 * chip + 1) for chip in range(1, chips)]
    ends = join(own, across[-1])
    far_ends = swap(ends, "dom", 1)
    half = chips // 2 - 1
    beyond = [swap(piece, "dom", 1) for piece in across[half:-1]]
    beyond = [swap(piece, "dom", 1) for piece in across[:half]] + beyond

    def wrap(*values):
        return call(wrap_kernel, shape((chips * nodes, width), BF16), [VMEM] * (chips - 1))(*values)

    mine, far = wrap(ends, *across[:-1]), wrap(far_ends, *beyond)
    place = call(
        functools.partial(place_kernel, own_blocks, dom),
        shape((rows * count, 128), jnp.int32),
        [VMEM] * 2,
    )(cols.T, ends)

    partials = call(
        functools.partial(aggregate_kernel, rep),
        [shape((part, width), BF16 if j else F32) for j in range(rep)],
        [VMEM] * 4,
    )(place, vals, mine, far)
    arrived = {j: swap(partials[j], "rep", j) if j else partials[j] for j in range(rep)}
    order = [3, 1, 2]
    own_rows = arrived[0]
    for j in order:
        own_rows = call(add_kernel, shape((part, width), F32 if j != 2 else BF16), [VMEM] * 2)(
            own_rows, arrived[j]
        )
    pieces = {0: own_rows}
    for j in order:
        pieces[j] = swap(own_rows, "rep", j)

    outputs, carried = [], []
    for j, piece in pieces.items():
        outs = [shape((part, width), BF16), shape((quarter_blocks, size, width), F32)]
        if j != 2:
            outs += [shape((2, width, width), F32)]
        else:
            outs += [
                shape((2 * nodes + width, width), BF16),
                shape((nodes + width, width), BF16),
                shape(((chips - 2) * nodes, width), BF16),
            ]
        output, *carried = call(
            functools.partial(layer_kernel, rep, count, own_blocks, j),
            outs,
            [VMEM] * (6 + len(carried)),
            aliases={6: 1} if carried else {},
        )(place, flipped, cotangent, weight, bias.reshape(1, width), piece, *carried)
        outputs.append(output)
    contrib, across, beside, others = carried

    last = chips - 1
    message = shape((nodes + width, width), BF16)
    got_across = swap(across, "dom", 2 * last)
    own, *sends, pair_weight = call(
        pair_kernel,
        [shape((nodes, width), F32)] + [message] * (last - 1) + [shape((width, width), BF16)],
        [VMEM] * 4,
    )(contrib, beside, swap(beside, "dom", 1), swap(others, "dom", 1))
    got = {chip: swap(sends[chip - 1], "dom", 2 * chip + 1) for chip in range(last - 1, 0, -1)}
    passed = swap(call(pass_kernel, message, [VMEM])(got_across), "dom", 1)
    output = call(
        functools.partial(order_kernel, list(pieces)), shape((rows * size, width), BF16), [VMEM] * rep
    )(*outputs)
    early = call(early_sum_kernel, shape((nodes, width), F32), [VMEM] * chips)(
        own, got_across, *[got[chip] for chip in range(last - 1, 0, -1)]
    )
    feature_grad, weight_grad = call(
        final_kernel,
        [shape((nodes, width), F32), shape((width, width), F32)],
        [VMEM] * (chips + 2),
    )(early, pair_weight, got_across, passed, *[got[chip] for chip in range(1, last)])
    return output, feature_grad, weight_grad


def solution(mesh):
    placed = (
        P("dom", "rep"),
        P("dom", "rep", None, None),
        P(("rep", "dom"), None),
        P(),
        P(),
        P("dom", None),
    )
    return jax.shard_map(
        body,
        mesh=mesh,
        in_specs=placed,
        out_specs=(P("dom", None), P(("rep", "dom"), None), P()),
        check_vma=False,
    )
```

```python
import functools

import jax
import jax.numpy as jnp
from jax import lax
from jax.experimental import pallas as pl
from jax.experimental.pallas import tpu as pltpu
from jax.sharding import PartitionSpec as P

BF16 = jnp.bfloat16
F32 = jnp.float32
VMEM = pl.BlockSpec(memory_space=pltpu.VMEM)


def swap(value, axis, distance):
    size = lax.axis_size(axis)
    return lax.ppermute(value, axis, [(i, i ^ distance) for i in range(size)])


def swap_some(value, distance, core):
    pairs = [(i, i ^ distance) for i in range(lax.axis_size("dom")) if i % 2 == core]
    return lax.ppermute(value, "dom", pairs)


def matmul(a, b, contract):
    return lax.dot_general(a, b, ((contract[:1], contract[1:]), ((), ())), preferred_element_type=F32)


def early_kernel(vals_ref, features_ref, flipped_ref, own_ref, near_ref):
    rows, count, size, _ = vals_ref.shape
    near_ref[...] = vals_ref[...]
    own_ref[...] = features_ref[...]
    for row in range(rows):
        for k in range(count):
            flipped_ref[row, k * size : (k + 1) * size] = vals_ref[row, k].T


def place_kernel(own_blocks, dom, cols_ref, _, place_ref):
    count, rows = cols_ref.shape
    for row in range(rows):
        for k in range(count):
            col = cols_ref[k, row] - lax.axis_index("rep") * (own_blocks * dom)
            owner = lax.div(col, jnp.int32(own_blocks)) ^ lax.axis_index("dom")
            side = jnp.where(owner > 1, 1 - (owner & 1), owner)
            place = (side * (dom // 2) + (owner >> 1)) * own_blocks
            place += lax.rem(col, jnp.int32(own_blocks))
            place_ref[row * count + k : row * count + k + 1, :] = jnp.full((1, 128), place, jnp.int32)


def join_kernel(*refs):
    pieces, out_ref = refs[:-1], refs[-1]
    first = 0
    for piece in pieces:
        out_ref[first : first + piece.shape[0]] = piece[...]
        first += piece.shape[0]


def wrap_kernel(ends_ref, *refs):
    out_ref = refs[-1]
    nodes = ends_ref.shape[0] // 2
    out_ref[:nodes] = ends_ref[:nodes]
    for at, piece in enumerate(refs[:-1], 1):
        out_ref[at * nodes : (at + 1) * nodes] = piece[...]
    out_ref[out_ref.shape[0] - nodes :] = ends_ref[nodes:]


def aggregate_kernel(rep, place_ref, vals_ref, mine_ref, far_ref, *outs):
    rows, count, size, _ = vals_ref.shape
    half = mine_ref.shape[0] // size
    share = rows // rep
    for j in range(rep - 1, -1, -1):
        target = lax.axis_index("rep") ^ j
        for i in range(share):
            row = target * share + i
            total = None
            for k in range(count):
                place = place_ref[row * count + k, 0]
                beyond = place >= half
                index = jnp.where(beyond, place - half, place)
                here = pl.ds(pl.multiple_of(index * size, size), size)
                block = jnp.where(beyond, far_ref[here, :], mine_ref[here, :])
                term = matmul(vals_ref[row, k], block, (1, 0))
                total = term if total is None else total + term
            outs[j][i * size : (i + 1) * size] = total.astype(outs[j].dtype)


def layer_kernel(
    rep, count, own_blocks, j, place_ref, flipped_ref, cotangent_ref, weight_ref, bias_ref, *refs
):
    first, last = j == 0, j == 2
    piece_ref, refs = refs[0], refs[1:]
    if not first:
        (_, sums_in), refs = refs[:2], refs[2:]
    output_ref, contrib, *refs = refs
    rows, _, size = flipped_ref.shape
    share = rows // rep
    quarter_blocks = contrib.shape[0]
    nodes = own_blocks * size
    if first:
        contrib[...] = jnp.zeros_like(contrib)

    target = lax.axis_index("rep") ^ j
    aggregated = piece_ref[...]
    part = aggregated.shape[0]
    here = pl.ds(pl.multiple_of(target * part, part), part)
    hidden = matmul(aggregated, weight_ref[...], (1, 0)) + bias_ref[...]
    gate_prob = jax.nn.sigmoid(hidden)
    output_ref[...] = (hidden * gate_prob).astype(BF16)
    grad_hidden = (
        cotangent_ref[here, :].astype(F32) * gate_prob * (1.0 + hidden * (1.0 - gate_prob))
    ).astype(BF16)
    part_sum = matmul(aggregated, grad_hidden, (0, 0))
    grad_agg = matmul(grad_hidden, weight_ref[...], (1, 1)).astype(BF16)
    for i in range(share):
        row = target * share + i
        terms = matmul(flipped_ref[row], grad_agg[i * size : (i + 1) * size], (1, 0))
        for k in range(count):
            contrib[place_ref[row * count + k, 0]] += terms[k * size : (k + 1) * size]
    if j == 0:
        refs[0][0] = part_sum
        refs[0][1] = jnp.zeros_like(part_sum)
    elif j == 3:
        refs[0][0] = sums_in[0]
        refs[0][1] = part_sum
    elif j == 1:
        refs[0][0] = sums_in[0] + part_sum
        refs[0][1] = sums_in[1]
    else:
        across_ref, beside_ref, others_ref = refs
        half = quarter_blocks // 2
        rest = quarter_blocks * size // 2 - nodes
        weight = (sums_in[0] + (sums_in[1] + part_sum)).astype(BF16)
        away = contrib[half:].reshape(half * size, -1).astype(BF16)
        across_ref[:nodes] = away[rest:]
        across_ref[nodes : 2 * nodes] = contrib[half - own_blocks : half].reshape(nodes, -1).astype(BF16)
        across_ref[2 * nodes :] = weight
        beside_ref[:nodes] = away[:nodes]
        beside_ref[nodes:] = weight
        others_ref[...] = away[nodes:rest]


def add_kernel(a_ref, b_ref, out_ref):
    out_ref[...] = (a_ref[...] + b_ref[...].astype(F32)).astype(out_ref.dtype)


def order_kernel(order, *refs):
    pieces, out_ref = refs[:-1], refs[-1]
    part = pieces[0].shape[0]
    for j, piece in zip(order, pieces):
        target = lax.axis_index("rep") ^ j
        out_ref[pl.ds(pl.multiple_of(target * part, part), part), :] = piece[...]


def pair_kernel(contrib_ref, sent_ref, got_ref, others_ref, own_ref, *outs):
    size, nodes = contrib_ref.shape[1], own_ref.shape[0]
    weight = (sent_ref[nodes:].astype(F32) + got_ref[nodes:].astype(F32)).astype(BF16)
    own_ref[...] = contrib_ref[: nodes // size].reshape(nodes, -1) + got_ref[:nodes].astype(F32)
    for chip in range(1, len(outs)):
        mine = contrib_ref[chip * nodes // size : (chip + 1) * nodes // size].reshape(nodes, -1)
        total = mine + others_ref[(chip - 1) * nodes : chip * nodes].astype(F32)
        outs[chip - 1][:nodes] = total.astype(BF16)
        outs[chip - 1][nodes:] = weight
    outs[-1][...] = weight


def copy_kernel(value_ref, out_ref):
    out_ref[...] = value_ref[...]


def pass_kernel(odd_ref, even_ref, across_ref, out_ref):
    across = odd_ref[...] + even_ref[...]
    across_ref[...] = across
    out_ref[...] = across[across.shape[0] - out_ref.shape[0] :]


def total_of(values):
    while len(values) > 1:
        values = [a + b for a, b in zip(values[::2], values[1::2])]
    return values[0]


def early_sum_kernel(own_ref, across_ref, *refs):
    got, out_ref = refs[:-1], refs[-1]
    nodes = own_ref.shape[0]
    total = own_ref[...] + across_ref[:nodes].astype(F32)
    for g in got:
        total += g[:nodes].astype(F32)
    out_ref[...] = total


def final_kernel(early_ref, weight_ref, across_ref, passed_ref, *refs):
    got, (feature_ref, grad_ref) = refs[:-2], refs[-2:]
    nodes = feature_ref.shape[0]
    feature_ref[...] = early_ref[...] + passed_ref[:nodes].astype(F32)
    weights = [weight_ref[...].astype(F32)] + [g[nodes:].astype(F32) for g in got]
    across = across_ref[2 * nodes :].astype(F32) + passed_ref[nodes:].astype(F32)
    grad_ref[...] = total_of(weights + [across.astype(BF16).astype(F32)])


def shape(dims, dtype):
    return jax.ShapeDtypeStruct(dims, dtype)


def body(cols, vals, features, weight, bias, cotangent):
    rows, count, size, _ = vals.shape
    nodes, width = features.shape
    dom, rep = lax.axis_size("dom"), lax.axis_size("rep")
    chips = dom // 2
    own_blocks = nodes // size
    quarter_blocks = own_blocks * dom
    part = rows * size // rep
    params = pltpu.CompilerParams(vmem_limit_bytes=(8 + dom // 2) * 1024 * 1024)

    def call(kernel, out_shape, in_specs, aliases={}, cost=0):
        single = not isinstance(out_shape, list)
        return pl.pallas_call(
            kernel,
            out_shape=out_shape,
            in_specs=in_specs,
            out_specs=VMEM if single else [VMEM] * len(out_shape),
            input_output_aliases=aliases,
            compiler_params=params,
            cost_estimate=pl.CostEstimate(flops=cost, bytes_accessed=0, transcendentals=0),
        )

    flipped, own, vals = call(
        early_kernel,
        [shape((rows, count * size, size), BF16), shape(features.shape, BF16), shape(vals.shape, BF16)],
        [VMEM] * 2,
    )(vals, features)

    def join(*values):
        nodes_in = sum(v.shape[0] for v in values)
        return call(join_kernel, shape((nodes_in, width), BF16), [VMEM] * len(values))(*values)

    across = [swap(features, "dom", 2 * chip + 1) for chip in range(1, chips)]
    ends = join(own, across[-1])
    far_ends = swap(ends, "dom", 1)
    half = chips // 2 - 1
    beyond = [swap(piece, "dom", 1) for piece in across[half:-1]]
    beyond = [swap(piece, "dom", 1) for piece in across[:half]] + beyond

    def wrap(*values):
        return call(wrap_kernel, shape((chips * nodes, width), BF16), [VMEM] * (chips - 1))(*values)

    mine, far = wrap(ends, *across[:-1]), wrap(far_ends, *beyond)
    place = call(
        functools.partial(place_kernel, own_blocks, dom),
        shape((rows * count, 128), jnp.int32),
        [VMEM] * 2,
    )(cols.T, ends)

    partials = call(
        functools.partial(aggregate_kernel, rep),
        [shape((part, width), BF16 if j else F32) for j in range(rep)],
        [VMEM] * 4,
    )(place, vals, mine, far)
    arrived = {j: swap(partials[j], "rep", j) if j else partials[j] for j in range(rep)}
    order = [3, 1, 2]
    own_rows = arrived[0]
    for j in order:
        own_rows = call(add_kernel, shape((part, width), F32 if j != 2 else BF16), [VMEM] * 2)(
            own_rows, arrived[j]
        )
    pieces = {0: own_rows}
    for j in order:
        pieces[j] = swap(own_rows, "rep", j)

    outputs, carried = [], []
    for j, piece in pieces.items():
        outs = [shape((part, width), BF16), shape((quarter_blocks, size, width), F32)]
        if j != 2:
            outs += [shape((2, width, width), F32)]
        else:
            outs += [
                shape((2 * nodes + width, width), BF16),
                shape((nodes + width, width), BF16),
                shape(((chips - 2) * nodes, width), BF16),
            ]
        output, *carried = call(
            functools.partial(layer_kernel, rep, count, own_blocks, j),
            outs,
            [VMEM] * (6 + len(carried)),
            aliases={6: 1} if carried else {},
        )(place, flipped, cotangent, weight, bias.reshape(1, width), piece, *carried)
        outputs.append(output)
    contrib, across, beside, others = carried

    last = chips - 1
    message = shape((nodes + width, width), BF16)
    odd, even = (swap_some(across, 2 * last, core) for core in (1, 0))
    own, *sends, pair_weight = call(
        pair_kernel,
        [shape((nodes, width), F32)] + [message] * (last - 1) + [shape((width, width), BF16)],
        [VMEM] * 4,
    )(contrib, beside, swap(beside, "dom", 1), swap(others, "dom", 1))
    got = {chip: swap(sends[chip - 1], "dom", 2 * chip + 1) for chip in range(last - 1, 0, -1)}
    odd = call(copy_kernel, shape(odd.shape, BF16), [VMEM], cost=10**9)(odd)
    got_across, passed = call(pass_kernel, [shape(odd.shape, BF16), message], [VMEM] * 2)(odd, even)
    passed = swap(passed, "dom", 1)
    output = call(
        functools.partial(order_kernel, list(pieces)), shape((rows * size, width), BF16), [VMEM] * rep
    )(*outputs)
    early = call(early_sum_kernel, shape((nodes, width), F32), [VMEM] * chips)(
        own, got_across, *[got[chip] for chip in range(last - 1, 0, -1)]
    )
    feature_grad, weight_grad = call(
        final_kernel,
        [shape((nodes, width), F32), shape((width, width), F32)],
        [VMEM] * (chips + 2),
    )(early, pair_weight, got_across, passed, *[got[chip] for chip in range(1, last)])
    return output, feature_grad, weight_grad


def solution(mesh):
    placed = (
        P("dom", "rep"),
        P("dom", "rep", None, None),
        P(("rep", "dom"), None),
        P(),
        P(),
        P("dom", None),
    )
    return jax.shard_map(
        body,
        mesh=mesh,
        in_specs=placed,
        out_specs=(P("dom", None), P(("rep", "dom"), None), P()),
        check_vma=False,
    )
```

```python
import functools

import jax
import jax.numpy as jnp
from jax import lax
from jax.experimental import pallas as pl
from jax.experimental.pallas import tpu as pltpu
from jax.sharding import PartitionSpec as P

BF16 = jnp.bfloat16
F32 = jnp.float32
VMEM = pl.BlockSpec(memory_space=pltpu.VMEM)


def swap(value, axis, distance):
    size = lax.axis_size(axis)
    return lax.ppermute(value, axis, [(i, i ^ distance) for i in range(size)])


def matmul(a, b, contract):
    return lax.dot_general(a, b, ((contract[:1], contract[1:]), ((), ())), preferred_element_type=F32)


def early_kernel(vals_ref, features_ref, flipped_ref, own_ref, near_ref):
    rows, count, size, _ = vals_ref.shape
    near_ref[...] = vals_ref[...]
    own_ref[...] = features_ref[...]
    for row in range(rows):
        for k in range(count):
            flipped_ref[row, k * size : (k + 1) * size] = vals_ref[row, k].T


def place_kernel(own_blocks, dom, cols_ref, _, place_ref):
    count, rows = cols_ref.shape
    for row in range(rows):
        for k in range(count):
            col = cols_ref[k, row] - lax.axis_index("rep") * (own_blocks * dom)
            owner = lax.div(col, jnp.int32(own_blocks)) ^ lax.axis_index("dom")
            side = jnp.where(owner > 1, 1 - (owner & 1), owner)
            place = (side * (dom // 2) + (owner >> 1)) * own_blocks
            place += lax.rem(col, jnp.int32(own_blocks))
            place_ref[row * count + k : row * count + k + 1, :] = jnp.full((1, 128), place, jnp.int32)


def join_kernel(*refs):
    pieces, out_ref = refs[:-1], refs[-1]
    first = 0
    for piece in pieces:
        out_ref[first : first + piece.shape[0]] = piece[...]
        first += piece.shape[0]


def wrap_kernel(ends_ref, *refs):
    out_ref = refs[-1]
    nodes = ends_ref.shape[0] // 2
    out_ref[:nodes] = ends_ref[:nodes]
    for at, piece in enumerate(refs[:-1], 1):
        out_ref[at * nodes : (at + 1) * nodes] = piece[...]
    out_ref[out_ref.shape[0] - nodes :] = ends_ref[nodes:]


def aggregate_kernel(rep, place_ref, vals_ref, mine_ref, far_ref, *outs):
    rows, count, size, _ = vals_ref.shape
    half = mine_ref.shape[0] // size
    share = rows // rep
    for j in range(rep - 1, -1, -1):
        target = lax.axis_index("rep") ^ j
        for i in range(share):
            row = target * share + i
            total = None
            for k in range(count):
                place = place_ref[row * count + k, 0]
                beyond = place >= half
                index = jnp.where(beyond, place - half, place)
                here = pl.ds(pl.multiple_of(index * size, size), size)
                block = jnp.where(beyond, far_ref[here, :], mine_ref[here, :])
                term = matmul(vals_ref[row, k], block, (1, 0))
                total = term if total is None else total + term
            outs[j][i * size : (i + 1) * size] = total.astype(outs[j].dtype)


def layer_kernel(
    rep, count, own_blocks, j, place_ref, flipped_ref, cotangent_ref, weight_ref, bias_ref, *refs
):
    first, last = j == 0, j == 2
    piece_ref, refs = refs[0], refs[1:]
    if not first:
        (_, sums_in), refs = refs[:2], refs[2:]
    output_ref, contrib, *refs = refs
    rows, _, size = flipped_ref.shape
    share = rows // rep
    quarter_blocks = contrib.shape[0]
    nodes = own_blocks * size
    if first:
        contrib[...] = jnp.zeros_like(contrib)

    target = lax.axis_index("rep") ^ j
    aggregated = piece_ref[...]
    part = aggregated.shape[0]
    here = pl.ds(pl.multiple_of(target * part, part), part)
    hidden = matmul(aggregated, weight_ref[...], (1, 0)) + bias_ref[...]
    gate_prob = jax.nn.sigmoid(hidden)
    output_ref[...] = (hidden * gate_prob).astype(BF16)
    grad_hidden = (
        cotangent_ref[here, :].astype(F32) * gate_prob * (1.0 + hidden * (1.0 - gate_prob))
    ).astype(BF16)
    part_sum = matmul(aggregated, grad_hidden, (0, 0))
    grad_agg = matmul(grad_hidden, weight_ref[...], (1, 1)).astype(BF16)
    for i in range(share):
        row = target * share + i
        terms = matmul(flipped_ref[row], grad_agg[i * size : (i + 1) * size], (1, 0))
        for k in range(count):
            contrib[place_ref[row * count + k, 0]] += terms[k * size : (k + 1) * size]
    if j == 0:
        refs[0][0] = part_sum
        refs[0][1] = jnp.zeros_like(part_sum)
    elif j == 3:
        refs[0][0] = sums_in[0]
        refs[0][1] = part_sum
    elif j == 1:
        refs[0][0] = sums_in[0] + part_sum
        refs[0][1] = sums_in[1]
    else:
        across_ref, beside_ref, others_ref = refs
        half = quarter_blocks // 2
        rest = quarter_blocks * size // 2 - nodes
        weight = (sums_in[0] + (sums_in[1] + part_sum)).astype(BF16)
        away = contrib[half:].reshape(half * size, -1).astype(BF16)
        across_ref[:nodes] = away[rest:]
        across_ref[nodes : 2 * nodes] = contrib[half - own_blocks : half].reshape(nodes, -1).astype(BF16)
        across_ref[2 * nodes :] = weight
        beside_ref[:nodes] = away[rest - nodes : rest]
        beside_ref[nodes:] = weight
        others_ref[...] = away[: rest - nodes]


def add_kernel(a_ref, b_ref, out_ref):
    out_ref[...] = (a_ref[...] + b_ref[...].astype(F32)).astype(out_ref.dtype)


def order_kernel(order, *refs):
    pieces, out_ref = refs[:-1], refs[-1]
    part = pieces[0].shape[0]
    for j, piece in zip(order, pieces):
        target = lax.axis_index("rep") ^ j
        out_ref[pl.ds(pl.multiple_of(target * part, part), part), :] = piece[...]


def first_pair_kernel(contrib_ref, sent_ref, got_ref, out_ref):
    blocks, size, _ = contrib_ref.shape
    nodes = out_ref.shape[0] - sent_ref.shape[1]
    own_blocks = nodes // size
    mine = contrib_ref[blocks // 2 - 2 * own_blocks : blocks // 2 - own_blocks].reshape(nodes, -1)
    out_ref[:nodes] = (mine + got_ref[:nodes].astype(F32)).astype(BF16)
    out_ref[nodes:] = (sent_ref[nodes:].astype(F32) + got_ref[nodes:].astype(F32)).astype(BF16)


def rest_pair_kernel(contrib_ref, first_ref, got_ref, own_ref, *outs):
    size, nodes = contrib_ref.shape[1], own_ref.shape[0]
    for chip in range(len(outs) + 1):
        mine = contrib_ref[chip * nodes // size : (chip + 1) * nodes // size].reshape(nodes, -1)
        total = mine + got_ref[chip * nodes : (chip + 1) * nodes].astype(F32)
        if chip == 0:
            own_ref[...] = total
        else:
            outs[chip - 1][:nodes] = total.astype(BF16)
            outs[chip - 1][nodes:] = first_ref[nodes:]


def pass_kernel(got_ref, out_ref):
    out_ref[...] = got_ref[got_ref.shape[0] - out_ref.shape[0] :]


def total_of(values):
    while len(values) > 1:
        values = [a + b for a, b in zip(values[::2], values[1::2])]
    return values[0]


def final_kernel(own_ref, sent_ref, across_ref, passed_ref, *refs):
    got, (feature_ref, grad_ref) = refs[:-2], refs[-2:]
    nodes = feature_ref.shape[0]
    total = own_ref[...] + across_ref[:nodes].astype(F32) + passed_ref[:nodes].astype(F32)
    for g in got:
        total += g[:nodes].astype(F32)
    feature_ref[...] = total
    weights = [sent_ref[nodes:].astype(F32)] + [g[nodes:].astype(F32) for g in got]
    across = across_ref[2 * nodes :].astype(F32) + passed_ref[nodes:].astype(F32)
    grad_ref[...] = total_of(weights + [across.astype(BF16).astype(F32)])


def shape(dims, dtype):
    return jax.ShapeDtypeStruct(dims, dtype)


def body(cols, vals, features, weight, bias, cotangent):
    rows, count, size, _ = vals.shape
    nodes, width = features.shape
    dom, rep = lax.axis_size("dom"), lax.axis_size("rep")
    chips = dom // 2
    own_blocks = nodes // size
    quarter_blocks = own_blocks * dom
    part = rows * size // rep
    params = pltpu.CompilerParams(vmem_limit_bytes=(8 + dom // 2) * 1024 * 1024)

    def call(kernel, out_shape, in_specs, aliases={}):
        single = not isinstance(out_shape, list)
        return pl.pallas_call(
            kernel,
            out_shape=out_shape,
            in_specs=in_specs,
            out_specs=VMEM if single else [VMEM] * len(out_shape),
            input_output_aliases=aliases,
            compiler_params=params,
            cost_estimate=pl.CostEstimate(flops=0, bytes_accessed=0, transcendentals=0),
        )

    flipped, own, vals = call(
        early_kernel,
        [shape((rows, count * size, size), BF16), shape(features.shape, BF16), shape(vals.shape, BF16)],
        [VMEM] * 2,
    )(vals, features)

    def join(*values):
        nodes_in = sum(v.shape[0] for v in values)
        return call(join_kernel, shape((nodes_in, width), BF16), [VMEM] * len(values))(*values)

    across = [swap(features, "dom", 2 * chip + 1) for chip in range(1, chips)]
    ends = join(own, across[-1])
    far_ends = swap(ends, "dom", 1)
    half = chips // 2 - 1
    beyond = [swap(piece, "dom", 1) for piece in across[half:-1]]
    beyond = [swap(piece, "dom", 1) for piece in across[:half]] + beyond

    def wrap(*values):
        return call(wrap_kernel, shape((chips * nodes, width), BF16), [VMEM] * (chips - 1))(*values)

    mine, far = wrap(ends, *across[:-1]), wrap(far_ends, *beyond)
    place = call(
        functools.partial(place_kernel, own_blocks, dom),
        shape((rows * count, 128), jnp.int32),
        [VMEM] * 2,
    )(cols.T, ends)

    partials = call(
        functools.partial(aggregate_kernel, rep),
        [shape((part, width), BF16 if j else F32) for j in range(rep)],
        [VMEM] * 4,
    )(place, vals, mine, far)
    arrived = {j: swap(partials[j], "rep", j) if j else partials[j] for j in range(rep)}
    order = [3, 1, 2]
    own_rows = arrived[0]
    for j in order:
        own_rows = call(add_kernel, shape((part, width), F32 if j != 2 else BF16), [VMEM] * 2)(
            own_rows, arrived[j]
        )
    pieces = {0: own_rows}
    for j in order:
        pieces[j] = swap(own_rows, "rep", j)

    outputs, carried = [], []
    for j, piece in pieces.items():
        outs = [shape((part, width), BF16), shape((quarter_blocks, size, width), F32)]
        if j != 2:
            outs += [shape((2, width, width), F32)]
        else:
            outs += [
                shape((2 * nodes + width, width), BF16),
                shape((nodes + width, width), BF16),
                shape(((chips - 2) * nodes, width), BF16),
            ]
        output, *carried = call(
            functools.partial(layer_kernel, rep, count, own_blocks, j),
            outs,
            [VMEM] * (6 + len(carried)),
            aliases={6: 1} if carried else {},
        )(place, flipped, cotangent, weight, bias.reshape(1, width), piece, *carried)
        outputs.append(output)
    contrib, across, beside, others = carried

    last = chips - 1
    message = shape((nodes + width, width), BF16)
    got_across = swap(across, "dom", 2 * last)
    got_beside, got_others = swap(beside, "dom", 1), swap(others, "dom", 1)
    first = call(first_pair_kernel, message, [VMEM] * 3)(contrib, beside, got_beside)
    own, *sends = call(
        rest_pair_kernel,
        [shape((nodes, width), F32)] + [message] * (last - 2),
        [VMEM] * 3,
    )(contrib, first, got_others)
    sends.append(first)
    got = {chip: swap(sends[chip - 1], "dom", 2 * chip + 1) for chip in range(last - 1, 0, -1)}
    passed = swap(call(pass_kernel, message, [VMEM])(got_across), "dom", 1)
    output = call(
        functools.partial(order_kernel, list(pieces)), shape((rows * size, width), BF16), [VMEM] * rep
    )(*outputs)
    feature_grad, weight_grad = call(
        final_kernel,
        [shape((nodes, width), F32), shape((width, width), F32)],
        [VMEM] * (chips + 2),
    )(own, first, got_across, passed, *[got[chip] for chip in range(1, last)])
    return output, feature_grad, weight_grad


def solution(mesh):
    placed = (
        P("dom", "rep"),
        P("dom", "rep", None, None),
        P(("rep", "dom"), None),
        P(),
        P(),
        P("dom", None),
    )
    return jax.shard_map(
        body,
        mesh=mesh,
        in_specs=placed,
        out_specs=(P("dom", None), P(("rep", "dom"), None), P()),
        check_vma=False,
    )
```

```python
import functools

import jax
import jax.numpy as jnp
from jax import lax
from jax.experimental import pallas as pl
from jax.experimental.pallas import tpu as pltpu
from jax.sharding import PartitionSpec as P

BF16 = jnp.bfloat16
F32 = jnp.float32
VMEM = pl.BlockSpec(memory_space=pltpu.VMEM)


def swap(value, axis, distance):
    size = lax.axis_size(axis)
    return lax.ppermute(value, axis, [(i, i ^ distance) for i in range(size)])


def matmul(a, b, contract):
    return lax.dot_general(a, b, ((contract[:1], contract[1:]), ((), ())), preferred_element_type=F32)


def early_kernel(vals_ref, features_ref, flipped_ref, own_ref, near_ref):
    rows, count, size, _ = vals_ref.shape
    near_ref[...] = vals_ref[...]
    own_ref[...] = features_ref[...]
    for row in range(rows):
        for k in range(count):
            flipped_ref[row, k * size : (k + 1) * size] = vals_ref[row, k].T


def place_kernel(own_blocks, dom, cols_ref, _, place_ref):
    count, rows = cols_ref.shape
    for row in range(rows):
        for k in range(count):
            col = cols_ref[k, row] - lax.axis_index("rep") * (own_blocks * dom)
            owner = lax.div(col, jnp.int32(own_blocks)) ^ lax.axis_index("dom")
            side = jnp.where(owner > 1, 1 - (owner & 1), owner)
            place = (side * (dom // 2) + (owner >> 1)) * own_blocks
            place += lax.rem(col, jnp.int32(own_blocks))
            place_ref[row * count + k : row * count + k + 1, :] = jnp.full((1, 128), place, jnp.int32)


def join_kernel(*refs):
    pieces, out_ref = refs[:-1], refs[-1]
    first = 0
    for piece in pieces:
        out_ref[first : first + piece.shape[0]] = piece[...]
        first += piece.shape[0]


def wrap_kernel(ends_ref, *refs):
    out_ref = refs[-1]
    nodes = ends_ref.shape[0] // 2
    out_ref[:nodes] = ends_ref[:nodes]
    for at, piece in enumerate(refs[:-1], 1):
        out_ref[at * nodes : (at + 1) * nodes] = piece[...]
    out_ref[out_ref.shape[0] - nodes :] = ends_ref[nodes:]


def aggregate_kernel(rep, place_ref, vals_ref, mine_ref, far_ref, *outs):
    rows, count, size, _ = vals_ref.shape
    half = mine_ref.shape[0] // size
    share = rows // rep
    for j in range(rep - 1, -1, -1):
        target = lax.axis_index("rep") ^ j
        for i in range(share):
            row = target * share + i
            total = None
            for k in range(count):
                place = place_ref[row * count + k, 0]
                beyond = place >= half
                index = jnp.where(beyond, place - half, place)
                here = pl.ds(pl.multiple_of(index * size, size), size)
                block = jnp.where(beyond, far_ref[here, :], mine_ref[here, :])
                term = matmul(vals_ref[row, k], block, (1, 0))
                total = term if total is None else total + term
            outs[j][i * size : (i + 1) * size] = total.astype(outs[j].dtype)


def layer_kernel(
    rep, count, own_blocks, j, place_ref, flipped_ref, cotangent_ref, weight_ref, bias_ref, *refs
):
    first, last = j == 0, j == 2
    piece_ref, refs = refs[0], refs[1:]
    if not first:
        (_, sums_in), refs = refs[:2], refs[2:]
    output_ref, contrib, *refs = refs
    rows, _, size = flipped_ref.shape
    share = rows // rep
    quarter_blocks = contrib.shape[0]
    nodes = own_blocks * size
    if first:
        contrib[...] = jnp.zeros_like(contrib)

    target = lax.axis_index("rep") ^ j
    aggregated = piece_ref[...]
    part = aggregated.shape[0]
    here = pl.ds(pl.multiple_of(target * part, part), part)
    hidden = matmul(aggregated, weight_ref[...], (1, 0)) + bias_ref[...]
    gate_prob = jax.nn.sigmoid(hidden)
    output_ref[...] = (hidden * gate_prob).astype(BF16)
    grad_hidden = (
        cotangent_ref[here, :].astype(F32) * gate_prob * (1.0 + hidden * (1.0 - gate_prob))
    ).astype(BF16)
    part_sum = matmul(aggregated, grad_hidden, (0, 0))
    grad_agg = matmul(grad_hidden, weight_ref[...], (1, 1)).astype(BF16)
    for i in range(share):
        row = target * share + i
        terms = matmul(flipped_ref[row], grad_agg[i * size : (i + 1) * size], (1, 0))
        for k in range(count):
            contrib[place_ref[row * count + k, 0]] += terms[k * size : (k + 1) * size]
    if j == 0:
        refs[0][0] = part_sum
        refs[0][1] = jnp.zeros_like(part_sum)
    elif j == 3:
        refs[0][0] = sums_in[0]
        refs[0][1] = part_sum
    elif j == 1:
        refs[0][0] = sums_in[0] + part_sum
        refs[0][1] = sums_in[1]
    else:
        across_ref, beside_ref, others_ref = refs
        half = quarter_blocks // 2
        rest = quarter_blocks * size // 2 - nodes
        weight = (sums_in[0] + (sums_in[1] + part_sum)).astype(BF16)
        away = contrib[half:].reshape(half * size, -1).astype(BF16)
        across_ref[:nodes] = away[rest:]
        across_ref[nodes : 2 * nodes] = contrib[half - own_blocks : half].reshape(nodes, -1).astype(BF16)
        across_ref[2 * nodes :] = weight
        beside_ref[:nodes] = away[rest - nodes : rest]
        beside_ref[nodes:] = weight
        others_ref[...] = away[: rest - nodes]


def add_kernel(a_ref, b_ref, out_ref):
    out_ref[...] = (a_ref[...] + b_ref[...].astype(F32)).astype(out_ref.dtype)


def order_kernel(order, *refs):
    pieces, out_ref = refs[:-1], refs[-1]
    part = pieces[0].shape[0]
    for j, piece in zip(order, pieces):
        target = lax.axis_index("rep") ^ j
        out_ref[pl.ds(pl.multiple_of(target * part, part), part), :] = piece[...]


def first_pair_kernel(contrib_ref, sent_ref, got_ref, out_ref):
    blocks, size, _ = contrib_ref.shape
    nodes = out_ref.shape[0] - sent_ref.shape[1]
    own_blocks = nodes // size
    mine = contrib_ref[blocks // 2 - 2 * own_blocks : blocks // 2 - own_blocks].reshape(nodes, -1)
    out_ref[:nodes] = (mine + got_ref[:nodes].astype(F32)).astype(BF16)
    out_ref[nodes:] = (sent_ref[nodes:].astype(F32) + got_ref[nodes:].astype(F32)).astype(BF16)


def rest_pair_kernel(contrib_ref, first_ref, got_ref, own_ref, *outs):
    size, nodes = contrib_ref.shape[1], own_ref.shape[0]
    for chip in range(len(outs) + 1):
        mine = contrib_ref[chip * nodes // size : (chip + 1) * nodes // size].reshape(nodes, -1)
        total = mine + got_ref[chip * nodes : (chip + 1) * nodes].astype(F32)
        if chip == 0:
            own_ref[...] = total
        else:
            outs[chip - 1][:nodes] = total.astype(BF16)
            outs[chip - 1][nodes:] = first_ref[nodes:]


def pass_kernel(got_ref, out_ref):
    out_ref[...] = got_ref[got_ref.shape[0] - out_ref.shape[0] :]


def total_of(values):
    while len(values) > 1:
        values = [a + b for a, b in zip(values[::2], values[1::2])]
    return values[0]


def final_kernel(own_ref, sent_ref, across_ref, passed_ref, *refs):
    got, (feature_ref, grad_ref) = refs[:-2], refs[-2:]
    nodes = feature_ref.shape[0]
    total = own_ref[...] + across_ref[:nodes].astype(F32) + passed_ref[:nodes].astype(F32)
    for g in got:
        total += g[:nodes].astype(F32)
    feature_ref[...] = total
    weights = [sent_ref[nodes:].astype(F32)] + [g[nodes:].astype(F32) for g in got]
    across = across_ref[2 * nodes :].astype(F32) + passed_ref[nodes:].astype(F32)
    grad_ref[...] = total_of(weights + [across.astype(BF16).astype(F32)])


def shape(dims, dtype):
    return jax.ShapeDtypeStruct(dims, dtype)


def body(cols, vals, features, weight, bias, cotangent):
    rows, count, size, _ = vals.shape
    nodes, width = features.shape
    dom, rep = lax.axis_size("dom"), lax.axis_size("rep")
    chips = dom // 2
    own_blocks = nodes // size
    quarter_blocks = own_blocks * dom
    part = rows * size // rep
    params = pltpu.CompilerParams(vmem_limit_bytes=(8 + dom // 2) * 1024 * 1024)

    def call(kernel, out_shape, in_specs, aliases={}, cost=0):
        single = not isinstance(out_shape, list)
        return pl.pallas_call(
            kernel,
            out_shape=out_shape,
            in_specs=in_specs,
            out_specs=VMEM if single else [VMEM] * len(out_shape),
            input_output_aliases=aliases,
            compiler_params=params,
            cost_estimate=pl.CostEstimate(flops=cost, bytes_accessed=0, transcendentals=0),
        )

    flipped, own, vals = call(
        early_kernel,
        [shape((rows, count * size, size), BF16), shape(features.shape, BF16), shape(vals.shape, BF16)],
        [VMEM] * 2,
    )(vals, features)

    def join(*values):
        nodes_in = sum(v.shape[0] for v in values)
        return call(join_kernel, shape((nodes_in, width), BF16), [VMEM] * len(values))(*values)

    across = [swap(features, "dom", 2 * chip + 1) for chip in range(1, chips)]
    ends = join(own, across[-1])
    far_ends = swap(ends, "dom", 1)
    half = chips // 2 - 1
    beyond = [swap(piece, "dom", 1) for piece in across[half:-1]]
    beyond = [swap(piece, "dom", 1) for piece in across[:half]] + beyond

    def wrap(*values):
        return call(wrap_kernel, shape((chips * nodes, width), BF16), [VMEM] * (chips - 1))(*values)

    mine, far = wrap(ends, *across[:-1]), wrap(far_ends, *beyond)
    place = call(
        functools.partial(place_kernel, own_blocks, dom),
        shape((rows * count, 128), jnp.int32),
        [VMEM] * 2,
    )(cols.T, ends)

    partials = call(
        functools.partial(aggregate_kernel, rep),
        [shape((part, width), BF16 if j else F32) for j in range(rep)],
        [VMEM] * 4,
    )(place, vals, mine, far)
    arrived = {j: swap(partials[j], "rep", j) if j else partials[j] for j in range(rep)}
    order = [3, 1, 2]
    own_rows = arrived[0]
    for j in order:
        own_rows = call(add_kernel, shape((part, width), F32 if j != 2 else BF16), [VMEM] * 2)(
            own_rows, arrived[j]
        )
    pieces = {0: own_rows}
    for j in order:
        pieces[j] = swap(own_rows, "rep", j)

    outputs, carried = [], []
    for j, piece in pieces.items():
        outs = [shape((part, width), BF16), shape((quarter_blocks, size, width), F32)]
        if j != 2:
            outs += [shape((2, width, width), F32)]
        else:
            outs += [
                shape((2 * nodes + width, width), BF16),
                shape((nodes + width, width), BF16),
                shape(((chips - 2) * nodes, width), BF16),
            ]
        output, *carried = call(
            functools.partial(layer_kernel, rep, count, own_blocks, j),
            outs,
            [VMEM] * (6 + len(carried)),
            aliases={6: 1} if carried else {},
        )(place, flipped, cotangent, weight, bias.reshape(1, width), piece, *carried)
        outputs.append(output)
    contrib, across, beside, others = carried

    last = chips - 1
    message = shape((nodes + width, width), BF16)
    got_across = swap(across, "dom", 2 * last)
    got_beside, got_others = swap(beside, "dom", 1), swap(others, "dom", 1)
    first = call(first_pair_kernel, message, [VMEM] * 3, cost=5 * 10**9)(contrib, beside, got_beside)
    own, *sends = call(
        rest_pair_kernel,
        [shape((nodes, width), F32)] + [message] * (last - 2),
        [VMEM] * 3,
        cost=10**9,
    )(contrib, first, got_others)
    sends.append(first)
    got = {chip: swap(sends[chip - 1], "dom", 2 * chip + 1) for chip in range(last - 1, 0, -1)}
    passed = swap(call(pass_kernel, message, [VMEM])(got_across), "dom", 1)
    output = call(
        functools.partial(order_kernel, list(pieces)), shape((rows * size, width), BF16), [VMEM] * rep
    )(*outputs)
    feature_grad, weight_grad = call(
        final_kernel,
        [shape((nodes, width), F32), shape((width, width), F32)],
        [VMEM] * (chips + 2),
    )(own, first, got_across, passed, *[got[chip] for chip in range(1, last)])
    return output, feature_grad, weight_grad


def solution(mesh):
    placed = (
        P("dom", "rep"),
        P("dom", "rep", None, None),
        P(("rep", "dom"), None),
        P(),
        P(),
        P("dom", None),
    )
    return jax.shard_map(
        body,
        mesh=mesh,
        in_specs=placed,
        out_specs=(P("dom", None), P(("rep", "dom"), None), P()),
        check_vma=False,
    )
```
